32 devices in a mesh: dp: 16 (over z, x, core), tensor: 2 (over y).
Axes of the slice: x: 2, y: 2, z: 4, core: 2. Of those that a mesh axis runs over, the one named last changes fastest.
Arguments:
- grads: bfloat16 [16, 24, 128, 4096], P('dp', None, None, 'tensor'), may hold values from -6 to 6
- owner: int32 [24], replicated, may hold values from 0 to 15, as said below
- momentum: float32 [16, 2, 128, 4096], P('dp', None, None, 'tensor'), may hold values from -6 to 6, as said below
Outputs:
- update: bfloat16 [24, 128, 4096], P(None, None, 'tensor')
- new_momentum: float32 [16, 2, 128, 4096], P('dp', None, None, 'tensor')
The draws below stay inside these ranges and needn't reach their ends.
Inputs may be any that keep to these rules, and one draw needn't show every extreme that they name: Every owner holds at least one matrix and no owner holds more than 2; some owner holds exactly 2. Slot s of owner p holds the momentum of the matrix of slot_rank s among those that owner p holds; slots beyond an owner's count hold values that are carried over.
All inputs are finite; a program needn't handle non-finite values.
Results may differ from the reference program's by a relative error of at most 0.03.
Values may be sent and summed in bfloat16 or wider, within the bound.
No kernel may reach another device: no remote copies, remote signals or barrier semaphores. Data moves between devices by JAX's collectives and lax.ppermute only.
A program may use at most 128 MiB of HBM per device.

```python
import math
import jax
import jax.numpy as jnp
from jax import lax

R = 128
D = 4096
EXTRA = 8
SLOTS = 2
ITERS = 5
OWNERS = 16
MATS = 24


def draw_owner(key, part):
    folded = jax.random.fold_in(key, 11)
    key_owner, key_extra, key_order = jax.random.split(folded, 3)
    owner_perm = jax.random.permutation(key_owner, OWNERS).astype(jnp.int32)
    base = jnp.arange(OWNERS, dtype=jnp.int32) * SLOTS
    forced = jnp.arange(1, SLOTS, dtype=jnp.int32)
    others = jnp.arange((OWNERS - 1) * (SLOTS - 1), dtype=jnp.int32)
    candidates = (1 + others // (SLOTS - 1)) * SLOTS + 1 + others % (SLOTS - 1)
    chosen = jax.random.permutation(key_extra, candidates)[:EXTRA - (SLOTS - 1)].astype(jnp.int32)
    picks = jnp.concatenate([base, forced, chosen])
    holders = owner_perm[picks // SLOTS]
    shuffle = jax.random.permutation(key_order, MATS).astype(jnp.int32)
    return holders[shuffle].astype(jnp.int32)


def draw_momentum(key, part):
    folded = jax.random.fold_in(key, 23)
    key_value, key_row, key_col = jax.random.split(folded, 3)
    entries = jax.random.truncated_normal(key_value, -3.0, 3.0, (OWNERS, SLOTS, R, D), jnp.float32)
    log_top = math.log(10.0)
    row_scale = jnp.exp(jax.random.uniform(key_row, (OWNERS, SLOTS, R, 1), jnp.float32, 0.0, log_top))
    col_scale = jnp.exp(jax.random.uniform(key_col, (1, 1, 1, D), jnp.float32, 0.0, log_top))
    return 0.02 * entries * row_scale * col_scale


def level_of(key, shape, cuts, low, largest):
    gain = 1.0
    for position, blocks in cuts:
        heights = jax.random.uniform(jax.random.fold_in(jax.random.fold_in(key, 6), position), (blocks,), jnp.float32, low / len(cuts), largest / len(cuts))
        gain = gain * jnp.repeat(jnp.exp(heights), shape[position] // blocks).reshape((-1,) + (1,) * (len(shape) - 1 - position))
    return gain


def bell_draw(rng, dims, deviation, bound, pieces=(), kind=jnp.bfloat16):
    drawn = deviation * jax.random.normal(rng, dims, jnp.float32)
    if pieces:
        drawn = drawn * level_of(rng, dims, pieces, -0.22, 0.18)
    return jnp.clip(drawn, -bound, bound).astype(kind)


def setup_inputs(seed: int = 0) -> dict:
    key_list = jax.random.split(jax.random.key(seed), 4)
    grads = bell_draw(key_list[0], (OWNERS, MATS, R, D), 1.0, 6.0, ((0, 16), (3, 2)))
    owner = draw_owner(jax.random.fold_in(key_list[3], 71), 0)
    momentum = draw_momentum(jax.random.fold_in(key_list[3], 71), 0)
    return dict(grads=grads, owner=owner, momentum=momentum)


COEF_A = 3.4445
COEF_B = -4.775
COEF_C = 2.0315
EPSILON = 1e-07
DECAY = 0.95

def orthogonalize(rounded):
    squares = jnp.sum(jnp.square(rounded.astype(jnp.float32)))
    iterate = (rounded.astype(jnp.float32) / (jnp.sqrt(squares) + EPSILON)).astype(jnp.bfloat16)
    factor = 0.2 * math.sqrt(max(R, D))
    following = None
    for step in range(ITERS):
        gram = jnp.dot(iterate, iterate.T, preferred_element_type=jnp.float32).astype(jnp.bfloat16)
        gram = lax.optimization_barrier(gram)
        polynomial = (COEF_B * gram.astype(jnp.float32) + COEF_C * jnp.dot(gram, gram, preferred_element_type=jnp.float32)).astype(jnp.bfloat16)
        following = COEF_A * iterate.astype(jnp.float32) + jnp.dot(polynomial, iterate, preferred_element_type=jnp.float32)
        if step + 1 < ITERS:
            iterate = following.astype(jnp.bfloat16)
    return (factor * following).astype(jnp.bfloat16)

def reference(grads, owner, momentum):
    positions = jnp.arange(MATS, dtype=jnp.int32)
    same_owner = owner[:, None] == owner[None, :]
    earlier = positions[None, :] < positions[:, None]
    slot_rank = lax.optimization_barrier(jnp.sum((same_owner & earlier).astype(jnp.int32), axis=1)).astype(jnp.int32)

    def one_matrix(matrix_id):
        replicas = lax.dynamic_index_in_dim(grads, matrix_id, 1, keepdims=False)
        mean_grad = lax.optimization_barrier(jnp.sum(replicas.astype(jnp.float32), axis=0)) / OWNERS
        previous = momentum[owner[matrix_id], slot_rank[matrix_id]]
        following = DECAY * previous + mean_grad
        rounded = (mean_grad + DECAY * following).astype(jnp.bfloat16)
        return (orthogonalize(rounded), following)
    update, momentum_next = lax.map(one_matrix, positions)
    new_momentum = momentum.at[owner, slot_rank].set(momentum_next)
    return (update, new_momentum)
```

```python
import functools
import math

import jax
import jax.numpy as jnp
from jax import lax
from jax.experimental import pallas as pl
from jax.experimental.pallas import tpu as pltpu
from jax.sharding import PartitionSpec as P

R = 128
D = 4096
ITERS = 5

COEF_A = 3.4445
COEF_B = -4.775
COEF_C = 2.0315
EPSILON = 1e-07
DECAY = 0.95

CORES = 2
PAIR = 2
VMEM_BYTES = 48 * 1024 * 1024


def copy_blocks(count, first, rows, idx_ref, src_ref, out_ref, sem):
    def copy(i):
        return pltpu.make_async_copy(
            src_ref.at[idx_ref[i], pl.ds(first, rows)], out_ref.at[i], sem.at[i]
        )

    def start(i, _):
        copy(i).start()
        return 0

    def wait(i, _):
        copy(i).wait()
        return 0

    lax.fori_loop(0, count, start, 0)
    lax.fori_loop(0, count, wait, 0)


def take_blocks(src, idx, first, rows):
    count = idx.shape[0]
    cols = src.shape[2]
    size = count * rows * cols * src.dtype.itemsize
    return pl.pallas_call(
        functools.partial(copy_blocks, count, first, rows),
        out_shape=jax.ShapeDtypeStruct((count, rows, cols), src.dtype),
        in_specs=[
            pl.BlockSpec(memory_space=pltpu.SMEM),
            pl.BlockSpec(memory_space=pl.ANY),
        ],
        out_specs=pl.BlockSpec(memory_space=pl.ANY),
        scratch_shapes=[pltpu.SemaphoreType.DMA((count,))],
        cost_estimate=pl.CostEstimate(flops=0, bytes_accessed=2 * size, transcendentals=0),
    )(idx, src)


def sum_blocks(count, first, rows, outs, idx_ref, src_ref, other_ref, *rest):
    out_refs = rest[:outs]
    mine, sums, sem_mine, sem_other, sem_out = rest[outs:]
    each = count // outs

    def copies(i):
        return (
            pltpu.make_async_copy(
                src_ref.at[idx_ref[i], pl.ds(first, rows)], mine.at[i], sem_mine.at[i]
            ),
            pltpu.make_async_copy(other_ref.at[i], sums.at[i], sem_other.at[i]),
        )

    def start(i, _):
        for c in copies(i):
            c.start()
        return 0

    lax.fori_loop(0, count, start, 0)
    for part, out_ref in enumerate(out_refs):

        def leave(i, part=part, out_ref=out_ref):
            return pltpu.make_async_copy(
                sums.at[part * each + i], out_ref.at[i], sem_out.at[part * each + i]
            )

        def body(i, _, part=part, leave=leave):
            at = part * each + i
            for c in copies(at):
                c.wait()
            sums[at] = sums[at] + mine[at]
            leave(i).start()
            return 0

        lax.fori_loop(0, each, body, 0)
    for part, out_ref in enumerate(out_refs):

        def finish(i, _, part=part, out_ref=out_ref):
            pltpu.make_async_copy(
                sums.at[part * each + i], out_ref.at[i], sem_out.at[part * each + i]
            ).wait()
            return 0

        lax.fori_loop(0, each, finish, 0)


def add_taken(src, idx, first, rows, other, outs):
    count = idx.shape[0]
    cols = src.shape[2]
    size = count * rows * cols * src.dtype.itemsize
    each = jax.ShapeDtypeStruct((count // outs, rows, cols), src.dtype)
    return pl.pallas_call(
        functools.partial(sum_blocks, count, first, rows, outs),
        out_shape=[each] * outs,
        in_specs=[
            pl.BlockSpec(memory_space=pltpu.SMEM),
            pl.BlockSpec(memory_space=pl.ANY),
            pl.BlockSpec(memory_space=pl.ANY),
        ],
        out_specs=[pl.BlockSpec(memory_space=pl.ANY)] * outs,
        scratch_shapes=[
            pltpu.VMEM((count, rows, cols), src.dtype),
            pltpu.VMEM((count, rows, cols), src.dtype),
            pltpu.SemaphoreType.DMA((count,)),
            pltpu.SemaphoreType.DMA((count,)),
            pltpu.SemaphoreType.DMA((count,)),
        ],
        compiler_params=pltpu.CompilerParams(vmem_limit_bytes=VMEM_BYTES),
        cost_estimate=pl.CostEstimate(
            flops=size // 2, bytes_accessed=3 * size, transcendentals=0
        ),
    )(idx, src, other)


def momentum_kernel(scale, sizes, held_ref, momentum_ref, *rest):
    part_refs = rest[: sum(sizes)]
    next_ref, rounded_ref, gram_ref = rest[sum(sizes) :]
    held = held_ref[pl.program_id(0)] > 0
    first, used = 0, 0
    for size in sizes:
        total = None
        for ref in part_refs[used : used + size]:
            term = ref[0].astype(jnp.float32)
            total = term if total is None else total + term
        rows = total.shape[0]
        here = pl.ds(first, rows)
        mean = total * scale
        previous = momentum_ref[0, here]
        following = DECAY * previous + mean
        next_ref[0, here] = jnp.where(held, following, previous)
        rounded_ref[0, here] = (mean + DECAY * following).astype(jnp.bfloat16)
        first += rows
        used += size
    rounded = rounded_ref[0]
    gram_ref[0] = lax.dot_general(
        rounded, rounded, (((1,), (1,)), ((), ())), preferred_element_type=jnp.float32
    )


def momentum_step(held, momentum, parts, owner_count):
    slots, rows, cols = momentum.shape
    flat = [a for part in parts for a in part]
    return pl.pallas_call(
        functools.partial(
            momentum_kernel, 1.0 / owner_count, [len(part) for part in parts]
        ),
        grid=(slots,),
        out_shape=[
            jax.ShapeDtypeStruct((slots, rows, cols), jnp.float32),
            jax.ShapeDtypeStruct((slots, rows, cols), jnp.bfloat16),
            jax.ShapeDtypeStruct((slots, rows, rows), jnp.float32),
        ],
        in_specs=[
            pl.BlockSpec(memory_space=pltpu.SMEM),
            pl.BlockSpec((1, rows, cols), lambda s: (s, 0, 0)),
        ]
        + [pl.BlockSpec((1,) + a.shape[1:], lambda s: (s, 0, 0)) for a in flat],
        out_specs=[
            pl.BlockSpec((1, rows, cols), lambda s: (s, 0, 0)),
            pl.BlockSpec((1, rows, cols), lambda s: (s, 0, 0)),
            pl.BlockSpec((1, rows, rows), lambda s: (s, 0, 0)),
        ],
        compiler_params=pltpu.CompilerParams(vmem_limit_bytes=VMEM_BYTES),
        cost_estimate=pl.CostEstimate(
            flops=2 * slots * rows * rows * cols,
            bytes_accessed=slots * rows * cols * 16,
            transcendentals=0,
        ),
    )(held, momentum, *flat)


def exact(a, b):
    return jnp.dot(
        a, b, preferred_element_type=jnp.float32, precision=lax.Precision.HIGHEST
    )


def orthogonalize_kernel(factor, slots, grams, *refs):
    gram_refs = refs[:grams]
    rounded_ref, out_ref = refs[grams:]
    rows = rounded_ref.shape[1]
    row_ids = lax.broadcasted_iota(jnp.int32, (rows, rows), 0)
    col_ids = lax.broadcasted_iota(jnp.int32, (rows, rows), 1)
    diagonal = row_ids == col_ids
    held = []
    for s in range(slots):
        gram = gram_refs[0][s]
        for ref in gram_refs[1:]:
            gram = gram + ref[s]
        squares = jnp.sum(
            jnp.sum(jnp.where(diagonal, gram, 0.0), axis=0, keepdims=True),
            axis=1,
            keepdims=True,
        )
        inverse = 1.0 / (jnp.sqrt(squares) + EPSILON)
        held.append([gram * inverse * inverse, None, inverse])
    for step in range(ITERS):
        squared = [exact(h[0], h[0]) for h in held]
        factors = [
            COEF_B * h[0] + COEF_C * q + jnp.where(diagonal, COEF_A, 0.0)
            for h, q in zip(held, squared)
        ]
        for h, m in zip(held, factors):
            h[1] = m if h[1] is None else exact(m, h[1])
        if step + 1 < ITERS:
            once = [exact(m, h[0]) for h, m in zip(held, factors)]
            for h, m, o in zip(held, factors, once):
                h[0] = exact(m, o)
    for s, h in enumerate(held):
        whole = h[1] * (factor * h[2])
        high = whole.astype(jnp.bfloat16)
        low = (whole - high.astype(jnp.float32)).astype(jnp.bfloat16)
        rounded = rounded_ref[s]
        out_ref[s] = (
            jnp.dot(high, rounded, preferred_element_type=jnp.float32)
            + jnp.dot(low, rounded, preferred_element_type=jnp.float32)
        ).astype(jnp.bfloat16)


def orthogonalize(grams, rounded, factor):
    slots, rows, cols = rounded.shape
    return pl.pallas_call(
        functools.partial(orthogonalize_kernel, factor, slots, len(grams)),
        out_shape=jax.ShapeDtypeStruct(rounded.shape, jnp.bfloat16),
        in_specs=[pl.BlockSpec(memory_space=pltpu.VMEM)] * (len(grams) + 1),
        out_specs=pl.BlockSpec(memory_space=pltpu.VMEM),
        compiler_params=pltpu.CompilerParams(vmem_limit_bytes=VMEM_BYTES),
        cost_estimate=pl.CostEstimate(
            flops=slots * (4 * rows * rows * cols + 20 * 12 * rows * rows * rows),
            bytes_accessed=slots * rows * cols * 4,
            transcendentals=0,
        ),
    )(*grams, rounded)


class Place:
    def __init__(self):
        self.count = lax.axis_size("dp")
        self.depth = self.count // (PAIR * CORES)
        me = lax.axis_index("dp")
        self.core = me % CORES
        self.x = (me // CORES) % PAIR
        self.z = me // (CORES * PAIR)

    def pairs(self, move):
        found = []
        for z in range(self.depth):
            for x in range(PAIR):
                for core in range(CORES):
                    to = move(z, x, core)
                    if to is not None:
                        a, b, c = to
                        found.append(
                            (
                                (z * PAIR + x) * CORES + core,
                                (a * PAIR + b) * CORES + c,
                            )
                        )
        return found

    def swap_cores(self, value):
        return lax.ppermute(value, "dp", self.pairs(lambda z, x, c: (z, x, 1 - c)))

    def swap_x(self, value):
        return lax.ppermute(value, "dp", self.pairs(lambda z, x, c: (z, 1 - x, c)))

    def shift_z(self, value, step, sources):
        return lax.ppermute(
            value,
            "dp",
            self.pairs(lambda z, x, c: (z + step, x, c) if z in sources else None),
        )


def chain_sum(place, blocks):
    depth = place.depth

    def own(at):
        return lax.dynamic_index_in_dim(blocks, jnp.clip(at, 0, depth - 1), 0, False)

    up, down = blocks[depth - 1], blocks[0]
    for t in range(1, depth):
        up = place.shift_z(up, 1, range(0, t))
        down = place.shift_z(down, -1, range(depth - t, depth))
        if t + 1 < depth:
            up = up + own(depth - 1 - t + place.z)
            down = down + own(t - (depth - 1) + place.z)
    return up, down, own(place.z)


def reduce_to_owners(place, gradient, source, slot_count, shares):
    cols = gradient.shape[2]
    core_first = jnp.take(source, place.core, axis=2)
    other_core = jnp.take(source, 1 - place.core, axis=2)

    def ordered(table, x_first):
        if not x_first:
            return table.reshape(-1)
        away = jnp.take(table, 1 - place.x, axis=1)
        home = jnp.take(table, place.x, axis=1)
        return jnp.concatenate([away.reshape(-1), home.reshape(-1)])

    first = 0
    received = []
    for rows, x_first in shares:
        sent = take_blocks(gradient, ordered(other_core, x_first), first, rows)
        received.append((first, rows, x_first, place.swap_cores(sent)))
        first += rows
    results = []
    for first, rows, x_first, other in received:
        mine = ordered(core_first, x_first)
        if x_first:
            away, home = add_taken(gradient, mine, first, rows, other, 2)
            blocks = home + place.swap_x(away)
            blocks = blocks.reshape(place.depth, slot_count, rows, cols)
            results.append(chain_sum(place, blocks))
        else:
            (blocks,) = add_taken(gradient, mine, first, rows, other, 1)
            blocks = blocks.reshape(place.depth, PAIR, slot_count, rows, cols)
            up, down, own = chain_sum(place, blocks)
            both = up + down + own
            away = lax.dynamic_index_in_dim(both, 1 - place.x, 0, False)
            home = lax.dynamic_index_in_dim(both, place.x, 0, False)
            got = place.swap_x(away)
            results.append((home, got))
    return results


def per_device(grads, owner, momentum):
    place = Place()
    owner_count = place.count
    matrices = owner.shape[0]
    slot_count = momentum.shape[1]
    head_rows = grads.shape[2]
    factor = 0.2 * math.sqrt(max(R, D))
    positions = jnp.arange(matrices, dtype=jnp.int32)
    same_owner = owner[:, None] == owner[None, :]
    earlier = positions[None, :] < positions[:, None]
    slot_rank = jnp.sum((same_owner & earlier).astype(jnp.int32), axis=1)
    spot = owner * slot_count + slot_rank
    spots = jnp.arange(owner_count * slot_count, dtype=jnp.int32)
    matches = spot[None, :] == spots[:, None]
    filled = jnp.any(matches, axis=1).astype(jnp.int32)
    source = jnp.sum(jnp.where(matches, positions[None, :], 0), axis=1)
    source = source.reshape(place.depth, PAIR, CORES, slot_count)
    held = lax.dynamic_slice_in_dim(
        filled, lax.axis_index("dp") * slot_count, slot_count, 0
    )

    cut = head_rows * 5 // 8
    shares = ((cut, True), (head_rows - cut, False))
    parts = reduce_to_owners(place, grads[0], source, slot_count, shares)
    new_momentum, rounded, gram = momentum_step(held, momentum[0], parts, owner_count)

    width = lax.axis_size("tensor")
    grams = [gram]
    for _ in range(width - 1):
        grams.append(
            lax.ppermute(
                grams[-1], "tensor", [(i, (i + 1) % width) for i in range(width)]
            )
        )
    result = orthogonalize(grams, rounded, factor)
    everything = lax.all_gather(result, "dp", axis=0, tiled=True)
    update = take_blocks(everything, spot, 0, head_rows)
    return (update, new_momentum[None])


def solution(mesh):
    in_specs = (P("dp", None, None, "tensor"), P(), P("dp", None, None, "tensor"))
    out_specs = (P(None, None, "tensor"), P("dp", None, None, "tensor"))
    return jax.shard_map(
        per_device, mesh=mesh, in_specs=in_specs, out_specs=out_specs, check_vma=False
    )
```

```python
import functools
import math

import jax
import jax.numpy as jnp
from jax import lax
from jax.experimental import pallas as pl
from jax.experimental.pallas import tpu as pltpu
from jax.sharding import PartitionSpec as P

R = 128
D = 4096
ITERS = 5

COEF_A = 3.4445
COEF_B = -4.775
COEF_C = 2.0315
EPSILON = 1e-07
DECAY = 0.95

CORES = 2
PAIR = 2
VMEM_BYTES = 48 * 1024 * 1024


def combine_kernel(plans, arrays, table_ref, *refs):
    sources = refs[:arrays]
    outs = refs[len(refs) - 3 * len(plans) : len(refs) - 2 * len(plans)]
    held = refs[len(refs) - 2 * len(plans) : len(refs) - len(plans)]
    sems = refs[len(refs) - len(plans) :]

    def load(p, t, i):
        count, rows, terms = plans[p]
        at, first, offset = terms[t]
        return pltpu.make_async_copy(
            sources[at].at[table_ref[offset + i], pl.ds(first, rows)],
            held[p].at[t, i],
            sems[p].at[t, i],
        )

    def leave(p, i):
        return pltpu.make_async_copy(
            held[p].at[0, i], outs[p].at[i], sems[p].at[len(plans[p][2]), i]
        )

    for p, (count, _, terms) in enumerate(plans):

        @pl.loop(0, count)
        def _(i, p=p, terms=terms):
            for t in range(len(terms)):
                load(p, t, i).start()

    for p, (count, _, terms) in enumerate(plans):

        @pl.loop(0, count)
        def _(i, p=p, terms=terms):
            for t in range(len(terms)):
                load(p, t, i).wait()
            if len(terms) > 1:
                total = held[p][0, i].astype(jnp.float32)
                for t in range(1, len(terms)):
                    total = total + held[p][t, i].astype(jnp.float32)
                held[p][0, i] = total.astype(held[p].dtype)
            leave(p, i).start()

    for p, (count, _, _) in enumerate(plans):

        @pl.loop(0, count)
        def _(i, p=p):
            leave(p, i).wait()


def combine(after, *wanted):
    arrays, tables, plans, offset, size = [], [], [], 0, 0
    for rows, terms in wanted:
        found = []
        for array, items, first in terms:
            places = [i for i, a in enumerate(arrays) if a is array]
            if not places:
                arrays.append(array)
                places = [len(arrays) - 1]
            found.append((places[0], first, offset))
            tables.append(jnp.asarray(items, jnp.int32).reshape(-1))
            offset += tables[-1].shape[0]
        count = tables[-1].shape[0]
        plans.append((count, rows, tuple(found)))
        size += (len(found) + 1) * count * rows
    cols, kind = arrays[0].shape[2], arrays[0].dtype
    size *= cols * kind.itemsize
    return pl.pallas_call(
        functools.partial(combine_kernel, tuple(plans), len(arrays)),
        out_shape=[
            jax.ShapeDtypeStruct((count, rows, cols), kind) for count, rows, _ in plans
        ],
        in_specs=[pl.BlockSpec(memory_space=pltpu.SMEM)]
        + [pl.BlockSpec(memory_space=pl.ANY)] * (len(arrays) + len(after)),
        out_specs=[pl.BlockSpec(memory_space=pl.ANY)] * len(plans),
        scratch_shapes=[
            pltpu.VMEM((len(terms), count, rows, cols), kind)
            for count, rows, terms in plans
        ]
        + [
            pltpu.SemaphoreType.DMA((len(terms) + 1, count)) for count, _, terms in plans
        ],
        compiler_params=pltpu.CompilerParams(vmem_limit_bytes=VMEM_BYTES),
        cost_estimate=pl.CostEstimate(
            flops=size // 4, bytes_accessed=size, transcendentals=0
        ),
    )(jnp.concatenate(tables), *arrays, *after)


def momentum_kernel(scale, sizes, held_ref, momentum_ref, *rest):
    part_refs = rest[: sum(sizes)]
    next_ref, rounded_ref, gram_ref = rest[sum(sizes) :]
    held = held_ref[pl.program_id(0)] > 0
    first, used = 0, 0
    for size in sizes:
        total = None
        for ref in part_refs[used : used + size]:
            term = ref[0].astype(jnp.float32)
            total = term if total is None else total + term
        rows = total.shape[0]
        here = pl.ds(first, rows)
        mean = total * scale
        previous = momentum_ref[0, here]
        following = DECAY * previous + mean
        next_ref[0, here] = jnp.where(held, following, previous)
        rounded_ref[0, here] = (mean + DECAY * following).astype(jnp.bfloat16)
        first += rows
        used += size
    rounded = rounded_ref[0]
    gram_ref[0] = lax.dot_general(
        rounded, rounded, (((1,), (1,)), ((), ())), preferred_element_type=jnp.float32
    )


def momentum_step(held, momentum, parts, owner_count):
    slots, rows, cols = momentum.shape
    flat = [a for part in parts for a in part]
    return pl.pallas_call(
        functools.partial(
            momentum_kernel, 1.0 / owner_count, [len(part) for part in parts]
        ),
        grid=(slots,),
        out_shape=[
            jax.ShapeDtypeStruct((slots, rows, cols), jnp.float32),
            jax.ShapeDtypeStruct((slots, rows, cols), jnp.bfloat16),
            jax.ShapeDtypeStruct((slots, rows, rows), jnp.float32),
        ],
        in_specs=[
            pl.BlockSpec(memory_space=pltpu.SMEM),
            pl.BlockSpec((1, rows, cols), lambda s: (s, 0, 0)),
        ]
        + [pl.BlockSpec((1,) + a.shape[1:], lambda s: (s, 0, 0)) for a in flat],
        out_specs=[
            pl.BlockSpec((1, rows, cols), lambda s: (s, 0, 0)),
            pl.BlockSpec((1, rows, cols), lambda s: (s, 0, 0)),
            pl.BlockSpec((1, rows, rows), lambda s: (s, 0, 0)),
        ],
        compiler_params=pltpu.CompilerParams(vmem_limit_bytes=VMEM_BYTES),
        cost_estimate=pl.CostEstimate(
            flops=2 * slots * rows * rows * cols,
            bytes_accessed=slots * rows * cols * 16,
            transcendentals=0,
        ),
    )(held, momentum, *flat)


def exact(a, b):
    return jnp.dot(
        a, b, preferred_element_type=jnp.float32, precision=lax.Precision.HIGHEST
    )


def orthogonalize_kernel(factor, slots, grams, *refs):
    gram_refs = refs[:grams]
    rounded_ref, out_ref = refs[grams:]
    rows = rounded_ref.shape[1]
    row_ids = lax.broadcasted_iota(jnp.int32, (rows, rows), 0)
    col_ids = lax.broadcasted_iota(jnp.int32, (rows, rows), 1)
    diagonal = row_ids == col_ids
    held = []
    for s in range(slots):
        gram = gram_refs[0][s]
        for ref in gram_refs[1:]:
            gram = gram + ref[s]
        squares = jnp.sum(
            jnp.sum(jnp.where(diagonal, gram, 0.0), axis=0, keepdims=True),
            axis=1,
            keepdims=True,
        )
        inverse = 1.0 / (jnp.sqrt(squares) + EPSILON)
        held.append([gram * inverse * inverse, None, inverse])
    for step in range(ITERS):
        squared = [exact(h[0], h[0]) for h in held]
        factors = [
            COEF_B * h[0] + COEF_C * q + jnp.where(diagonal, COEF_A, 0.0)
            for h, q in zip(held, squared)
        ]
        for h, m in zip(held, factors):
            h[1] = m if h[1] is None else exact(m, h[1])
        if step + 1 < ITERS:
            once = [exact(m, h[0]) for h, m in zip(held, factors)]
            for h, m, o in zip(held, factors, once):
                h[0] = exact(m, o)
    for s, h in enumerate(held):
        whole = h[1] * (factor * h[2])
        high = whole.astype(jnp.bfloat16)
        low = (whole - high.astype(jnp.float32)).astype(jnp.bfloat16)
        rounded = rounded_ref[s]
        out_ref[s] = (
            jnp.dot(high, rounded, preferred_element_type=jnp.float32)
            + jnp.dot(low, rounded, preferred_element_type=jnp.float32)
        ).astype(jnp.bfloat16)


def orthogonalize(grams, rounded, factor):
    slots, rows, cols = rounded.shape
    return pl.pallas_call(
        functools.partial(orthogonalize_kernel, factor, slots, len(grams)),
        out_shape=jax.ShapeDtypeStruct(rounded.shape, jnp.bfloat16),
        in_specs=[pl.BlockSpec(memory_space=pltpu.VMEM)] * (len(grams) + 1),
        out_specs=pl.BlockSpec(memory_space=pltpu.VMEM),
        compiler_params=pltpu.CompilerParams(vmem_limit_bytes=VMEM_BYTES),
        cost_estimate=pl.CostEstimate(
            flops=slots * (4 * rows * rows * cols + 20 * 12 * rows * rows * rows),
            bytes_accessed=slots * rows * cols * 4,
            transcendentals=0,
        ),
    )(*grams, rounded)


class Place:
    def __init__(self):
        self.count = lax.axis_size("dp")
        self.depth = self.count // (PAIR * CORES)
        me = lax.axis_index("dp")
        self.core = me % CORES
        self.x = (me // CORES) % PAIR
        self.z = me // (CORES * PAIR)

    def pairs(self, move):
        found = []
        for z in range(self.depth):
            for x in range(PAIR):
                for core in range(CORES):
                    to = move(z, x, core)
                    if to is not None:
                        a, b, c = to
                        found.append(
                            (
                                (z * PAIR + x) * CORES + core,
                                (a * PAIR + b) * CORES + c,
                            )
                        )
        return found

    def swap_cores(self, value):
        return lax.ppermute(value, "dp", self.pairs(lambda z, x, c: (z, x, 1 - c)))

    def swap_x(self, value):
        return lax.ppermute(value, "dp", self.pairs(lambda z, x, c: (z, 1 - x, c)))

    def shift_z(self, value, step, sources):
        return lax.ppermute(
            value,
            "dp",
            self.pairs(lambda z, x, c: (z + step, x, c) if z in sources else None),
        )


class Flow:
    def __init__(self, place, gradient, source, slots, first, rows, x_first):
        self.place, self.gradient, self.slots = place, gradient, slots
        self.first, self.rows, self.x_first = first, rows, x_first
        self.mine = jnp.take(source, place.core, axis=2)
        self.theirs = jnp.take(source, 1 - place.core, axis=2)
        self.group = slots if x_first else slots * PAIR
        self.step = 0

    def ordered(self, table):
        if not self.x_first:
            return table.reshape(-1)
        away = jnp.take(table, 1 - self.place.x, axis=1)
        home = jnp.take(table, self.place.x, axis=1)
        return jnp.concatenate([away.reshape(-1), home.reshape(-1)])

    def block(self, at):
        at = jnp.clip(at, 0, self.place.depth - 1)
        return at * self.group + jnp.arange(self.group, dtype=jnp.int32)

    def every(self, array):
        return jnp.arange(array.shape[0], dtype=jnp.int32)

    def pack(self, after):
        term = (self.gradient, self.ordered(self.theirs), self.first)
        (sent,) = combine(after, (self.rows, [term]))
        self.got = self.place.swap_cores(sent)
        return [sent]

    def add_core(self, after):
        items = self.ordered(self.mine)
        count = items.shape[0]
        half = count // 2
        ids = jnp.arange(count, dtype=jnp.int32)

        def part(a, b):
            return (
                self.rows,
                [(self.gradient, items[a:b], self.first), (self.got, ids[a:b], 0)],
            )

        if self.x_first:
            away, self.home = combine(after, part(0, half), part(half, count))
            self.got = self.place.swap_x(away)
            return [away]
        (self.blocks,) = combine(after, part(0, count))
        self.send_first()
        return [self.blocks]

    def send_first(self):
        depth, group = self.place.depth, self.group
        self.up = self.blocks[(depth - 1) * group :]
        self.down = self.blocks[:group]
        self.send()

    def send(self):
        self.step += 1
        t, depth = self.step, self.place.depth
        self.up = self.place.shift_z(self.up, 1, range(0, t))
        self.down = self.place.shift_z(self.down, -1, range(depth - t, depth))

    def add_x(self, after):
        ids = self.every(self.home)
        (self.blocks,) = combine(
            after, (self.rows, [(self.home, ids, 0), (self.got, ids, 0)])
        )
        self.send_first()
        return [self.blocks]

    def add_z(self, after):
        t, z, depth = self.step, self.place.z, self.place.depth
        ids = jnp.arange(self.group, dtype=jnp.int32)
        self.up, self.down = combine(
            after,
            (self.rows, [(self.up, ids, 0), (self.blocks, self.block(depth - 1 - t + z), 0)]),
            (self.rows, [(self.down, ids, 0), (self.blocks, self.block(t - depth + 1 + z), 0)]),
        )
        made = [self.up]
        self.send()
        return made

    def last_z(self, after):
        slots, x = self.slots, self.place.x
        ids = jnp.arange(slots, dtype=jnp.int32)

        def part(x):
            return (
                self.rows,
                [
                    (self.up, x * slots + ids, 0),
                    (self.down, x * slots + ids, 0),
                    (self.blocks, self.block(self.place.z)[: slots] + x * slots, 0),
                ],
            )

        away, self.home = combine(after, part(1 - x), part(x))
        self.got = self.place.swap_x(away)
        return [away]

    def sums(self):
        if not self.x_first:
            return [self.home, self.got]
        rows, cols = self.blocks.shape[1:]
        own = self.blocks.reshape(self.place.depth, self.slots, rows, cols)
        own = lax.dynamic_index_in_dim(own, self.place.z, 0, False)
        return [self.up, self.down, own]


def reduce_to_owners(place, gradient, source, slots):
    rows = gradient.shape[1]
    unit = rows // 8
    make = functools.partial(Flow, place, gradient, source, slots)
    b = make(0, 3 * unit, False)
    a = make(3 * unit, 3 * unit, True)
    c = make(6 * unit, 2 * unit, True)
    order = [b.pack, a.pack, c.pack, b.add_core, a.add_core]
    steps = place.depth - 2
    order += [b.add_z] * steps
    order += [c.add_core, a.add_x, b.last_z]
    order += [a.add_z] * steps
    order += [c.add_x]
    order += [c.add_z] * steps
    after = []
    for work in order:
        after = work(after)
    return [flow.sums() for flow in (b, a, c)]


def per_device(grads, owner, momentum):
    place = Place()
    owner_count = place.count
    matrices = owner.shape[0]
    slot_count = momentum.shape[1]
    head_rows = grads.shape[2]
    factor = 0.2 * math.sqrt(max(R, D))
    positions = jnp.arange(matrices, dtype=jnp.int32)
    same_owner = owner[:, None] == owner[None, :]
    earlier = positions[None, :] < positions[:, None]
    slot_rank = jnp.sum((same_owner & earlier).astype(jnp.int32), axis=1)
    spot = owner * slot_count + slot_rank
    spots = jnp.arange(owner_count * slot_count, dtype=jnp.int32)
    matches = spot[None, :] == spots[:, None]
    filled = jnp.any(matches, axis=1).astype(jnp.int32)
    source = jnp.sum(jnp.where(matches, positions[None, :], 0), axis=1)
    source = source.reshape(place.depth, PAIR, CORES, slot_count)
    held = lax.dynamic_slice_in_dim(
        filled, lax.axis_index("dp") * slot_count, slot_count, 0
    )

    parts = reduce_to_owners(place, grads[0], source, slot_count)
    new_momentum, rounded, gram = momentum_step(held, momentum[0], parts, owner_count)

    width = lax.axis_size("tensor")
    grams = [gram]
    for _ in range(width - 1):
        grams.append(
            lax.ppermute(
                grams[-1], "tensor", [(i, (i + 1) % width) for i in range(width)]
            )
        )
    result = orthogonalize(grams, rounded, factor)
    everything = lax.all_gather(result, "dp", axis=0, tiled=True)
    (update,) = combine([], (head_rows, [(everything, spot, 0)]))
    return (update, new_momentum[None])


def solution(mesh):
    in_specs = (P("dp", None, None, "tensor"), P(), P("dp", None, None, "tensor"))
    out_specs = (P(None, None, "tensor"), P("dp", None, None, "tensor"))
    return jax.shard_map(
        per_device, mesh=mesh, in_specs=in_specs, out_specs=out_specs, check_vma=False
    )
```

```python
import functools
import math

import jax
import jax.numpy as jnp
import numpy as np
from jax import lax
from jax.experimental import pallas as pl
from jax.experimental.pallas import tpu as pltpu
from jax.sharding import PartitionSpec as P

R = 128
D = 4096
ITERS = 5

COEF_A = 3.4445
COEF_B = -4.775
COEF_C = 2.0315
EPSILON = 1e-07
DECAY = 0.95

CORE_BIT = 1
X_BIT = 2
VMEM_BYTES = 24 * 1024 * 1024
MORE_VMEM_BYTES = 44 * 1024 * 1024


def in_vmem(count=1):
    return [pl.BlockSpec(memory_space=pltpu.VMEM)] * count


def anywhere(count=1):
    return [pl.BlockSpec(memory_space=pl.ANY)] * count


def in_hbm():
    return [pl.BlockSpec(memory_space=pltpu.HBM)]


def in_smem(count=1):
    return [pl.BlockSpec(memory_space=pltpu.SMEM)] * count


def limits(size=VMEM_BYTES):
    return pltpu.CompilerParams(vmem_limit_bytes=size)


def cost(size, flops=0):
    return pl.CostEstimate(flops=flops, bytes_accessed=size, transcendentals=0)


def nbytes(*arrays):
    return sum(math.prod(a.shape) * a.dtype.itemsize for a in arrays)


def pack_kernel(first, ids_ref, src_ref, *rest):
    out_ref, sem = rest[-2:]
    count, rows = out_ref.shape[:2]

    def copy(i):
        return pltpu.make_async_copy(
            src_ref.at[ids_ref[i], pl.ds(first, rows)], out_ref.at[i], sem.at[i]
        )

    @pl.loop(0, count)
    def _(i):
        copy(i).start()

    @pl.loop(0, count)
    def _(i):
        copy(i).wait()


def pack(after, src, ids, first, rows):
    count = ids.shape[0]
    out = jax.ShapeDtypeStruct((count, rows, src.shape[2]), src.dtype)
    return pl.pallas_call(
        functools.partial(pack_kernel, first),
        out_shape=out,
        in_specs=in_smem() + in_hbm() + anywhere(len(after)),
        out_specs=in_vmem()[0],
        scratch_shapes=[pltpu.SemaphoreType.DMA((count,))],
        compiler_params=limits(MORE_VMEM_BYTES),
        cost_estimate=cost(2 * nbytes(out)),
    )(ids, src, *after)


def add_taken_kernel(first, ids_ref, src_ref, got_ref, *rest):
    away_ref, home_ref, mine, sem = rest[-4:]
    count, rows = mine.shape[:2]
    half = count // 2

    def copy(i):
        return pltpu.make_async_copy(
            src_ref.at[ids_ref[i], pl.ds(first, rows)], mine.at[i], sem.at[i]
        )

    @pl.loop(0, count)
    def _(i):
        copy(i).start()

    for start, out_ref in ((0, away_ref), (half, home_ref)):

        @pl.loop(0, half)
        def _(i, start=start, out_ref=out_ref):
            copy(start + i).wait()
            out_ref[i] = got_ref[start + i] + mine[start + i]


def add_taken(after, src, ids, first, got):
    count, rows, cols = got.shape
    half = jax.ShapeDtypeStruct((count // 2, rows, cols), got.dtype)
    return pl.pallas_call(
        functools.partial(add_taken_kernel, first),
        out_shape=[half, half],
        in_specs=in_smem() + in_hbm() + in_vmem() + anywhere(len(after)),
        out_specs=in_vmem(2),
        scratch_shapes=[
            pltpu.VMEM(got.shape, got.dtype),
            pltpu.SemaphoreType.DMA((count,)),
        ],
        compiler_params=limits(MORE_VMEM_BYTES),
        cost_estimate=cost(3 * nbytes(got), nbytes(got) // 2),
    )(ids, src, got, *after)


def add_halves_kernel(home_ref, got_ref, *rest):
    away_out, home_out = rest[-2:]
    half = away_out.shape[0]
    for start, out_ref in ((0, away_out), (half, home_out)):

        @pl.loop(0, half)
        def _(i, start=start, out_ref=out_ref):
            out_ref[i] = home_ref[start + i] + got_ref[start + i]


def add_halves(after, home, got):
    count, rows, cols = got.shape
    half = jax.ShapeDtypeStruct((count // 2, rows, cols), got.dtype)
    return pl.pallas_call(
        add_halves_kernel,
        out_shape=[half, half],
        in_specs=in_vmem(2) + anywhere(len(after)),
        out_specs=in_vmem(2),
        compiler_params=limits(),
        cost_estimate=cost(3 * nbytes(got), nbytes(got) // 2),
    )(home, got, *after)


def spread_kernel(first, pieces, to_ref, *refs):
    piece_refs = refs[:pieces]
    out_ref, sem = refs[-2:]
    slots, rows = piece_refs[0].shape[:2]
    for wait in (False, True):
        for p in range(pieces):
            for s in range(slots):
                to = to_ref[p * slots + s]

                @pl.when(to >= 0)
                def _(p=p, s=s, to=to, wait=wait):
                    copy = pltpu.make_async_copy(
                        piece_refs[p].at[s],
                        out_ref.at[to, pl.ds(first, rows)],
                        sem.at[p, s],
                    )
                    if wait:
                        copy.wait()
                    else:
                        copy.start()


def spread(target, matrices, head_rows, pieces, to, first):
    slots, rows, cols = pieces[0].shape
    out = jax.ShapeDtypeStruct((matrices, head_rows, cols), pieces[0].dtype)
    count = len(pieces)
    more = [] if target is None else [target]
    return pl.pallas_call(
        functools.partial(spread_kernel, first, count),
        out_shape=out,
        in_specs=in_smem() + in_vmem(count) + anywhere(len(more)),
        out_specs=anywhere()[0],
        scratch_shapes=[pltpu.SemaphoreType.DMA((count, slots))],
        input_output_aliases={1 + count: 0} if more else {},
        compiler_params=limits(),
        cost_estimate=cost(2 * nbytes(*pieces)),
    )(to, *pieces, *more)


def momentum_kernel(scale, sizes, held_ref, momentum_ref, *rest):
    part_refs = rest[: sum(sizes)]
    next_ref, rounded_ref, gram_ref = rest[sum(sizes) :]
    held = held_ref[pl.program_id(0)] > 0
    first, used = 0, 0
    for size in sizes:
        total = None
        for ref in part_refs[used : used + size]:
            term = ref[0].astype(jnp.float32)
            total = term if total is None else total + term
        rows = total.shape[0]
        here = pl.ds(first, rows)
        mean = total * scale
        previous = momentum_ref[0, here]
        following = DECAY * previous + mean
        next_ref[0, here] = jnp.where(held, following, previous)
        rounded_ref[0, here] = (mean + DECAY * following).astype(jnp.bfloat16)
        first += rows
        used += size
    rounded = rounded_ref[0]
    gram_ref[0] = lax.dot_general(
        rounded, rounded, (((1,), (1,)), ((), ())), preferred_element_type=jnp.float32
    )


def momentum_step(held, momentum, parts, owner_count):
    slots, rows, cols = momentum.shape
    flat = [a for part in parts for a in part]
    return pl.pallas_call(
        functools.partial(
            momentum_kernel, 1.0 / owner_count, [len(part) for part in parts]
        ),
        grid=(slots,),
        out_shape=[
            jax.ShapeDtypeStruct((slots, rows, cols), jnp.float32),
            jax.ShapeDtypeStruct((slots, rows, cols), jnp.bfloat16),
            jax.ShapeDtypeStruct((slots, rows, rows), jnp.float32),
        ],
        in_specs=[
            pl.BlockSpec(memory_space=pltpu.SMEM),
            pl.BlockSpec((1, rows, cols), lambda s: (s, 0, 0)),
        ]
        + [pl.BlockSpec((1,) + a.shape[1:], lambda s: (s, 0, 0)) for a in flat],
        out_specs=[
            pl.BlockSpec((1, rows, cols), lambda s: (s, 0, 0)),
            pl.BlockSpec((1, rows, cols), lambda s: (s, 0, 0)),
            pl.BlockSpec((1, rows, rows), lambda s: (s, 0, 0)),
        ],
        compiler_params=limits(),
        cost_estimate=pl.CostEstimate(
            flops=2 * slots * rows * rows * cols,
            bytes_accessed=slots * rows * cols * 16,
            transcendentals=0,
        ),
    )(held, momentum, *flat)


def exact(a, b):
    return jnp.dot(
        a, b, preferred_element_type=jnp.float32, precision=lax.Precision.HIGHEST
    )


def orthogonalize_kernel(factor, slots, grams, *refs):
    gram_refs = refs[:grams]
    rounded_ref = refs[grams]
    out_refs = refs[grams + 1 :]
    rows = rounded_ref.shape[1]
    row_ids = lax.broadcasted_iota(jnp.int32, (rows, rows), 0)
    col_ids = lax.broadcasted_iota(jnp.int32, (rows, rows), 1)
    diagonal = row_ids == col_ids
    held = []
    for s in range(slots):
        gram = gram_refs[0][s]
        for ref in gram_refs[1:]:
            gram = gram + ref[s]
        squares = jnp.sum(
            jnp.sum(jnp.where(diagonal, gram, 0.0), axis=0, keepdims=True),
            axis=1,
            keepdims=True,
        )
        inverse = 1.0 / (jnp.sqrt(squares) + EPSILON)
        held.append([gram * inverse * inverse, None, inverse])
    for step in range(ITERS):
        squared = [exact(h[0], h[0]) for h in held]
        factors = [
            COEF_B * h[0] + COEF_C * q + jnp.where(diagonal, COEF_A, 0.0)
            for h, q in zip(held, squared)
        ]
        for h, m in zip(held, factors):
            h[1] = m if h[1] is None else exact(m, h[1])
        if step + 1 < ITERS:
            once = [exact(m, h[0]) for h, m in zip(held, factors)]
            for h, m, o in zip(held, factors, once):
                h[0] = exact(m, o)
    for s, h in enumerate(held):
        whole = h[1] * (factor * h[2])
        high = whole.astype(jnp.bfloat16)
        low = (whole - high.astype(jnp.float32)).astype(jnp.bfloat16)
        rounded = rounded_ref[s]
        result = (
            jnp.dot(high, rounded, preferred_element_type=jnp.float32)
            + jnp.dot(low, rounded, preferred_element_type=jnp.float32)
        ).astype(jnp.bfloat16)
        first = 0
        for out_ref in out_refs:
            out_ref[s] = result[first : first + out_ref.shape[1]]
            first += out_ref.shape[1]


def orthogonalize(grams, rounded, factor, shares):
    slots, rows, cols = rounded.shape
    return pl.pallas_call(
        functools.partial(orthogonalize_kernel, factor, slots, len(grams)),
        out_shape=[
            jax.ShapeDtypeStruct((slots, share, cols), jnp.bfloat16) for share in shares
        ],
        in_specs=in_vmem(len(grams) + 1),
        out_specs=in_vmem(len(shares)),
        compiler_params=limits(),
        cost_estimate=pl.CostEstimate(
            flops=slots * (4 * rows * rows * cols + 20 * 12 * rows * rows * rows),
            bytes_accessed=slots * rows * cols * 4,
            transcendentals=0,
        ),
    )(*grams, rounded)


def swap(value, bit):
    count = lax.axis_size("dp")
    return lax.ppermute(value, "dp", [(i, i ^ bit) for i in range(count)])


def z_bits():
    bits, bit = [], 2 * X_BIT
    while bit < lax.axis_size("dp"):
        bits.append(bit)
        bit *= 2
    return bits


def offsets(bits):
    if not bits:
        return [0]
    rest = offsets(bits[1:])
    return [bits[0] | o for o in rest] + rest


def sum_shares(unit, z):
    return (
        (3 * unit, z + [X_BIT]),
        (2 * unit, [X_BIT] + z),
        (3 * unit, [X_BIT] + z),
    )


def sum_order(depth):
    order = [(0, "pack"), (1, "pack"), (2, "pack"), (0, "add"), (1, "add")]
    order += [(0, "add"), (2, "add"), (1, "add")]
    for _ in range(depth - 1):
        order += [(0, "add"), (1, "add"), (2, "add")]
    return order + [(2, "add")]


class Flow:
    def __init__(self, gradient, by_owner, first, rows, bits):
        self.gradient, self.first, self.rows, self.bits = gradient, first, rows, bits
        me = lax.axis_index("dp")
        order = np.array(offsets(bits), np.int32)
        self.mine = by_owner[me ^ order].reshape(-1)
        self.theirs = by_owner[me ^ CORE_BIT ^ order].reshape(-1)
        self.done = 0

    def pack(self, after):
        sent = pack(after, self.gradient, self.theirs, self.first, self.rows)
        self.got = swap(sent, CORE_BIT)
        return [sent]

    def add(self, after):
        if self.done == 0:
            away, self.home = add_taken(
                after, self.gradient, self.mine, self.first, self.got
            )
        else:
            away, self.home = add_halves(after, self.home, self.got)
        self.got = swap(away, self.bits[self.done])
        self.done += 1
        return [away]


def gather_pieces(own, bits):
    pieces = {0: own}
    for bit in bits:
        for offset in list(pieces):
            pieces[offset | bit] = swap(pieces[offset], bit)
    return pieces


def per_device(grads, owner, momentum):
    owner_count = lax.axis_size("dp")
    me = lax.axis_index("dp")
    matrices = owner.shape[0]
    slot_count = momentum.shape[1]
    head_rows = grads.shape[2]
    factor = 0.2 * math.sqrt(max(R, D))
    positions = jnp.arange(matrices, dtype=jnp.int32)
    same_owner = owner[:, None] == owner[None, :]
    earlier = positions[None, :] < positions[:, None]
    slot_rank = jnp.sum((same_owner & earlier).astype(jnp.int32), axis=1)
    spot = owner * slot_count + slot_rank
    spots = jnp.arange(owner_count * slot_count, dtype=jnp.int32)
    matches = spot[None, :] == spots[:, None]
    filled = jnp.any(matches, axis=1)
    source = jnp.sum(jnp.where(matches, positions[None, :], 0), axis=1)
    by_owner = source.reshape(owner_count, slot_count)
    target = jnp.where(filled, source, -1).reshape(owner_count, slot_count)
    held = (target[me] >= 0).astype(jnp.int32)

    unit = head_rows // 8
    z = z_bits()
    flows, first = [], 0
    for rows, bits in sum_shares(unit, z):
        flows.append(Flow(grads[0], by_owner, first, rows, bits))
        first += rows
    after = []
    for flow, work in sum_order(len(z)):
        after = getattr(flows[flow], work)(after)
    parts = [(flow.home, flow.got) for flow in flows]
    new_momentum, rounded, gram = momentum_step(held, momentum[0], parts, owner_count)

    width = lax.axis_size("tensor")
    grams = [gram]
    for _ in range(width - 1):
        grams.append(
            lax.ppermute(
                grams[-1], "tensor", [(i, (i + 1) % width) for i in range(width)]
            )
        )
    back = z[::-1]
    shares = ((6 * unit, back + [X_BIT]), (2 * unit, back[:1] + [X_BIT] + back[1:]))
    blocks = orthogonalize(grams, rounded, factor, [rows for rows, _ in shares])
    update, first = None, 0
    for (rows, bits), block in zip(shares, blocks):
        pieces = gather_pieces(block, bits)
        names = list(pieces)
        half = len(names) // 2
        for part in (names[:half], names[half:]):
            there = [pieces[o] for o in part] + [swap(pieces[o], CORE_BIT) for o in part]
            places = np.array(part + [o | CORE_BIT for o in part], np.int32)
            to = target[me ^ places].reshape(-1)
            update = spread(update, matrices, head_rows, there, to, first)
        first += rows
    return (update, new_momentum[None])


def solution(mesh):
    in_specs = (P("dp", None, None, "tensor"), P(), P("dp", None, None, "tensor"))
    out_specs = (P(None, None, "tensor"), P("dp", None, None, "tensor"))
    return jax.shard_map(
        per_device, mesh=mesh, in_specs=in_specs, out_specs=out_specs, check_vma=False
    )
```

```python
import functools
import math

import jax
import jax.numpy as jnp
from jax import lax
from jax.experimental import pallas as pl
from jax.experimental.pallas import tpu as pltpu
from jax.sharding import PartitionSpec as P

R = 128
D = 4096
ITERS = 5

COEF_A = 3.4445
COEF_B = -4.775
COEF_C = 2.0315
EPSILON = 1e-07
DECAY = 0.95

CORE_BIT = 1
X_BIT = 2
VMEM_BYTES = 24 * 1024 * 1024
MORE_VMEM_BYTES = 44 * 1024 * 1024


def in_vmem(count=1):
    return [pl.BlockSpec(memory_space=pltpu.VMEM)] * count


def anywhere(count=1):
    return [pl.BlockSpec(memory_space=pl.ANY)] * count


def in_hbm():
    return [pl.BlockSpec(memory_space=pltpu.HBM)]


def in_smem(count=1):
    return [pl.BlockSpec(memory_space=pltpu.SMEM)] * count


def limits(size=VMEM_BYTES):
    return pltpu.CompilerParams(vmem_limit_bytes=size)


def small_cost():
    return pl.CostEstimate(flops=0, bytes_accessed=0, transcendentals=0)


def table_kernel(slots, me_ref, owner_ref, table_ref, used):
    spots, matrices = table_ref.shape[0], owner_ref.shape[0]

    @pl.loop(0, spots)
    def _(i):
        table_ref[i] = -1

    @pl.loop(0, spots // slots)
    def _(i):
        used[i] = 0

    @pl.loop(0, matrices)
    def _(m):
        at = owner_ref[m]
        rank = used[at]
        table_ref[(at ^ me_ref[0]) * slots + rank] = m
        used[at] = rank + 1


def build_table(me, owner, owners, slots):
    return pl.pallas_call(
        functools.partial(table_kernel, slots),
        out_shape=jax.ShapeDtypeStruct((owners * slots,), jnp.int32),
        in_specs=in_smem(2),
        out_specs=in_smem()[0],
        scratch_shapes=[pltpu.SMEM((owners,), jnp.int32)],
        cost_estimate=small_cost(),
    )(me, owner)


def starts(order, slots):
    return [
        (n * slots + s, offset * slots + s)
        for n, offset in enumerate(order)
        for s in range(slots)
    ]


def fetch(table_ref, src_ref, first, order, slots, into, sem):
    rows = into.shape[1]
    for item, place in starts(order, slots):
        matrix = jnp.maximum(table_ref[place], 0)
        pltpu.make_async_copy(
            src_ref.at[matrix, pl.ds(first, rows)], into.at[item], sem.at[item]
        ).start()
    return lambda i: pltpu.make_async_copy(
        src_ref.at[0, pl.ds(first, rows)], into.at[i], sem.at[i]
    )


def pack_kernel(first, order, slots, table_ref, src_ref, *rest):
    out_ref, sem = rest[-2:]
    copy = fetch(table_ref, src_ref, first, order, slots, out_ref, sem)

    @pl.loop(0, out_ref.shape[0])
    def _(i):
        copy(i).wait()


def pack(after, table, src, order, slots, first, rows):
    count = len(order) * slots
    return pl.pallas_call(
        functools.partial(pack_kernel, first, order, slots),
        out_shape=jax.ShapeDtypeStruct((count, rows, src.shape[2]), src.dtype),
        in_specs=in_smem() + in_hbm() + anywhere(len(after)),
        out_specs=in_vmem()[0],
        scratch_shapes=[pltpu.SemaphoreType.DMA((count,))],
        compiler_params=limits(MORE_VMEM_BYTES),
        cost_estimate=small_cost(),
    )(table, src, *after)


def add_taken_kernel(first, order, slots, parts, table_ref, src_ref, got_ref, *rest):
    mine, sem = rest[-2:]
    out_refs = rest[-2 - len(parts) : -2]
    copy = fetch(table_ref, src_ref, first, order, slots, mine, sem)
    start = 0
    for size, out_ref in zip(parts, out_refs):

        @pl.loop(0, size)
        def _(i, start=start, out_ref=out_ref):
            copy(start + i).wait()
            out_ref[i] = got_ref[start + i] + mine[start + i]

        start += size


def add_taken(after, table, src, order, slots, first, got, parts):
    count, rows, cols = got.shape
    return pl.pallas_call(
        functools.partial(add_taken_kernel, first, order, slots, parts),
        out_shape=[jax.ShapeDtypeStruct((n, rows, cols), got.dtype) for n in parts],
        in_specs=in_smem() + in_hbm() + in_vmem() + anywhere(len(after)),
        out_specs=in_vmem(len(parts)),
        scratch_shapes=[
            pltpu.VMEM(got.shape, got.dtype),
            pltpu.SemaphoreType.DMA((count,)),
        ],
        compiler_params=limits(MORE_VMEM_BYTES),
        cost_estimate=small_cost(),
    )(table, src, got, *after)


def combine_kernel(arrays, plans, *refs):
    sources = refs[:arrays]
    outs = refs[len(refs) - len(plans) :]
    for out_ref, items in zip(outs, plans):
        for i, terms in enumerate(items):
            total = sources[terms[0][0]][terms[0][1]]
            for at, item in terms[1:]:
                total = total + sources[at][item]
            out_ref[i] = total


def combine(after, *wanted):
    arrays, plans = [], []
    for items in wanted:
        plan = []
        for terms in items:
            found = []
            for array, item in terms:
                places = [i for i, a in enumerate(arrays) if a is array]
                if not places:
                    arrays.append(array)
                    places = [len(arrays) - 1]
                found.append((places[0], item))
            plan.append(tuple(found))
        plans.append(tuple(plan))
    shapes = []
    for items in wanted:
        sample = items[0][0][0]
        shapes.append(
            jax.ShapeDtypeStruct((len(items),) + sample.shape[1:], sample.dtype)
        )
    return pl.pallas_call(
        functools.partial(combine_kernel, len(arrays), tuple(plans)),
        out_shape=shapes,
        in_specs=in_vmem(len(arrays)) + anywhere(len(after)),
        out_specs=in_vmem(len(plans)),
        compiler_params=limits(),
        cost_estimate=small_cost(),
    )(*arrays, *after)


def joined(*arrays):
    return [[(array, i)] for array in arrays for i in range(array.shape[0])]


def summed(home, got, first, last):
    return [[(home, i), (got, i)] for i in range(first, last)]


def spread_kernel(plans, slots, table_ref, *refs):
    piece_refs = refs[: len(plans)]
    out_ref, sem = refs[-2:]
    for wait in (False, True):
        for p, (first, order) in enumerate(plans):
            for item, place in starts(order, slots):
                to = table_ref[place]

                @pl.when(to >= 0)
                def _(p=p, item=item, to=to, wait=wait, first=first):
                    rows = piece_refs[p].shape[1]
                    copy = pltpu.make_async_copy(
                        piece_refs[p].at[item],
                        out_ref.at[to, pl.ds(first, rows)],
                        sem.at[p, item],
                    )
                    if wait:
                        copy.wait()
                    else:
                        copy.start()


def spread(after, target, shape, table, slots, pieces):
    count = len(pieces)
    arrays = [array for array, _, _ in pieces]
    plans = tuple((first, tuple(order)) for _, first, order in pieces)
    most = max(a.shape[0] for a in arrays)
    more = [] if target is None else [target]
    after = [a for a in after if a is not target]
    return pl.pallas_call(
        functools.partial(spread_kernel, plans, slots),
        out_shape=jax.ShapeDtypeStruct(shape, arrays[0].dtype),
        in_specs=in_smem() + in_vmem(count) + anywhere(len(more) + len(after)),
        out_specs=anywhere()[0],
        scratch_shapes=[pltpu.SemaphoreType.DMA((count, most))],
        input_output_aliases={1 + count: 0} if more else {},
        compiler_params=limits(MORE_VMEM_BYTES),
        cost_estimate=small_cost(),
    )(table, *arrays, *more, *after)


def momentum_kernel(scale, sizes, held_ref, momentum_ref, *rest):
    part_refs = rest[: sum(sizes)]
    next_ref, rounded_ref, gram_ref = rest[sum(sizes) :]
    held = held_ref[pl.program_id(0)] >= 0
    first, used = 0, 0
    for size in sizes:
        total = None
        for ref in part_refs[used : used + size]:
            term = ref[0].astype(jnp.float32)
            total = term if total is None else total + term
        rows = total.shape[0]
        here = pl.ds(first, rows)
        mean = total * scale
        previous = momentum_ref[0, here]
        following = DECAY * previous + mean
        next_ref[0, here] = jnp.where(held, following, previous)
        rounded_ref[0, here] = (mean + DECAY * following).astype(jnp.bfloat16)
        first += rows
        used += size
    rounded = rounded_ref[0]
    gram_ref[0] = lax.dot_general(
        rounded, rounded, (((1,), (1,)), ((), ())), preferred_element_type=jnp.float32
    )


def momentum_step(held, momentum, parts, owner_count):
    slots, rows, cols = momentum.shape
    flat = [b for part in parts for b in part]
    return pl.pallas_call(
        functools.partial(
            momentum_kernel, 1.0 / owner_count, [len(part) for part in parts]
        ),
        grid=(slots,),
        out_shape=[
            jax.ShapeDtypeStruct((slots, rows, cols), jnp.float32),
            jax.ShapeDtypeStruct((slots, rows, cols), jnp.bfloat16),
            jax.ShapeDtypeStruct((slots, rows, rows), jnp.float32),
        ],
        in_specs=[
            pl.BlockSpec(memory_space=pltpu.SMEM),
            pl.BlockSpec((1, rows, cols), lambda s: (s, 0, 0)),
        ]
        + [
            pl.BlockSpec((1,) + b.array.shape[1:], lambda s, at=b.start: (s + at, 0, 0))
            for b in flat
        ],
        out_specs=[
            pl.BlockSpec((1, rows, cols), lambda s: (s, 0, 0)),
            pl.BlockSpec((1, rows, cols), lambda s: (s, 0, 0)),
            pl.BlockSpec((1, rows, rows), lambda s: (s, 0, 0)),
        ],
        compiler_params=limits(),
        cost_estimate=small_cost(),
    )(held, momentum, *[b.array for b in flat])


def exact(a, b):
    return jnp.dot(
        a, b, preferred_element_type=jnp.float32, precision=lax.Precision.HIGHEST
    )


def orthogonalize_kernel(factor, slots, grams, *refs):
    gram_refs = refs[:grams]
    rounded_ref = refs[grams]
    out_refs = refs[grams + 1 :]
    rows = rounded_ref.shape[1]
    row_ids = lax.broadcasted_iota(jnp.int32, (rows, rows), 0)
    col_ids = lax.broadcasted_iota(jnp.int32, (rows, rows), 1)
    diagonal = row_ids == col_ids
    held = []
    for s in range(slots):
        gram = gram_refs[0][s]
        for ref in gram_refs[1:]:
            gram = gram + ref[s]
        squares = jnp.sum(
            jnp.sum(jnp.where(diagonal, gram, 0.0), axis=0, keepdims=True),
            axis=1,
            keepdims=True,
        )
        inverse = 1.0 / (jnp.sqrt(squares) + EPSILON)
        held.append([gram * inverse * inverse, None, inverse])
    for step in range(ITERS):
        squared = [exact(h[0], h[0]) for h in held]
        factors = [
            COEF_B * h[0] + COEF_C * q + jnp.where(diagonal, COEF_A, 0.0)
            for h, q in zip(held, squared)
        ]
        for h, m in zip(held, factors):
            h[1] = m if h[1] is None else exact(m, h[1])
        if step + 1 < ITERS:
            once = [exact(m, h[0]) for h, m in zip(held, factors)]
            for h, m, o in zip(held, factors, once):
                h[0] = exact(m, o)
    for s, h in enumerate(held):
        whole = h[1] * (factor * h[2])
        high = whole.astype(jnp.bfloat16)
        low = (whole - high.astype(jnp.float32)).astype(jnp.bfloat16)
        rounded = rounded_ref[s]
        result = (
            jnp.dot(high, rounded, preferred_element_type=jnp.float32)
            + jnp.dot(low, rounded, preferred_element_type=jnp.float32)
        ).astype(jnp.bfloat16)
        first = 0
        for out_ref in out_refs:
            out_ref[s] = result[first : first + out_ref.shape[1]]
            first += out_ref.shape[1]


def orthogonalize(grams, rounded, factor, shares):
    slots, rows, cols = rounded.shape
    return pl.pallas_call(
        functools.partial(orthogonalize_kernel, factor, slots, len(grams)),
        out_shape=[
            jax.ShapeDtypeStruct((slots, share, cols), jnp.bfloat16) for share in shares
        ],
        in_specs=in_vmem(len(grams) + 1),
        out_specs=in_vmem(len(shares)),
        compiler_params=limits(),
        cost_estimate=small_cost(),
    )(*grams, rounded)


def swap(value, bit):
    count = lax.axis_size("dp")
    return lax.ppermute(value, "dp", [(i, i ^ bit) for i in range(count)])


def z_bits():
    bits, bit = [], 2 * X_BIT
    while bit < lax.axis_size("dp"):
        bits.append(bit)
        bit *= 2
    return bits


def offsets(bits):
    if not bits:
        return [0]
    rest = offsets(bits[1:])
    return [bits[0] | o for o in rest] + rest


def levels(bits):
    found = [[(0, -1)]]
    for _ in bits:
        longer = []
        for j, bit in enumerate(bits):
            longer += [(o | bit, j) for o, last in found[-1] if last < j]
        found.append(longer)
    return found


class Block:
    def __init__(self, array, start):
        self.array, self.start = array, start


def sum_to_owners(gradient, table, slots, bits, cut):
    rest = gradient.shape[1] - cut
    level = [[o for o, _ in found] for found in levels(bits)]
    last = {o: bits[j] for found in levels(bits) for o, j in found if j >= 0}
    top = len(bits)
    other_bits = bits[::-1] + [X_BIT]
    other_order = tuple(offsets(other_bits))

    def batch(k):
        order = [o | X_BIT for o in level[k]]
        return tuple(order + (level[k + 1] if k < top else []))

    batches = {k: batch(k) for k in range(top, -1, -1)}
    batches[-1] = (0,)
    merged = {k: batches[k] for k in range(top, 0, -1)}
    merged[0] = batches[0] + batches[-1]

    def send(order, first, rows, after):
        theirs = tuple(CORE_BIT | o for o in order)
        packed = pack(after, table, gradient, theirs, slots, first, rows)
        return packed, swap(packed, CORE_BIT)

    got, packed = {}, {}

    def take_off(k, after):
        packed[k], got[k] = send(merged[k], 0, cut, after)
        return [packed[k]]

    home = {}
    over_x = {}

    def take(k, after):
        order = merged[k]
        crossing = len(level[k]) * slots
        parts = (crossing,)
        if len(order) * slots > crossing:
            parts += (len(order) * slots - crossing,)
        made = add_taken(after, table, gradient, order, slots, 0, got[k], parts)
        over_x[k] = made[0]
        for n, o in enumerate(order[len(level[k]) :]):
            home[o] = Block(made[1], n * slots)
        return [made[0]]

    half = len(other_order) * slots // 2
    packed[None], other_got = send(other_order, cut, rest, [])
    after = take_off(top - 1, take_off(top, [packed[None]]))
    away, kept = add_taken(
        after, table, gradient, other_order, slots, cut, other_got, (half, half)
    )
    other_got = swap(away, other_bits[0])
    after = take(top, [away])
    x_got = swap(over_x[top], X_BIT)
    for k in range(top - 2, -1, -1):
        after = take_off(k, after)

    pending = {}
    for k in range(top, -1, -1):
        terms = {o: [] for o in level[k]}
        for n, o in enumerate(level[k]):
            terms[o].append(Block(x_got, n * slots))
        for o, value in pending.items():
            terms[o ^ last[o]].append(Block(value, 0))
        if k == 0:
            break
        if k == top:
            after = take(k - 1, after)
        wanted = []
        for o in level[k]:
            parts = [home[o]] + terms[o]
            wanted.append(
                [[(b.array, b.start + s) for b in parts] for s in range(slots)]
            )
        half //= 2
        wanted.append(summed(kept, other_got, 0, half))
        wanted.append(summed(kept, other_got, half, 2 * half))
        held_back = k == 1
        if held_back:
            wanted.append(joined(over_x[0]))
        made = list(combine(after, *wanted))
        after = [made[0]]
        if held_back:
            over_x[0] = made.pop()
        else:
            after = take(k - 2, after)
        pending = {o: swap(made[n], last[o]) for n, o in enumerate(level[k])}
        kept = made[-1]
        other_got = swap(made[-2], other_bits[top - k + 1])
        x_got = swap(over_x[k - 1], X_BIT)
    return [[home[0]] + terms[0], [Block(kept, 0), Block(other_got, 0)]]


def spread_updates(blocks, table, slots, bits, cut, shape):
    level = levels(bits)
    last = [dict(found) for found in level]
    own, cur = blocks
    top = len(bits)
    cur_order = [0]
    other_bits = [X_BIT] + bits
    front, front_order = own, [0]
    pieces = {0: own}
    after, update, waiting = [], None, []
    for k in range(top + 1):
        x_got = swap(front, X_BIT)
        longer = {}
        for j, bit in enumerate(bits):
            for o, at in level[k]:
                if at < j:
                    longer[o | bit] = swap(pieces[o], bit)
        other_got = swap(cur, other_bits[k])
        made = [(front, 0, front_order), (x_got, 0, [X_BIT | o for o in front_order])]
        if k == top:
            break
        if k == 0:
            (both,) = combine(after, joined(front, x_got))
            made = [(both, 0, front_order + [X_BIT | o for o in front_order])]
            after = [both]
        order = [o for o, _ in level[k + 1]]
        wanted = [joined(*[longer[o] for o in order]), joined(cur, other_got)]
        front, cur = combine(after, *wanted)
        after = [front]
        pieces = longer
        front_order = order
        cur_order = cur_order + [other_bits[k] | o for o in cur_order]
        if waiting:
            update = spread(after, update, shape, table, slots, waiting)
            after = [update]
        waiting = []
        for array, first, order in made:
            waiting.append((array, first, order))
            waiting.append((swap(array, CORE_BIT), first, [CORE_BIT | o for o in order]))
    update = spread(after, update, shape, table, slots, waiting)

    def with_core(array, first, order):
        return [
            (array, first, order),
            (swap(array, CORE_BIT), first, [CORE_BIT | o for o in order]),
        ]

    waiting = with_core(front, 0, front_order) + with_core(cur, cut, cur_order)
    update = spread([], update, shape, table, slots, waiting)
    waiting = with_core(x_got, 0, [X_BIT | o for o in front_order])
    waiting += with_core(other_got, cut, [other_bits[top] | o for o in cur_order])
    return spread([], update, shape, table, slots, waiting)


def per_device(grads, owner, momentum):
    owner_count = lax.axis_size("dp")
    matrices = owner.shape[0]
    slot_count = momentum.shape[1]
    head_rows, cols = grads.shape[2:]
    factor = 0.2 * math.sqrt(max(R, D))
    me = lax.axis_index("dp").astype(jnp.int32).reshape(1)
    table = build_table(me, owner, owner_count, slot_count)

    cut = head_rows * 3 // 4
    bits = z_bits()[::-1]
    parts = sum_to_owners(grads[0], table, slot_count, bits, cut)
    new_momentum, rounded, gram = momentum_step(table, momentum[0], parts, owner_count)

    width = lax.axis_size("tensor")
    grams = [gram]
    for _ in range(width - 1):
        grams.append(
            lax.ppermute(
                grams[-1], "tensor", [(i, (i + 1) % width) for i in range(width)]
            )
        )
    blocks = orthogonalize(grams, rounded, factor, [cut, head_rows - cut])
    shape = (matrices, head_rows, cols)
    update = spread_updates(blocks, table, slot_count, bits, cut, shape)
    return (update, new_momentum[None])


def solution(mesh):
    in_specs = (P("dp", None, None, "tensor"), P(), P("dp", None, None, "tensor"))
    out_specs = (P(None, None, "tensor"), P("dp", None, None, "tensor"))
    return jax.shard_map(
        per_device, mesh=mesh, in_specs=in_specs, out_specs=out_specs, check_vma=False
    )
```

```python
import functools
import math

import jax
import jax.numpy as jnp
from jax import lax
from jax.experimental import pallas as pl
from jax.experimental.pallas import tpu as pltpu
from jax.sharding import PartitionSpec as P

R = 128
D = 4096
ITERS = 5

COEF_A = 3.4445
COEF_B = -4.775
COEF_C = 2.0315
EPSILON = 1e-07
DECAY = 0.95

CORE_BIT = 1
X_BIT = 2
VMEM_BYTES = 24 * 1024 * 1024
MORE_VMEM_BYTES = 44 * 1024 * 1024


def in_vmem(count=1):
    return [pl.BlockSpec(memory_space=pltpu.VMEM)] * count


def anywhere(count=1):
    return [pl.BlockSpec(memory_space=pl.ANY)] * count


def in_hbm():
    return [pl.BlockSpec(memory_space=pltpu.HBM)]


def in_smem(count=1):
    return [pl.BlockSpec(memory_space=pltpu.SMEM)] * count


def limits(size=VMEM_BYTES):
    return pltpu.CompilerParams(vmem_limit_bytes=size)


def small_cost():
    return pl.CostEstimate(flops=0, bytes_accessed=0, transcendentals=0)


def token():
    return jax.ShapeDtypeStruct((8, 128), jnp.float32)


def table_kernel(slots, me_ref, owner_ref, table_ref, used):
    spots, matrices = table_ref.shape[0], owner_ref.shape[0]

    @pl.loop(0, spots)
    def _(i):
        table_ref[i] = -1

    @pl.loop(0, spots // slots)
    def _(i):
        used[i] = 0

    @pl.loop(0, matrices)
    def _(m):
        at = owner_ref[m]
        rank = used[at]
        table_ref[(at ^ me_ref[0]) * slots + rank] = m
        used[at] = rank + 1


def build_table(me, owner, owners, slots):
    return pl.pallas_call(
        functools.partial(table_kernel, slots),
        out_shape=jax.ShapeDtypeStruct((owners * slots,), jnp.int32),
        in_specs=in_smem(2),
        out_specs=in_smem()[0],
        scratch_shapes=[pltpu.SMEM((owners,), jnp.int32)],
        cost_estimate=small_cost(),
    )(me, owner)


def starts(order, slots):
    return [
        (n * slots + s, offset * slots + s)
        for n, offset in enumerate(order)
        for s in range(slots)
    ]


def fetch(table_ref, src_ref, first, order, slots, into, sem):
    rows = into.shape[1]
    for item, place in starts(order, slots):
        matrix = jnp.maximum(table_ref[place], 0)
        pltpu.make_async_copy(
            src_ref.at[matrix, pl.ds(first, rows)], into.at[item], sem.at[item]
        ).start()
    return lambda i: pltpu.make_async_copy(
        src_ref.at[0, pl.ds(first, rows)], into.at[i], sem.at[i]
    )


def pack_kernel(first, order, slots, table_ref, src_ref, *rest):
    out_ref, sem = rest[-2:]
    copy = fetch(table_ref, src_ref, first, order, slots, out_ref, sem)

    @pl.loop(0, out_ref.shape[0])
    def _(i):
        copy(i).wait()


def pack(after, table, src, order, slots, first, rows):
    count = len(order) * slots
    return pl.pallas_call(
        functools.partial(pack_kernel, first, order, slots),
        out_shape=jax.ShapeDtypeStruct((count, rows, src.shape[2]), src.dtype),
        in_specs=in_smem() + in_hbm() + anywhere(len(after)),
        out_specs=in_vmem()[0],
        scratch_shapes=[pltpu.SemaphoreType.DMA((count,))],
        compiler_params=limits(MORE_VMEM_BYTES),
        cost_estimate=small_cost(),
    )(table, src, *after)


def add_taken_kernel(first, order, slots, parts, table_ref, src_ref, got_ref, *rest):
    mine, sem = rest[-2:]
    out_refs = rest[-2 - len(parts) : -2]
    copy = fetch(table_ref, src_ref, first, order, slots, mine, sem)
    start = 0
    for size, out_ref in zip(parts, out_refs):

        @pl.loop(0, size)
        def _(i, start=start, out_ref=out_ref):
            copy(start + i).wait()
            out_ref[i] = got_ref[start + i] + mine[start + i]

        start += size


def add_taken(after, table, src, order, slots, first, got, parts):
    count, rows, cols = got.shape
    return pl.pallas_call(
        functools.partial(add_taken_kernel, first, order, slots, parts),
        out_shape=[jax.ShapeDtypeStruct((n, rows, cols), got.dtype) for n in parts],
        in_specs=in_smem() + in_hbm() + in_vmem() + anywhere(len(after)),
        out_specs=in_vmem(len(parts)),
        scratch_shapes=[
            pltpu.VMEM(got.shape, got.dtype),
            pltpu.SemaphoreType.DMA((count,)),
        ],
        compiler_params=limits(MORE_VMEM_BYTES),
        cost_estimate=small_cost(),
    )(table, src, got, *after)


def combine_kernel(arrays, plans, *refs):
    sources = refs[:arrays]
    outs = refs[len(refs) - len(plans) :]
    for out_ref, items in zip(outs, plans):
        for i, terms in enumerate(items):
            total = sources[terms[0][0]][terms[0][1]]
            for at, item in terms[1:]:
                total = total + sources[at][item]
            out_ref[i] = total


def combine(after, *wanted):
    arrays, plans = [], []
    for items in wanted:
        plan = []
        for terms in items:
            found = []
            for array, item in terms:
                places = [i for i, a in enumerate(arrays) if a is array]
                if not places:
                    arrays.append(array)
                    places = [len(arrays) - 1]
                found.append((places[0], item))
            plan.append(tuple(found))
        plans.append(tuple(plan))
    shapes = []
    for items in wanted:
        sample = items[0][0][0]
        shapes.append(
            jax.ShapeDtypeStruct((len(items),) + sample.shape[1:], sample.dtype)
        )
    return pl.pallas_call(
        functools.partial(combine_kernel, len(arrays), tuple(plans)),
        out_shape=shapes,
        in_specs=in_vmem(len(arrays)) + anywhere(len(after)),
        out_specs=in_vmem(len(plans)),
        compiler_params=limits(),
        cost_estimate=small_cost(),
    )(*arrays, *after)


def joined(*arrays):
    return [[(array, i)] for array in arrays for i in range(array.shape[0])]


def summed(home, got, first, last):
    return [[(home, i), (got, i)] for i in range(first, last)]


def spread_kernel(plans, slots, table_ref, *refs):
    piece_refs = refs[: len(plans)]
    out_ref, token_ref, sem = refs[-3:]
    token_ref[...] = jnp.zeros_like(token_ref)
    for wait in (False, True):
        for p, (first, order) in enumerate(plans):
            for item, place in starts(order, slots):
                to = table_ref[place]

                @pl.when(to >= 0)
                def _(p=p, item=item, to=to, wait=wait, first=first):
                    rows = piece_refs[p].shape[1]
                    copy = pltpu.make_async_copy(
                        piece_refs[p].at[item],
                        out_ref.at[to, pl.ds(first, rows)],
                        sem.at[p, item],
                    )
                    if wait:
                        copy.wait()
                    else:
                        copy.start()


def spread(after, target, shape, table, slots, pieces):
    count = len(pieces)
    arrays = [array for array, _, _ in pieces]
    plans = tuple((first, tuple(order)) for _, first, order in pieces)
    most = max(a.shape[0] for a in arrays)
    more = [] if target is None else [target]
    return pl.pallas_call(
        functools.partial(spread_kernel, plans, slots),
        out_shape=[jax.ShapeDtypeStruct(shape, arrays[0].dtype), token()],
        in_specs=in_smem() + in_vmem(count) + anywhere(len(more) + len(after)),
        out_specs=anywhere() + in_vmem(),
        scratch_shapes=[pltpu.SemaphoreType.DMA((count, most))],
        input_output_aliases={1 + count: 0} if more else {},
        compiler_params=limits(MORE_VMEM_BYTES),
        cost_estimate=small_cost(),
    )(table, *arrays, *more, *after)


def mean_rows(scale, sizes, refs):
    first, used = 0, 0
    for size in sizes:
        total = None
        for ref, item in refs[used : used + size]:
            term = ref[item].astype(jnp.float32)
            total = term if total is None else total + term
        yield first, total * scale
        first += total.shape[0]
        used += size


def nesterov_kernel(scale, sizes, items, momentum_ref, *rest):
    part_refs, (rounded_ref, gram_ref) = rest[: len(items)], rest[len(items) :]
    for s in range(momentum_ref.shape[0]):
        refs = [(ref, item + s) for ref, item in zip(part_refs, items)]
        for first, mean in mean_rows(scale, sizes, refs):
            here = pl.ds(first, mean.shape[0])
            following = DECAY * momentum_ref[s, here] + mean
            rounded_ref[s, here] = (mean + DECAY * following).astype(jnp.bfloat16)
        rounded = rounded_ref[s]
        gram_ref[s] = lax.dot_general(
            rounded,
            rounded,
            (((1,), (1,)), ((), ())),
            preferred_element_type=jnp.float32,
        )


def momentum_kernel(scale, sizes, count, table_ref, momentum_ref, *rest):
    part_refs, (next_ref, token_ref) = rest[:count], rest[-2:]
    token_ref[...] = jnp.zeros_like(token_ref)
    held = table_ref[pl.program_id(0)] >= 0
    for first, mean in mean_rows(scale, sizes, [(ref, 0) for ref in part_refs]):
        here = pl.ds(first, mean.shape[0])
        previous = momentum_ref[0, here]
        next_ref[0, here] = jnp.where(held, DECAY * previous + mean, previous)


def nesterov_step(momentum, parts, owner_count):
    slots, rows, cols = momentum.shape
    flat = [b for part in parts for b in part]
    sizes = [len(part) for part in parts]
    items = [b.start for b in flat]
    return pl.pallas_call(
        functools.partial(nesterov_kernel, 1.0 / owner_count, sizes, items),
        out_shape=[
            jax.ShapeDtypeStruct((slots, rows, cols), jnp.bfloat16),
            jax.ShapeDtypeStruct((slots, rows, rows), jnp.float32),
        ],
        in_specs=in_vmem(1 + len(flat)),
        out_specs=in_vmem(2),
        compiler_params=limits(),
        cost_estimate=small_cost(),
    )(momentum, *[b.array for b in flat])


def momentum_step(after, table, momentum, parts, owner_count):
    slots, rows, cols = momentum.shape
    flat = [b for part in parts for b in part]
    sizes = [len(part) for part in parts]
    return pl.pallas_call(
        functools.partial(momentum_kernel, 1.0 / owner_count, sizes, len(flat)),
        grid=(slots,),
        out_shape=[jax.ShapeDtypeStruct((slots, rows, cols), jnp.float32), token()],
        in_specs=in_smem()
        + [pl.BlockSpec((1, rows, cols), lambda s: (s, 0, 0))]
        + [
            pl.BlockSpec((1,) + b.array.shape[1:], lambda s, at=b.start: (s + at, 0, 0))
            for b in flat
        ]
        + anywhere(len(after)),
        out_specs=[
            pl.BlockSpec((1, rows, cols), lambda s: (s, 0, 0)),
            pl.BlockSpec((8, 128), lambda s: (0, 0)),
        ],
        compiler_params=limits(),
        cost_estimate=small_cost(),
    )(table, momentum, *[b.array for b in flat], *after)


def exact(a, b):
    return jnp.dot(
        a, b, preferred_element_type=jnp.float32, precision=lax.Precision.HIGHEST
    )


def orthogonalize_kernel(factor, slots, grams, *refs):
    gram_refs = refs[:grams]
    rounded_ref = refs[grams]
    out_refs = refs[grams + 1 :]
    rows = rounded_ref.shape[1]
    row_ids = lax.broadcasted_iota(jnp.int32, (rows, rows), 0)
    col_ids = lax.broadcasted_iota(jnp.int32, (rows, rows), 1)
    diagonal = row_ids == col_ids
    held = []
    for s in range(slots):
        gram = gram_refs[0][s]
        for ref in gram_refs[1:]:
            gram = gram + ref[s]
        squares = jnp.sum(
            jnp.sum(jnp.where(diagonal, gram, 0.0), axis=0, keepdims=True),
            axis=1,
            keepdims=True,
        )
        inverse = 1.0 / (jnp.sqrt(squares) + EPSILON)
        held.append([gram * inverse * inverse, None, inverse])
    for step in range(ITERS):
        squared = [exact(h[0], h[0]) for h in held]
        factors = [
            COEF_B * h[0] + COEF_C * q + jnp.where(diagonal, COEF_A, 0.0)
            for h, q in zip(held, squared)
        ]
        for h, m in zip(held, factors):
            h[1] = m if h[1] is None else exact(m, h[1])
        if step + 1 < ITERS:
            once = [exact(m, h[0]) for h, m in zip(held, factors)]
            for h, m, o in zip(held, factors, once):
                h[0] = exact(m, o)
    for s, h in enumerate(held):
        whole = h[1] * (factor * h[2])
        high = whole.astype(jnp.bfloat16)
        low = (whole - high.astype(jnp.float32)).astype(jnp.bfloat16)
        rounded = rounded_ref[s]
        result = (
            jnp.dot(high, rounded, preferred_element_type=jnp.float32)
            + jnp.dot(low, rounded, preferred_element_type=jnp.float32)
        ).astype(jnp.bfloat16)
        first = 0
        for out_ref in out_refs:
            out_ref[s] = result[first : first + out_ref.shape[1]]
            first += out_ref.shape[1]


def orthogonalize(grams, rounded, factor, shares):
    slots, rows, cols = rounded.shape
    return pl.pallas_call(
        functools.partial(orthogonalize_kernel, factor, slots, len(grams)),
        out_shape=[
            jax.ShapeDtypeStruct((slots, share, cols), jnp.bfloat16) for share in shares
        ],
        in_specs=in_vmem(len(grams) + 1),
        out_specs=in_vmem(len(shares)),
        compiler_params=limits(),
        cost_estimate=small_cost(),
    )(*grams, rounded)


def swap(value, bit):
    count = lax.axis_size("dp")
    return lax.ppermute(value, "dp", [(i, i ^ bit) for i in range(count)])


def z_bits():
    bits, bit = [], 2 * X_BIT
    while bit < lax.axis_size("dp"):
        bits.append(bit)
        bit *= 2
    return bits


def offsets(bits):
    if not bits:
        return [0]
    rest = offsets(bits[1:])
    return [bits[0] | o for o in rest] + rest


def levels(bits):
    found = [[(0, -1)]]
    for _ in bits:
        longer = []
        for j, bit in enumerate(bits):
            longer += [(o | bit, j) for o, last in found[-1] if last < j]
        found.append(longer)
    return found


class Block:
    def __init__(self, array, start):
        self.array, self.start = array, start


def sum_to_owners(gradient, table, slots, bits, cut):
    rest = gradient.shape[1] - cut
    level = [[o for o, _ in found] for found in levels(bits)]
    last = {o: bits[j] for found in levels(bits) for o, j in found if j >= 0}
    top = len(bits)
    other_bits = bits[::-1] + [X_BIT]
    other_order = tuple(offsets(other_bits))

    def batch(k):
        order = [o | X_BIT for o in level[k]]
        return tuple(order + (level[k + 1] if k < top else []))

    batches = {k: batch(k) for k in range(top, -1, -1)}
    batches[-1] = (0,)
    merged = {k: batches[k] for k in range(top, 0, -1)}
    merged[0] = batches[0] + batches[-1]

    def send(order, first, rows, after):
        theirs = tuple(CORE_BIT | o for o in order)
        packed = pack(after, table, gradient, theirs, slots, first, rows)
        return packed, swap(packed, CORE_BIT)

    got, packed = {}, {}

    def take_off(k, after):
        packed[k], got[k] = send(merged[k], 0, cut, after)
        return [packed[k]]

    home = {}
    over_x = {}

    def take(k, after):
        order = merged[k]
        crossing = len(level[k]) * slots
        parts = (crossing,)
        if len(order) * slots > crossing:
            parts += (len(order) * slots - crossing,)
        made = add_taken(after, table, gradient, order, slots, 0, got[k], parts)
        over_x[k] = made[0]
        for n, o in enumerate(order[len(level[k]) :]):
            home[o] = Block(made[1], n * slots)
        return [made[0]]

    half = len(other_order) * slots // 2
    packed[None], other_got = send(other_order, cut, rest, [])
    after = take_off(top - 1, take_off(top, [packed[None]]))
    away, kept = add_taken(
        after, table, gradient, other_order, slots, cut, other_got, (half, half)
    )
    other_got = swap(away, other_bits[0])
    after = take(top, [away])
    x_got = swap(over_x[top], X_BIT)
    pending = {}
    for k in range(top, -1, -1):
        terms = {o: [] for o in level[k]}
        for n, o in enumerate(level[k]):
            terms[o].append(Block(x_got, n * slots))
        for o, value in pending.items():
            terms[o ^ last[o]].append(Block(value, 0))
        if k == 0:
            break
        if k == top:
            after = take(k - 1, after)
        wanted = []
        for o in level[k]:
            parts = [home[o]] + terms[o]
            wanted.append(
                [[(b.array, b.start + s) for b in parts] for s in range(slots)]
            )
        half //= 2
        wanted.append(summed(kept, other_got, 0, half))
        wanted.append(summed(kept, other_got, half, 2 * half))
        held_back = k == 1
        if held_back:
            wanted.append(joined(over_x[0]))
        made = list(combine(after, *wanted))
        after = [made[0]]
        if held_back:
            over_x[0] = made.pop()
        else:
            if k == top:
                for n in range(top - 2, -1, -1):
                    after = take_off(n, after)
            after = take(k - 2, after)
        pending = {o: swap(made[n], last[o]) for n, o in enumerate(level[k])}
        kept = made[-1]
        other_got = swap(made[-2], other_bits[top - k + 1])
        x_got = swap(over_x[k - 1], X_BIT)
    return [[home[0]] + terms[0], [Block(kept, 0), Block(other_got, 0)]]


def spread_updates(blocks, table, slots, bits, cut, shape, early):
    level = levels(bits)
    last = [dict(found) for found in level]
    own, cur = blocks
    top = len(bits)
    cur_order = [0]
    other_bits = [X_BIT] + bits
    front, front_order = own, [0]
    pieces = {0: own}
    after, update = [early], None

    def with_core(array, first, order):
        return [
            (array, first, order),
            (swap(array, CORE_BIT), first, [CORE_BIT | o for o in order]),
        ]

    for k in range(top + 1):
        x_got = swap(front, X_BIT)
        longer = {}
        for j, bit in enumerate(bits):
            for o, at in level[k]:
                if at < j:
                    longer[o | bit] = swap(pieces[o], bit)
        other_got = swap(cur, other_bits[k])
        crossed = (x_got, 0, [X_BIT | o for o in front_order])
        crossed_other = (other_got, cut, [other_bits[k] | o for o in cur_order])
        if k == top:
            break
        if k == 0:
            (both,) = combine(after, joined(front, x_got))
            waiting = with_core(both, 0, front_order + crossed[2])
            after = [both]
        else:
            update, ran = spread(after, update, shape, table, slots, waiting)
            waiting = with_core(*crossed)
            after = [ran]
        front_order = [o for o, _ in level[k + 1]]
        wanted = [joined(*[longer[o] for o in front_order]), joined(cur, other_got)]
        front, cur = combine(after, *wanted)
        after = [front]
        pieces = longer
        cur_order = cur_order + crossed_other[2]
        waiting += with_core(front, 0, front_order)
    waiting += with_core(cur, cut, cur_order)
    update, _ = spread(after, update, shape, table, slots, waiting)
    waiting = with_core(*crossed) + with_core(*crossed_other)
    return spread([], update, shape, table, slots, waiting)[0]


def per_device(grads, owner, momentum):
    owner_count = lax.axis_size("dp")
    matrices = owner.shape[0]
    slot_count = momentum.shape[1]
    head_rows, cols = grads.shape[2:]
    factor = 0.2 * math.sqrt(max(R, D))
    me = lax.axis_index("dp").astype(jnp.int32).reshape(1)
    table = build_table(me, owner, owner_count, slot_count)

    cut = head_rows * 3 // 4
    bits = z_bits()[::-1]
    parts = sum_to_owners(grads[0], table, slot_count, bits, cut)
    rounded, gram = nesterov_step(momentum[0], parts, owner_count)

    width = lax.axis_size("tensor")
    grams = [gram]
    for _ in range(width - 1):
        grams.append(
            lax.ppermute(
                grams[-1], "tensor", [(i, (i + 1) % width) for i in range(width)]
            )
        )
    blocks = orthogonalize(grams, rounded, factor, [cut, head_rows - cut])
    new_momentum, early = momentum_step(
        blocks[:1], table, momentum[0], parts, owner_count
    )
    shape = (matrices, head_rows, cols)
    update = spread_updates(
        blocks, table, slot_count, bits, cut, shape, early
    )
    return (update, new_momentum[None])


def solution(mesh):
    in_specs = (P("dp", None, None, "tensor"), P(), P("dp", None, None, "tensor"))
    out_specs = (P(None, None, "tensor"), P("dp", None, None, "tensor"))
    return jax.shard_map(
        per_device, mesh=mesh, in_specs=in_specs, out_specs=out_specs, check_vma=False
    )
```

```python
import functools
import math

import jax
import jax.numpy as jnp
from jax import lax
from jax.experimental import pallas as pl
from jax.experimental.pallas import tpu as pltpu
from jax.sharding import PartitionSpec as P

R = 128
D = 4096
ITERS = 5

COEF_A = 3.4445
COEF_B = -4.775
COEF_C = 2.0315
EPSILON = 1e-07
DECAY = 0.95

CORE_BIT = 1
X_BIT = 2
VMEM_BYTES = 24 * 1024 * 1024
MORE_VMEM_BYTES = 44 * 1024 * 1024


def in_vmem(count=1):
    return [pl.BlockSpec(memory_space=pltpu.VMEM)] * count


def anywhere(count=1):
    return [pl.BlockSpec(memory_space=pl.ANY)] * count


def in_hbm():
    return [pl.BlockSpec(memory_space=pltpu.HBM)]


def in_smem(count=1):
    return [pl.BlockSpec(memory_space=pltpu.SMEM)] * count


def limits(size=VMEM_BYTES):
    return pltpu.CompilerParams(vmem_limit_bytes=size)


def small_cost():
    return pl.CostEstimate(flops=0, bytes_accessed=0, transcendentals=0)


def token():
    return jax.ShapeDtypeStruct((8, 128), jnp.float32)


def table_kernel(slots, me_ref, owner_ref, table_ref, used):
    spots, matrices = table_ref.shape[0], owner_ref.shape[0]

    @pl.loop(0, spots)
    def _(i):
        table_ref[i] = -1

    @pl.loop(0, spots // slots)
    def _(i):
        used[i] = 0

    @pl.loop(0, matrices)
    def _(m):
        at = owner_ref[m]
        rank = used[at]
        table_ref[(at ^ me_ref[0]) * slots + rank] = m
        used[at] = rank + 1


def build_table(me, owner, owners, slots):
    return pl.pallas_call(
        functools.partial(table_kernel, slots),
        out_shape=jax.ShapeDtypeStruct((owners * slots,), jnp.int32),
        in_specs=in_smem(2),
        out_specs=in_smem()[0],
        scratch_shapes=[pltpu.SMEM((owners,), jnp.int32)],
        cost_estimate=small_cost(),
    )(me, owner)


def starts(order, slots):
    return [
        (n * slots + s, offset * slots + s)
        for n, offset in enumerate(order)
        for s in range(slots)
    ]


def fetch(table_ref, src_ref, first, order, slots, into, sem):
    rows = into.shape[1]
    for item, place in starts(order, slots):
        matrix = jnp.maximum(table_ref[place], 0)
        pltpu.make_async_copy(
            src_ref.at[matrix, pl.ds(first, rows)], into.at[item], sem.at[item]
        ).start()
    return lambda i: pltpu.make_async_copy(
        src_ref.at[0, pl.ds(first, rows)], into.at[i], sem.at[i]
    )


def pack_kernel(first, orders, slots, table_ref, src_ref, *rest):
    out_refs = rest[-2 * len(orders) : -len(orders)]
    sems = rest[-len(orders) :]
    copies = [
        fetch(table_ref, src_ref, first, order, slots, out_ref, sem)
        for order, out_ref, sem in zip(orders, out_refs, sems)
    ]
    for copy, out_ref in zip(copies, out_refs):

        @pl.loop(0, out_ref.shape[0])
        def _(i, copy=copy):
            copy(i).wait()


def pack(after, table, src, orders, slots, first, rows):
    counts = [len(order) * slots for order in orders]
    return pl.pallas_call(
        functools.partial(pack_kernel, first, tuple(orders), slots),
        out_shape=[
            jax.ShapeDtypeStruct((n, rows, src.shape[2]), src.dtype) for n in counts
        ],
        in_specs=in_smem() + in_hbm() + anywhere(len(after)),
        out_specs=in_vmem(len(orders)),
        scratch_shapes=[pltpu.SemaphoreType.DMA((n,)) for n in counts],
        compiler_params=limits(MORE_VMEM_BYTES),
        cost_estimate=small_cost(),
    )(table, src, *after)


def add_taken_kernel(first, order, slots, parts, table_ref, src_ref, got_ref, *rest):
    mine, sem = rest[-2:]
    out_refs = rest[-2 - len(parts) : -2]
    copy = fetch(table_ref, src_ref, first, order, slots, mine, sem)
    start = 0
    for size, out_ref in zip(parts, out_refs):

        @pl.loop(0, size)
        def _(i, start=start, out_ref=out_ref):
            copy(start + i).wait()
            out_ref[i] = got_ref[start + i] + mine[start + i]

        start += size


def add_taken(after, table, src, order, slots, first, got, parts):
    count, rows, cols = got.shape
    return pl.pallas_call(
        functools.partial(add_taken_kernel, first, order, slots, parts),
        out_shape=[jax.ShapeDtypeStruct((n, rows, cols), got.dtype) for n in parts],
        in_specs=in_smem() + in_hbm() + in_vmem() + anywhere(len(after)),
        out_specs=in_vmem(len(parts)),
        scratch_shapes=[
            pltpu.VMEM(got.shape, got.dtype),
            pltpu.SemaphoreType.DMA((count,)),
        ],
        compiler_params=limits(MORE_VMEM_BYTES),
        cost_estimate=small_cost(),
    )(table, src, got, *after)


def combine_kernel(arrays, plans, *refs):
    sources = refs[:arrays]
    outs = refs[len(refs) - len(plans) :]
    for out_ref, items in zip(outs, plans):
        for i, terms in enumerate(items):
            total = sources[terms[0][0]][terms[0][1]]
            for at, item in terms[1:]:
                total = total + sources[at][item]
            out_ref[i] = total


def combine(after, *wanted):
    arrays, plans = [], []
    for items in wanted:
        plan = []
        for terms in items:
            found = []
            for array, item in terms:
                places = [i for i, a in enumerate(arrays) if a is array]
                if not places:
                    arrays.append(array)
                    places = [len(arrays) - 1]
                found.append((places[0], item))
            plan.append(tuple(found))
        plans.append(tuple(plan))
    shapes = []
    for items in wanted:
        sample = items[0][0][0]
        shapes.append(
            jax.ShapeDtypeStruct((len(items),) + sample.shape[1:], sample.dtype)
        )
    return pl.pallas_call(
        functools.partial(combine_kernel, len(arrays), tuple(plans)),
        out_shape=shapes,
        in_specs=in_vmem(len(arrays)) + anywhere(len(after)),
        out_specs=in_vmem(len(plans)),
        compiler_params=limits(),
        cost_estimate=small_cost(),
    )(*arrays, *after)


def joined(*arrays):
    return [[(array, i)] for array in arrays for i in range(array.shape[0])]


def summed(home, got, first, last):
    return [[(home, i), (got, i)] for i in range(first, last)]


def spread_kernel(plans, slots, table_ref, *refs):
    piece_refs = refs[: len(plans)]
    out_ref, token_ref, sem = refs[-3:]
    token_ref[...] = jnp.zeros_like(token_ref)
    for wait in (False, True):
        for p, (first, order) in enumerate(plans):
            for item, place in starts(order, slots):
                to = table_ref[place]

                @pl.when(to >= 0)
                def _(p=p, item=item, to=to, wait=wait, first=first):
                    rows = piece_refs[p].shape[1]
                    copy = pltpu.make_async_copy(
                        piece_refs[p].at[item],
                        out_ref.at[to, pl.ds(first, rows)],
                        sem.at[p, item],
                    )
                    if wait:
                        copy.wait()
                    else:
                        copy.start()


def spread(after, target, shape, table, slots, pieces):
    count = len(pieces)
    arrays = [array for array, _, _ in pieces]
    plans = tuple((first, tuple(order)) for _, first, order in pieces)
    most = max(a.shape[0] for a in arrays)
    more = [] if target is None else [target]
    return pl.pallas_call(
        functools.partial(spread_kernel, plans, slots),
        out_shape=[jax.ShapeDtypeStruct(shape, arrays[0].dtype), token()],
        in_specs=in_smem() + in_vmem(count) + anywhere(len(more) + len(after)),
        out_specs=anywhere() + in_vmem(),
        scratch_shapes=[pltpu.SemaphoreType.DMA((count, most))],
        input_output_aliases={1 + count: 0} if more else {},
        compiler_params=limits(MORE_VMEM_BYTES),
        cost_estimate=small_cost(),
    )(table, *arrays, *more, *after)


def mean_rows(scale, sizes, refs):
    first, used = 0, 0
    for size in sizes:
        total = None
        for ref, item in refs[used : used + size]:
            term = ref[item].astype(jnp.float32)
            total = term if total is None else total + term
        yield first, total * scale
        first += total.shape[0]
        used += size


def nesterov_kernel(scale, sizes, items, momentum_ref, *rest):
    part_refs, (rounded_ref, gram_ref) = rest[: len(items)], rest[len(items) :]
    for s in range(momentum_ref.shape[0]):
        refs = [(ref, item + s) for ref, item in zip(part_refs, items)]
        for first, mean in mean_rows(scale, sizes, refs):
            here = pl.ds(first, mean.shape[0])
            following = DECAY * momentum_ref[s, here] + mean
            rounded_ref[s, here] = (mean + DECAY * following).astype(jnp.bfloat16)
        rounded = rounded_ref[s]
        gram_ref[s] = lax.dot_general(
            rounded,
            rounded,
            (((1,), (1,)), ((), ())),
            preferred_element_type=jnp.float32,
        )


def momentum_kernel(scale, sizes, count, table_ref, momentum_ref, *rest):
    part_refs, (next_ref, token_ref) = rest[:count], rest[-2:]
    token_ref[...] = jnp.zeros_like(token_ref)
    held = table_ref[pl.program_id(0)] >= 0
    for first, mean in mean_rows(scale, sizes, [(ref, 0) for ref in part_refs]):
        here = pl.ds(first, mean.shape[0])
        previous = momentum_ref[0, here]
        next_ref[0, here] = jnp.where(held, DECAY * previous + mean, previous)


def nesterov_step(momentum, parts, owner_count):
    slots, rows, cols = momentum.shape
    flat = [b for part in parts for b in part]
    sizes = [len(part) for part in parts]
    items = [b.start for b in flat]
    return pl.pallas_call(
        functools.partial(nesterov_kernel, 1.0 / owner_count, sizes, items),
        out_shape=[
            jax.ShapeDtypeStruct((slots, rows, cols), jnp.bfloat16),
            jax.ShapeDtypeStruct((slots, rows, rows), jnp.float32),
        ],
        in_specs=in_vmem(1 + len(flat)),
        out_specs=in_vmem(2),
        compiler_params=limits(),
        cost_estimate=small_cost(),
    )(momentum, *[b.array for b in flat])


def momentum_step(after, table, momentum, parts, owner_count):
    slots, rows, cols = momentum.shape
    flat = [b for part in parts for b in part]
    sizes = [len(part) for part in parts]
    return pl.pallas_call(
        functools.partial(momentum_kernel, 1.0 / owner_count, sizes, len(flat)),
        grid=(slots,),
        out_shape=[jax.ShapeDtypeStruct((slots, rows, cols), jnp.float32), token()],
        in_specs=in_smem()
        + [pl.BlockSpec((1, rows, cols), lambda s: (s, 0, 0))]
        + [
            pl.BlockSpec((1,) + b.array.shape[1:], lambda s, at=b.start: (s + at, 0, 0))
            for b in flat
        ]
        + anywhere(len(after)),
        out_specs=[
            pl.BlockSpec((1, rows, cols), lambda s: (s, 0, 0)),
            pl.BlockSpec((8, 128), lambda s: (0, 0)),
        ],
        compiler_params=limits(),
        cost_estimate=small_cost(),
    )(table, momentum, *[b.array for b in flat], *after)


def exact(a, b):
    return jnp.dot(
        a, b, preferred_element_type=jnp.float32, precision=lax.Precision.HIGHEST
    )


def orthogonalize_kernel(factor, slots, grams, *refs):
    gram_refs = refs[:grams]
    rounded_ref = refs[grams]
    out_refs = refs[grams + 1 :]
    rows = rounded_ref.shape[1]
    row_ids = lax.broadcasted_iota(jnp.int32, (rows, rows), 0)
    col_ids = lax.broadcasted_iota(jnp.int32, (rows, rows), 1)
    diagonal = row_ids == col_ids
    held = []
    for s in range(slots):
        gram = gram_refs[0][s]
        for ref in gram_refs[1:]:
            gram = gram + ref[s]
        squares = jnp.sum(
            jnp.sum(jnp.where(diagonal, gram, 0.0), axis=0, keepdims=True),
            axis=1,
            keepdims=True,
        )
        inverse = 1.0 / (jnp.sqrt(squares) + EPSILON)
        held.append([gram * inverse * inverse, None, inverse])
    for step in range(ITERS):
        squared = [exact(h[0], h[0]) for h in held]
        factors = [
            COEF_B * h[0] + COEF_C * q + jnp.where(diagonal, COEF_A, 0.0)
            for h, q in zip(held, squared)
        ]
        for h, m in zip(held, factors):
            h[1] = m if h[1] is None else exact(m, h[1])
        if step + 1 < ITERS:
            once = [exact(m, h[0]) for h, m in zip(held, factors)]
            for h, m, o in zip(held, factors, once):
                h[0] = exact(m, o)
    for s, h in enumerate(held):
        whole = h[1] * (factor * h[2])
        high = whole.astype(jnp.bfloat16)
        low = (whole - high.astype(jnp.float32)).astype(jnp.bfloat16)
        rounded = rounded_ref[s]
        result = (
            jnp.dot(high, rounded, preferred_element_type=jnp.float32)
            + jnp.dot(low, rounded, preferred_element_type=jnp.float32)
        ).astype(jnp.bfloat16)
        first = 0
        for out_ref in out_refs:
            out_ref[s] = result[first : first + out_ref.shape[1]]
            first += out_ref.shape[1]


def orthogonalize(grams, rounded, factor, shares):
    slots, rows, cols = rounded.shape
    return pl.pallas_call(
        functools.partial(orthogonalize_kernel, factor, slots, len(grams)),
        out_shape=[
            jax.ShapeDtypeStruct((slots, share, cols), jnp.bfloat16) for share in shares
        ],
        in_specs=in_vmem(len(grams) + 1),
        out_specs=in_vmem(len(shares)),
        compiler_params=limits(),
        cost_estimate=small_cost(),
    )(*grams, rounded)


def swap(value, bit):
    count = lax.axis_size("dp")
    return lax.ppermute(value, "dp", [(i, i ^ bit) for i in range(count)])


def z_bits():
    bits, bit = [], 2 * X_BIT
    while bit < lax.axis_size("dp"):
        bits.append(bit)
        bit *= 2
    return bits


def offsets(bits):
    if not bits:
        return [0]
    rest = offsets(bits[1:])
    return [bits[0] | o for o in rest] + rest


def levels(bits):
    found = [[(0, -1)]]
    for _ in bits:
        longer = []
        for j, bit in enumerate(bits):
            longer += [(o | bit, j) for o, last in found[-1] if last < j]
        found.append(longer)
    return found


class Block:
    def __init__(self, array, start):
        self.array, self.start = array, start


def sum_to_owners(gradient, table, slots, bits, cut):
    rest = gradient.shape[1] - cut
    level = [[o for o, _ in found] for found in levels(bits)]
    last = {o: bits[j] for found in levels(bits) for o, j in found if j >= 0}
    top = len(bits)
    other_bits = bits[::-1] + [X_BIT]
    other_order = tuple(offsets(other_bits))

    def batch(k):
        order = [o | X_BIT for o in level[k]]
        return tuple(order + (level[k + 1] if k < top else []))

    merged = {k: batch(k) for k in range(top, 0, -1)}
    merged[0] = batch(0) + (0,)

    def theirs(order):
        return tuple(CORE_BIT | o for o in order)

    packed = pack([], table, gradient, [theirs(other_order)], slots, cut, rest)
    other_got = swap(packed[0], CORE_BIT)
    falling = range(top, -1, -1)
    orders = [theirs(merged[k]) for k in falling]
    packed = pack(packed, table, gradient, orders, slots, 0, cut)
    got = {k: swap(block, CORE_BIT) for k, block in zip(falling, packed)}
    after = [packed[0]]

    home = {}
    over_x = {}

    def take(k, after):
        order = merged[k]
        crossing = len(level[k]) * slots
        parts = (crossing,)
        if len(order) * slots > crossing:
            parts += (len(order) * slots - crossing,)
        made = add_taken(after, table, gradient, order, slots, 0, got[k], parts)
        over_x[k] = made[0]
        for n, o in enumerate(order[len(level[k]) :]):
            home[o] = Block(made[1], n * slots)
        return [made[0]]

    half = len(other_order) * slots // 2
    away, kept = add_taken(
        after, table, gradient, other_order, slots, cut, other_got, (half, half)
    )
    other_got = swap(away, other_bits[0])
    after = take(top, [away])
    x_got = swap(over_x[top], X_BIT)
    pending = {}
    for k in range(top, -1, -1):
        terms = {o: [] for o in level[k]}
        for n, o in enumerate(level[k]):
            terms[o].append(Block(x_got, n * slots))
        for o, value in pending.items():
            terms[o ^ last[o]].append(Block(value, 0))
        if k == 0:
            break
        if k == top:
            after = take(k - 1, after)
        wanted = []
        for o in level[k]:
            parts = [home[o]] + terms[o]
            wanted.append(
                [[(b.array, b.start + s) for b in parts] for s in range(slots)]
            )
        half //= 2
        wanted.append(summed(kept, other_got, 0, half))
        wanted.append(summed(kept, other_got, half, 2 * half))
        held_back = k == 1
        if held_back:
            wanted.append(joined(over_x[0]))
        made = list(combine(after, *wanted))
        after = [made[0]]
        if held_back:
            over_x[0] = made.pop()
        else:
            after = take(k - 2, after)
        pending = {o: swap(made[n], last[o]) for n, o in enumerate(level[k])}
        kept = made[-1]
        other_got = swap(made[-2], other_bits[top - k + 1])
        x_got = swap(over_x[k - 1], X_BIT)
    return [[home[0]] + terms[0], [Block(kept, 0), Block(other_got, 0)]]


def spread_updates(blocks, table, slots, bits, cut, shape, early):
    level = levels(bits)
    last = [dict(found) for found in level]
    own, cur = blocks
    top = len(bits)
    cur_order = [0]
    other_bits = [X_BIT] + bits
    front, front_order = own, [0]
    pieces = {0: own}
    after, update = [early], None

    def with_core(array, first, order):
        return [
            (array, first, order),
            (swap(array, CORE_BIT), first, [CORE_BIT | o for o in order]),
        ]

    for k in range(top + 1):
        longer = {}
        for j, bit in enumerate(bits):
            for o, at in level[k]:
                if at < j:
                    longer[o | bit] = swap(pieces[o], bit)
        x_got = swap(front, X_BIT)
        other_got = swap(cur, other_bits[k])
        crossed = (x_got, 0, [X_BIT | o for o in front_order])
        crossed_other = (other_got, cut, [other_bits[k] | o for o in cur_order])
        if k == top:
            break
        if k > 0:
            update, ran = spread(after, update, shape, table, slots, waiting)
            after = [ran]
        waiting = []
        order = [o for o, _ in level[k + 1]]
        new = joined(*[longer[o] for o in order])
        wanted = [new, joined(cur, other_got)]
        if k == 0:
            wanted.append(joined(front, x_got))
            more = front_order + crossed[2]
        else:
            wanted.append(joined(x_got) + new)
            more = crossed[2] + order
        front, cur, both = combine(after, *wanted)
        after = [front]
        pieces = longer
        front_order = order
        cur_order = cur_order + crossed_other[2]
        waiting += with_core(both, 0, more)
        if k == 0:
            waiting += with_core(front, 0, front_order)
    waiting += with_core(cur, cut, cur_order)
    update, _ = spread(after, update, shape, table, slots, waiting)
    waiting = with_core(*crossed) + with_core(*crossed_other)
    return spread([], update, shape, table, slots, waiting)[0]


def per_device(grads, owner, momentum):
    owner_count = lax.axis_size("dp")
    matrices = owner.shape[0]
    slot_count = momentum.shape[1]
    head_rows, cols = grads.shape[2:]
    factor = 0.2 * math.sqrt(max(R, D))
    me = lax.axis_index("dp").astype(jnp.int32).reshape(1)
    table = build_table(me, owner, owner_count, slot_count)

    cut = head_rows * 3 // 4
    bits = z_bits()[::-1]
    parts = sum_to_owners(grads[0], table, slot_count, bits, cut)
    rounded, gram = nesterov_step(momentum[0], parts, owner_count)

    width = lax.axis_size("tensor")
    grams = [gram]
    for _ in range(width - 1):
        grams.append(
            lax.ppermute(
                grams[-1], "tensor", [(i, (i + 1) % width) for i in range(width)]
            )
        )
    blocks = orthogonalize(grams, rounded, factor, [cut, head_rows - cut])
    new_momentum, early = momentum_step(
        blocks[:1], table, momentum[0], parts, owner_count
    )
    shape = (matrices, head_rows, cols)
    update = spread_updates(
        blocks, table, slot_count, bits, cut, shape, early
    )
    return (update, new_momentum[None])


def solution(mesh):
    in_specs = (P("dp", None, None, "tensor"), P(), P("dp", None, None, "tensor"))
    out_specs = (P(None, None, "tensor"), P("dp", None, None, "tensor"))
    return jax.shard_map(
        per_device, mesh=mesh, in_specs=in_specs, out_specs=out_specs, check_vma=False
    )
```

```python
import functools
import math

import jax
import jax.numpy as jnp
from jax import lax
from jax.experimental import pallas as pl
from jax.experimental.pallas import tpu as pltpu
from jax.sharding import PartitionSpec as P

R = 128
D = 4096
ITERS = 5

COEF_A = 3.4445
COEF_B = -4.775
COEF_C = 2.0315
EPSILON = 1e-07
DECAY = 0.95

CORE_BIT = 1
X_BIT = 2
VMEM_BYTES = 24 * 1024 * 1024
MORE_VMEM_BYTES = 44 * 1024 * 1024


def in_vmem(count=1):
    return [pl.BlockSpec(memory_space=pltpu.VMEM)] * count


def anywhere(count=1):
    return [pl.BlockSpec(memory_space=pl.ANY)] * count


def in_hbm():
    return [pl.BlockSpec(memory_space=pltpu.HBM)]


def in_smem(count=1):
    return [pl.BlockSpec(memory_space=pltpu.SMEM)] * count


def limits(size=VMEM_BYTES):
    return pltpu.CompilerParams(vmem_limit_bytes=size)


def small_cost():
    return pl.CostEstimate(flops=0, bytes_accessed=0, transcendentals=0)


def token():
    return jax.ShapeDtypeStruct((8, 128), jnp.float32)


def table_kernel(slots, me_ref, owner_ref, table_ref, used):
    spots, matrices = table_ref.shape[0], owner_ref.shape[0]

    @pl.loop(0, spots)
    def _(i):
        table_ref[i] = -1

    @pl.loop(0, spots // slots)
    def _(i):
        used[i] = 0

    @pl.loop(0, matrices)
    def _(m):
        at = owner_ref[m]
        rank = used[at]
        table_ref[(at ^ me_ref[0]) * slots + rank] = m
        used[at] = rank + 1


def starts(order, slots):
    return [
        (n * slots + s, offset * slots + s)
        for n, offset in enumerate(order)
        for s in range(slots)
    ]


def items_of(order, slots, first, rows, split=1):
    return tuple(
        (place, first + c * rows) for _, place in starts(order, slots) for c in range(split)
    )


def fetch(table_ref, src_ref, items, into, sem):
    rows = into.shape[1]
    for item, (place, first) in enumerate(items):
        matrix = jnp.maximum(table_ref[place], 0)
        pltpu.make_async_copy(
            src_ref.at[matrix, pl.ds(first, rows)], into.at[item], sem.at[item]
        ).start()
    return lambda i: pltpu.make_async_copy(
        src_ref.at[0, pl.ds(0, rows)], into.at[i], sem.at[i]
    )


def pack_kernel(plans, table_ref, src_ref, *rest):
    out_refs = rest[-2 * len(plans) : -len(plans)]
    sems = rest[-len(plans) :]
    copies = [
        fetch(table_ref, src_ref, items, out_ref, sem)
        for items, out_ref, sem in zip(plans, out_refs, sems)
    ]
    for copy, out_ref in zip(copies, out_refs):

        @pl.loop(0, out_ref.shape[0])
        def _(i, copy=copy):
            copy(i).wait()


def pack(after, table, src, plans, rows):
    return pl.pallas_call(
        functools.partial(pack_kernel, tuple(plans)),
        out_shape=[
            jax.ShapeDtypeStruct((len(items), rows, src.shape[2]), src.dtype)
            for items in plans
        ],
        in_specs=in_smem() + in_hbm() + anywhere(len(after)),
        out_specs=in_vmem(len(plans)),
        scratch_shapes=[pltpu.SemaphoreType.DMA((len(items),)) for items in plans],
        compiler_params=limits(MORE_VMEM_BYTES),
        cost_estimate=small_cost(),
    )(table, src, *after)


def first_pack_kernel(items, slots, me_ref, owner_ref, src_ref, *rest):
    table_ref, out_ref, used, sem = rest
    table_kernel(slots, me_ref, owner_ref, table_ref, used)
    copy = fetch(table_ref, src_ref, items, out_ref, sem)

    @pl.loop(0, out_ref.shape[0])
    def _(i):
        copy(i).wait()


def first_pack(me, owner, owners, slots, src, items, rows):
    count = len(items)
    return pl.pallas_call(
        functools.partial(first_pack_kernel, items, slots),
        out_shape=[
            jax.ShapeDtypeStruct((owners * slots,), jnp.int32),
            jax.ShapeDtypeStruct((count, rows, src.shape[2]), src.dtype),
        ],
        in_specs=in_smem(2) + in_hbm(),
        out_specs=in_smem() + in_vmem(),
        scratch_shapes=[
            pltpu.SMEM((owners,), jnp.int32),
            pltpu.SemaphoreType.DMA((count,)),
        ],
        compiler_params=limits(MORE_VMEM_BYTES),
        cost_estimate=small_cost(),
    )(me, owner, src)


def add_taken_kernel(items, parts, table_ref, src_ref, got_ref, *rest):
    mine, sem = rest[-2:]
    out_refs = rest[-2 - len(parts) : -2]
    copy = fetch(table_ref, src_ref, items, mine, sem)
    start = 0
    for size, out_ref in zip(parts, out_refs):

        @pl.loop(0, size)
        def _(i, start=start, out_ref=out_ref):
            copy(start + i).wait()
            out_ref[i] = got_ref[start + i] + mine[start + i]

        start += size


def add_taken(after, table, src, items, got, parts):
    count, rows, cols = got.shape
    return pl.pallas_call(
        functools.partial(add_taken_kernel, items, parts),
        out_shape=[jax.ShapeDtypeStruct((n, rows, cols), got.dtype) for n in parts],
        in_specs=in_smem() + in_hbm() + in_vmem() + anywhere(len(after)),
        out_specs=in_vmem(len(parts)),
        scratch_shapes=[
            pltpu.VMEM(got.shape, got.dtype),
            pltpu.SemaphoreType.DMA((count,)),
        ],
        compiler_params=limits(MORE_VMEM_BYTES),
        cost_estimate=small_cost(),
    )(table, src, got, *after)


def combine_kernel(arrays, plans, *refs):
    sources = refs[:arrays]
    outs = refs[len(refs) - len(plans) :]
    for out_ref, items in zip(outs, plans):
        for i, terms in enumerate(items):
            cuts = max(len(item) for _, item in terms)
            rows = out_ref.shape[1] // cuts
            for c in range(cuts):
                here = pl.ds(c * rows, rows)
                total = None
                for at, item in terms:
                    if len(item) == cuts:
                        term = sources[at][item[c]]
                    else:
                        term = sources[at][item[0], here]
                    total = term if total is None else total + term
                out_ref[i, here] = total


def combine(after, *wanted):
    arrays, plans = [], []
    for items in wanted:
        plan = []
        for terms in items:
            found = []
            for array, item in terms:
                places = [i for i, a in enumerate(arrays) if a is array]
                if not places:
                    arrays.append(array)
                    places = [len(arrays) - 1]
                found.append((places[0], item if isinstance(item, tuple) else (item,)))
            plan.append(tuple(found))
        plans.append(tuple(plan))
    shapes = []
    for items in wanted:
        sample = items[0][0][0]
        shapes.append(
            jax.ShapeDtypeStruct((len(items),) + sample.shape[1:], sample.dtype)
        )
    return pl.pallas_call(
        functools.partial(combine_kernel, len(arrays), tuple(plans)),
        out_shape=shapes,
        in_specs=in_vmem(len(arrays)) + anywhere(len(after)),
        out_specs=in_vmem(len(plans)),
        compiler_params=limits(),
        cost_estimate=small_cost(),
    )(*arrays, *after)


def joined(*arrays):
    return [[(array, i)] for array in arrays for i in range(array.shape[0])]


def summed(home, got, first, last):
    return [[(home, i), (got, i)] for i in range(first, last)]


def spread_kernel(plans, slots, table_ref, *refs):
    piece_refs = refs[: len(plans)]
    out_ref, token_ref, sem = refs[-3:]
    token_ref[...] = jnp.zeros_like(token_ref)
    for wait in (False, True):
        for p, (first, order) in enumerate(plans):
            for item, place in starts(order, slots):
                to = table_ref[place]

                @pl.when(to >= 0)
                def _(p=p, item=item, to=to, wait=wait, first=first):
                    rows = piece_refs[p].shape[1]
                    copy = pltpu.make_async_copy(
                        piece_refs[p].at[item],
                        out_ref.at[to, pl.ds(first, rows)],
                        sem.at[p, item],
                    )
                    if wait:
                        copy.wait()
                    else:
                        copy.start()


def spread(after, target, shape, table, slots, pieces):
    count = len(pieces)
    arrays = [array for array, _, _ in pieces]
    plans = tuple((first, tuple(order)) for _, first, order in pieces)
    most = max(a.shape[0] for a in arrays)
    more = [] if target is None else [target]
    return pl.pallas_call(
        functools.partial(spread_kernel, plans, slots),
        out_shape=[jax.ShapeDtypeStruct(shape, arrays[0].dtype), token()],
        in_specs=in_smem() + in_vmem(count) + anywhere(len(more) + len(after)),
        out_specs=anywhere() + in_vmem(),
        scratch_shapes=[pltpu.SemaphoreType.DMA((count, most))],
        input_output_aliases={1 + count: 0} if more else {},
        compiler_params=limits(MORE_VMEM_BYTES),
        cost_estimate=small_cost(),
    )(table, *arrays, *more, *after)


def mean_rows(scale, sizes, refs):
    first, used = 0, 0
    for size in sizes:
        total = None
        for ref, item in refs[used : used + size]:
            term = ref[item].astype(jnp.float32)
            total = term if total is None else total + term
        yield first, total * scale
        first += total.shape[0]
        used += size


def nesterov_kernel(scale, sizes, items, momentum_ref, *rest):
    part_refs, (rounded_ref, gram_ref) = rest[: len(items)], rest[len(items) :]
    for s in range(momentum_ref.shape[0]):
        refs = [(ref, item + s) for ref, item in zip(part_refs, items)]
        for first, mean in mean_rows(scale, sizes, refs):
            here = pl.ds(first, mean.shape[0])
            following = DECAY * momentum_ref[s, here] + mean
            rounded_ref[s, here] = (mean + DECAY * following).astype(jnp.bfloat16)
        rounded = rounded_ref[s]
        gram_ref[s] = lax.dot_general(
            rounded,
            rounded,
            (((1,), (1,)), ((), ())),
            preferred_element_type=jnp.float32,
        )


def momentum_kernel(scale, sizes, count, table_ref, momentum_ref, *rest):
    part_refs, (next_ref, token_ref) = rest[:count], rest[-2:]
    token_ref[...] = jnp.zeros_like(token_ref)
    held = table_ref[pl.program_id(0)] >= 0
    for first, mean in mean_rows(scale, sizes, [(ref, 0) for ref in part_refs]):
        here = pl.ds(first, mean.shape[0])
        previous = momentum_ref[0, here]
        next_ref[0, here] = jnp.where(held, DECAY * previous + mean, previous)


def nesterov_step(momentum, parts, owner_count):
    slots, rows, cols = momentum.shape
    flat = [b for part in parts for b in part]
    sizes = [len(part) for part in parts]
    items = [b.start for b in flat]
    return pl.pallas_call(
        functools.partial(nesterov_kernel, 1.0 / owner_count, sizes, items),
        out_shape=[
            jax.ShapeDtypeStruct((slots, rows, cols), jnp.bfloat16),
            jax.ShapeDtypeStruct((slots, rows, rows), jnp.float32),
        ],
        in_specs=in_vmem(1 + len(flat)),
        out_specs=in_vmem(2),
        compiler_params=limits(),
        cost_estimate=small_cost(),
    )(momentum, *[b.array for b in flat])


def momentum_step(after, table, momentum, parts, owner_count):
    slots, rows, cols = momentum.shape
    flat = [b for part in parts for b in part]
    sizes = [len(part) for part in parts]
    return pl.pallas_call(
        functools.partial(momentum_kernel, 1.0 / owner_count, sizes, len(flat)),
        grid=(slots,),
        out_shape=[jax.ShapeDtypeStruct((slots, rows, cols), jnp.float32), token()],
        in_specs=in_smem()
        + [pl.BlockSpec((1, rows, cols), lambda s: (s, 0, 0))]
        + [
            pl.BlockSpec((1,) + b.array.shape[1:], lambda s, at=b.start: (s + at, 0, 0))
            for b in flat
        ]
        + anywhere(len(after)),
        out_specs=[
            pl.BlockSpec((1, rows, cols), lambda s: (s, 0, 0)),
            pl.BlockSpec((8, 128), lambda s: (0, 0)),
        ],
        compiler_params=limits(),
        cost_estimate=small_cost(),
    )(table, momentum, *[b.array for b in flat], *after)


def exact(a, b):
    return jnp.dot(
        a, b, preferred_element_type=jnp.float32, precision=lax.Precision.HIGHEST
    )


def orthogonalize_kernel(factor, slots, grams, *refs):
    gram_refs = refs[:grams]
    rounded_ref = refs[grams]
    out_refs = refs[grams + 1 :]
    rows = rounded_ref.shape[1]
    row_ids = lax.broadcasted_iota(jnp.int32, (rows, rows), 0)
    col_ids = lax.broadcasted_iota(jnp.int32, (rows, rows), 1)
    diagonal = row_ids == col_ids
    held = []
    for s in range(slots):
        gram = gram_refs[0][s]
        for ref in gram_refs[1:]:
            gram = gram + ref[s]
        squares = jnp.sum(
            jnp.sum(jnp.where(diagonal, gram, 0.0), axis=0, keepdims=True),
            axis=1,
            keepdims=True,
        )
        inverse = 1.0 / (jnp.sqrt(squares) + EPSILON)
        held.append([gram * inverse * inverse, None, inverse])
    for step in range(ITERS):
        squared = [exact(h[0], h[0]) for h in held]
        factors = [
            COEF_B * h[0] + COEF_C * q + jnp.where(diagonal, COEF_A, 0.0)
            for h, q in zip(held, squared)
        ]
        for h, m in zip(held, factors):
            h[1] = m if h[1] is None else exact(m, h[1])
        if step + 1 < ITERS:
            once = [exact(m, h[0]) for h, m in zip(held, factors)]
            for h, m, o in zip(held, factors, once):
                h[0] = exact(m, o)
    for s, h in enumerate(held):
        whole = h[1] * (factor * h[2])
        high = whole.astype(jnp.bfloat16)
        low = (whole - high.astype(jnp.float32)).astype(jnp.bfloat16)
        rounded = rounded_ref[s]
        result = (
            jnp.dot(high, rounded, preferred_element_type=jnp.float32)
            + jnp.dot(low, rounded, preferred_element_type=jnp.float32)
        ).astype(jnp.bfloat16)
        first = 0
        for out_ref in out_refs:
            out_ref[s] = result[first : first + out_ref.shape[1]]
            first += out_ref.shape[1]


def orthogonalize(grams, rounded, factor, shares):
    slots, rows, cols = rounded.shape
    return pl.pallas_call(
        functools.partial(orthogonalize_kernel, factor, slots, len(grams)),
        out_shape=[
            jax.ShapeDtypeStruct((slots, share, cols), jnp.bfloat16) for share in shares
        ],
        in_specs=in_vmem(len(grams) + 1),
        out_specs=in_vmem(len(shares)),
        compiler_params=limits(),
        cost_estimate=small_cost(),
    )(*grams, rounded)


def swap(value, bit):
    count = lax.axis_size("dp")
    return lax.ppermute(value, "dp", [(i, i ^ bit) for i in range(count)])


def z_bits():
    bits, bit = [], 2 * X_BIT
    while bit < lax.axis_size("dp"):
        bits.append(bit)
        bit *= 2
    return bits


def offsets(bits):
    if not bits:
        return [0]
    rest = offsets(bits[1:])
    return [bits[0] | o for o in rest] + rest


def levels(bits):
    found = [[(0, -1)]]
    for _ in bits:
        longer = []
        for j, bit in enumerate(bits):
            longer += [(o | bit, j) for o, last in found[-1] if last < j]
        found.append(longer)
    return found


class Block:
    def __init__(self, array, start, split=1):
        self.array, self.start, self.split = array, start, split

    def item(self, slot):
        first = self.start + slot * self.split
        return tuple(range(first, first + self.split))


def sum_to_owners(gradient, me, owner, owners, slots, bits, cut):
    rest = gradient.shape[1] - cut
    level = [[o for o, _ in found] for found in levels(bits)]
    last = {o: bits[j] for found in levels(bits) for o, j in found if j >= 0}
    top = len(bits)
    other_bits = bits[::-1] + [X_BIT]
    other_order = tuple(offsets(other_bits))

    def batch(k):
        order = [o | X_BIT for o in level[k]]
        return tuple(order + (level[k + 1] if k < top else []))

    merged = {k: batch(k) for k in range(top, 0, -1)}
    merged[0] = batch(0) + (0,)

    def theirs(order):
        return tuple(CORE_BIT | o for o in order)

    split = cut // rest
    half = len(other_order) * slots // 2

    def first_items(places):
        return items_of(places(other_order), slots, cut, rest) + items_of(
            places(merged[top]), slots, 0, rest, split
        )

    def same(order):
        return order

    table, packed = first_pack(
        me, owner, owners, slots, gradient, first_items(theirs), rest
    )
    first_got = swap(packed, CORE_BIT)
    falling = range(top - 1, -1, -1)
    plans = [items_of(theirs(merged[k]), slots, 0, cut) for k in falling]
    packed = pack([packed], table, gradient, plans, cut)
    got = {k: swap(block, CORE_BIT) for k, block in zip(falling, packed)}
    after = [packed[0]]

    home = {}
    over_x = {}

    def take(k, after):
        order = merged[k]
        crossing = len(level[k]) * slots
        parts = (crossing,)
        if len(order) * slots > crossing:
            parts += (len(order) * slots - crossing,)
        items = items_of(order, slots, 0, cut)
        made = add_taken(after, table, gradient, items, got[k], parts)
        over_x[k] = made[0]
        for n, o in enumerate(order[len(level[k]) :]):
            home[o] = Block(made[1], n * slots)
        return [made[0]]

    parts = (half, half, len(merged[top]) * slots * split)
    away, kept, far = add_taken(
        after, table, gradient, first_items(same), first_got, parts
    )
    after = [away]
    other_got = swap(away, other_bits[0])
    x_got = swap(far, X_BIT)

    pending = {}
    for k in range(top, -1, -1):
        terms = {o: [] for o in level[k]}
        for n, o in enumerate(level[k]):
            cuts = split if k == top else 1
            terms[o].append(Block(x_got, n * slots * cuts, cuts))
        for o, value in pending.items():
            terms[o ^ last[o]].append(Block(value, 0))
        if k == 0:
            break
        if k == top:
            after = take(k - 1, after)
        wanted = []
        for o in level[k]:
            parts = [home[o]] + terms[o]
            wanted.append([[(b.array, b.item(s)) for b in parts] for s in range(slots)])
        half //= 2
        wanted.append(summed(kept, other_got, 0, half))
        wanted.append(summed(kept, other_got, half, 2 * half))
        held_back = k == 1
        if held_back:
            wanted.append(joined(over_x[0]))
        made = list(combine(after, *wanted))
        after = [made[0]]
        if held_back:
            over_x[0] = made.pop()
        else:
            after = take(k - 2, after)
        pending = {o: swap(made[n], last[o]) for n, o in enumerate(level[k])}
        kept = made[-1]
        other_got = swap(made[-2], other_bits[top - k + 1])
        x_got = swap(over_x[k - 1], X_BIT)
    parts = [[home[0]] + terms[0], [Block(kept, 0), Block(other_got, 0)]]
    return table, parts


def spread_updates(blocks, table, slots, bits, cut, shape, early):
    level = levels(bits)
    last = [dict(found) for found in level]
    own, cur = blocks
    top = len(bits)
    cur_order = [0]
    other_bits = [X_BIT] + bits
    front, front_order = own, [0]
    pieces = {0: own}
    after, update = [early], None

    def with_core(array, first, order):
        return [
            (array, first, order),
            (swap(array, CORE_BIT), first, [CORE_BIT | o for o in order]),
        ]

    for k in range(top + 1):
        longer = {}
        for j, bit in enumerate(bits):
            for o, at in level[k]:
                if at < j:
                    longer[o | bit] = swap(pieces[o], bit)
        x_got = swap(front, X_BIT)
        other_got = swap(cur, other_bits[k])
        crossed = (x_got, 0, [X_BIT | o for o in front_order])
        crossed_other = (other_got, cut, [other_bits[k] | o for o in cur_order])
        if k == top:
            break
        if k > 0:
            update, ran = spread(after, update, shape, table, slots, waiting)
            after = [ran]
        waiting = []
        order = [o for o, _ in level[k + 1]]
        wanted = [joined(*[longer[o] for o in order]), joined(cur, other_got)]
        if k == 0:
            wanted.append(joined(front, x_got))
            front, cur, both = combine(after, *wanted)
            waiting += with_core(both, 0, front_order + crossed[2])
        else:
            front, cur = combine(after, *wanted)
            waiting += with_core(*crossed)
        after = [front]
        pieces = longer
        front_order = order
        cur_order = cur_order + crossed_other[2]
        last = with_core(front, 0, front_order)
        waiting += last if k + 1 < top else last[:1]
    waiting += with_core(cur, cut, cur_order)
    update, _ = spread(after, update, shape, table, slots, waiting)
    waiting = last[1:] + with_core(*crossed) + with_core(*crossed_other)
    return spread([], update, shape, table, slots, waiting)[0]


def per_device(grads, owner, momentum):
    owner_count = lax.axis_size("dp")
    matrices = owner.shape[0]
    slot_count = momentum.shape[1]
    head_rows, cols = grads.shape[2:]
    factor = 0.2 * math.sqrt(max(R, D))
    me = lax.axis_index("dp").astype(jnp.int32).reshape(1)

    cut = head_rows * 3 // 4
    bits = z_bits()[::-1]
    table, parts = sum_to_owners(
        grads[0], me, owner, owner_count, slot_count, bits, cut
    )
    rounded, gram = nesterov_step(momentum[0], parts, owner_count)

    width = lax.axis_size("tensor")
    grams = [gram]
    for _ in range(width - 1):
        grams.append(
            lax.ppermute(
                grams[-1], "tensor", [(i, (i + 1) % width) for i in range(width)]
            )
        )
    blocks = orthogonalize(grams, rounded, factor, [cut, head_rows - cut])
    new_momentum, early = momentum_step(
        blocks[:1], table, momentum[0], parts, owner_count
    )
    shape = (matrices, head_rows, cols)
    update = spread_updates(
        blocks, table, slot_count, bits, cut, shape, early
    )
    return (update, new_momentum[None])


def solution(mesh):
    in_specs = (P("dp", None, None, "tensor"), P(), P("dp", None, None, "tensor"))
    out_specs = (P(None, None, "tensor"), P("dp", None, None, "tensor"))
    return jax.shard_map(
        per_device, mesh=mesh, in_specs=in_specs, out_specs=out_specs, check_vma=False
    )
```

```python
import functools
import math

import jax
import jax.numpy as jnp
from jax import lax
from jax.experimental import pallas as pl
from jax.experimental.pallas import tpu as pltpu
from jax.sharding import PartitionSpec as P

R = 128
D = 4096
ITERS = 5

COEF_A = 3.4445
COEF_B = -4.775
COEF_C = 2.0315
EPSILON = 1e-07
DECAY = 0.95

CORE_BIT = 1
X_BIT = 2
VMEM_BYTES = 24 * 1024 * 1024
MORE_VMEM_BYTES = 44 * 1024 * 1024


def in_vmem(count=1):
    return [pl.BlockSpec(memory_space=pltpu.VMEM)] * count


def anywhere(count=1):
    return [pl.BlockSpec(memory_space=pl.ANY)] * count


def in_hbm():
    return [pl.BlockSpec(memory_space=pltpu.HBM)]


def in_smem(count=1):
    return [pl.BlockSpec(memory_space=pltpu.SMEM)] * count


def limits(size=VMEM_BYTES):
    return pltpu.CompilerParams(vmem_limit_bytes=size)


def small_cost():
    return pl.CostEstimate(flops=0, bytes_accessed=0, transcendentals=0)


def token():
    return jax.ShapeDtypeStruct((8, 128), jnp.float32)


def table_kernel(slots, me_ref, owner_ref, table_ref, used):
    spots, matrices = table_ref.shape[0], owner_ref.shape[0]

    @pl.loop(0, spots)
    def _(i):
        table_ref[i] = -1

    @pl.loop(0, spots // slots)
    def _(i):
        used[i] = 0

    @pl.loop(0, matrices)
    def _(m):
        at = owner_ref[m]
        rank = used[at]
        table_ref[(at ^ me_ref[0]) * slots + rank] = m
        used[at] = rank + 1


def starts(order, slots):
    return [
        (n * slots + s, offset * slots + s)
        for n, offset in enumerate(order)
        for s in range(slots)
    ]


def items_of(order, slots, first, rows, split=1):
    return tuple(
        (place, first + c * rows) for _, place in starts(order, slots) for c in range(split)
    )


def fetch(table_ref, src_ref, items, into, sem):
    rows = into.shape[1]
    for item, (place, first) in enumerate(items):
        matrix = jnp.maximum(table_ref[place], 0)
        pltpu.make_async_copy(
            src_ref.at[matrix, pl.ds(first, rows)], into.at[item], sem.at[item]
        ).start()
    return lambda i: pltpu.make_async_copy(
        src_ref.at[0, pl.ds(0, rows)], into.at[i], sem.at[i]
    )


def pack_kernel(plans, table_ref, src_ref, *rest):
    out_refs = rest[-2 * len(plans) : -len(plans)]
    sems = rest[-len(plans) :]
    copies = [
        fetch(table_ref, src_ref, items, out_ref, sem)
        for items, out_ref, sem in zip(plans, out_refs, sems)
    ]
    for copy, out_ref in zip(copies, out_refs):

        @pl.loop(0, out_ref.shape[0])
        def _(i, copy=copy):
            copy(i).wait()


def pack(after, table, src, plans, rows):
    return pl.pallas_call(
        functools.partial(pack_kernel, tuple(plans)),
        out_shape=[
            jax.ShapeDtypeStruct((len(items), rows, src.shape[2]), src.dtype)
            for items in plans
        ],
        in_specs=in_smem() + in_hbm() + anywhere(len(after)),
        out_specs=in_vmem(len(plans)),
        scratch_shapes=[pltpu.SemaphoreType.DMA((len(items),)) for items in plans],
        compiler_params=limits(MORE_VMEM_BYTES),
        cost_estimate=small_cost(),
    )(table, src, *after)


def first_pack_kernel(items, slots, me_ref, owner_ref, src_ref, *rest):
    table_ref, out_ref, used, sem = rest
    table_kernel(slots, me_ref, owner_ref, table_ref, used)
    copy = fetch(table_ref, src_ref, items, out_ref, sem)

    @pl.loop(0, out_ref.shape[0])
    def _(i):
        copy(i).wait()


def first_pack(me, owner, owners, slots, src, items, rows):
    count = len(items)
    return pl.pallas_call(
        functools.partial(first_pack_kernel, items, slots),
        out_shape=[
            jax.ShapeDtypeStruct((owners * slots,), jnp.int32),
            jax.ShapeDtypeStruct((count, rows, src.shape[2]), src.dtype),
        ],
        in_specs=in_smem(2) + in_hbm(),
        out_specs=in_smem() + in_vmem(),
        scratch_shapes=[
            pltpu.SMEM((owners,), jnp.int32),
            pltpu.SemaphoreType.DMA((count,)),
        ],
        compiler_params=limits(MORE_VMEM_BYTES),
        cost_estimate=small_cost(),
    )(me, owner, src)


def add_taken_kernel(items, parts, table_ref, src_ref, got_ref, *rest):
    mine, sem = rest[-2:]
    out_refs = rest[-2 - len(parts) : -2]
    copy = fetch(table_ref, src_ref, items, mine, sem)
    start = 0
    for size, out_ref in zip(parts, out_refs):

        @pl.loop(0, size)
        def _(i, start=start, out_ref=out_ref):
            copy(start + i).wait()
            out_ref[i] = got_ref[start + i] + mine[start + i]

        start += size


def add_taken(after, table, src, items, got, parts):
    count, rows, cols = got.shape
    return pl.pallas_call(
        functools.partial(add_taken_kernel, items, parts),
        out_shape=[jax.ShapeDtypeStruct((n, rows, cols), got.dtype) for n in parts],
        in_specs=in_smem() + in_hbm() + in_vmem() + anywhere(len(after)),
        out_specs=in_vmem(len(parts)),
        scratch_shapes=[
            pltpu.VMEM(got.shape, got.dtype),
            pltpu.SemaphoreType.DMA((count,)),
        ],
        compiler_params=limits(MORE_VMEM_BYTES),
        cost_estimate=small_cost(),
    )(table, src, got, *after)


def combine_kernel(arrays, plans, *refs):
    sources = refs[:arrays]
    outs = refs[len(refs) - len(plans) :]
    for out_ref, items in zip(outs, plans):
        for i, terms in enumerate(items):
            cuts = max(len(item) for _, item in terms)
            rows = out_ref.shape[1] // cuts
            for c in range(cuts):
                here = pl.ds(c * rows, rows)
                total = None
                for at, item in terms:
                    if len(item) == cuts:
                        term = sources[at][item[c]]
                    else:
                        term = sources[at][item[0], here]
                    total = term if total is None else total + term
                out_ref[i, here] = total


def combine(after, *wanted):
    arrays, plans = [], []
    for items in wanted:
        plan = []
        for terms in items:
            found = []
            for array, item in terms:
                places = [i for i, a in enumerate(arrays) if a is array]
                if not places:
                    arrays.append(array)
                    places = [len(arrays) - 1]
                found.append((places[0], item if isinstance(item, tuple) else (item,)))
            plan.append(tuple(found))
        plans.append(tuple(plan))
    shapes = []
    for items in wanted:
        sample = items[0][0][0]
        shapes.append(
            jax.ShapeDtypeStruct((len(items),) + sample.shape[1:], sample.dtype)
        )
    return pl.pallas_call(
        functools.partial(combine_kernel, len(arrays), tuple(plans)),
        out_shape=shapes,
        in_specs=in_vmem(len(arrays)) + anywhere(len(after)),
        out_specs=in_vmem(len(plans)),
        compiler_params=limits(),
        cost_estimate=small_cost(),
    )(*arrays, *after)


def joined(*arrays):
    return [[(array, i)] for array in arrays for i in range(array.shape[0])]


def summed(home, got, first, last):
    return [[(home, i), (got, i)] for i in range(first, last)]


def spread_kernel(plans, slots, table_ref, *refs):
    piece_refs = refs[: len(plans)]
    out_ref, token_ref, sem = refs[-3:]
    token_ref[...] = jnp.zeros_like(token_ref)
    for wait in (False, True):
        for p, (first, order) in enumerate(plans):
            for item, place in starts(order, slots):
                to = table_ref[place]

                @pl.when(to >= 0)
                def _(p=p, item=item, to=to, wait=wait, first=first):
                    rows = piece_refs[p].shape[1]
                    copy = pltpu.make_async_copy(
                        piece_refs[p].at[item],
                        out_ref.at[to, pl.ds(first, rows)],
                        sem.at[p, item],
                    )
                    if wait:
                        copy.wait()
                    else:
                        copy.start()


def spread(after, target, shape, table, slots, pieces):
    count = len(pieces)
    arrays = [array for array, _, _ in pieces]
    plans = tuple((first, tuple(order)) for _, first, order in pieces)
    most = max(a.shape[0] for a in arrays)
    more = [] if target is None else [target]
    return pl.pallas_call(
        functools.partial(spread_kernel, plans, slots),
        out_shape=[jax.ShapeDtypeStruct(shape, arrays[0].dtype), token()],
        in_specs=in_smem() + in_vmem(count) + anywhere(len(more) + len(after)),
        out_specs=anywhere() + in_vmem(),
        scratch_shapes=[pltpu.SemaphoreType.DMA((count, most))],
        input_output_aliases={1 + count: 0} if more else {},
        compiler_params=limits(MORE_VMEM_BYTES),
        cost_estimate=small_cost(),
    )(table, *arrays, *more, *after)


def mean_rows(scale, sizes, refs):
    first, used = 0, 0
    for size in sizes:
        total = None
        for ref, item in refs[used : used + size]:
            term = ref[item].astype(jnp.float32)
            total = term if total is None else total + term
        yield first, total * scale
        first += total.shape[0]
        used += size


def nesterov_kernel(scale, sizes, items, momentum_ref, *rest):
    part_refs, (rounded_ref, gram_ref) = rest[: len(items)], rest[len(items) :]
    for s in range(momentum_ref.shape[0]):
        refs = [(ref, item + s) for ref, item in zip(part_refs, items)]
        for first, mean in mean_rows(scale, sizes, refs):
            here = pl.ds(first, mean.shape[0])
            following = DECAY * momentum_ref[s, here] + mean
            rounded_ref[s, here] = (mean + DECAY * following).astype(jnp.bfloat16)
        rounded = rounded_ref[s]
        gram_ref[s] = lax.dot_general(
            rounded,
            rounded,
            (((1,), (1,)), ((), ())),
            preferred_element_type=jnp.float32,
        )


def momentum_kernel(scale, sizes, count, table_ref, momentum_ref, *rest):
    part_refs, (next_ref, token_ref) = rest[:count], rest[-2:]
    token_ref[...] = jnp.zeros_like(token_ref)
    held = table_ref[pl.program_id(0)] >= 0
    for first, mean in mean_rows(scale, sizes, [(ref, 0) for ref in part_refs]):
        here = pl.ds(first, mean.shape[0])
        previous = momentum_ref[0, here]
        next_ref[0, here] = jnp.where(held, DECAY * previous + mean, previous)


def nesterov_step(momentum, parts, owner_count):
    slots, rows, cols = momentum.shape
    flat = [b for part in parts for b in part]
    sizes = [len(part) for part in parts]
    items = [b.start for b in flat]
    return pl.pallas_call(
        functools.partial(nesterov_kernel, 1.0 / owner_count, sizes, items),
        out_shape=[
            jax.ShapeDtypeStruct((slots, rows, cols), jnp.bfloat16),
            jax.ShapeDtypeStruct((slots, rows, rows), jnp.float32),
        ],
        in_specs=in_vmem(1 + len(flat)),
        out_specs=in_vmem(2),
        compiler_params=limits(),
        cost_estimate=small_cost(),
    )(momentum, *[b.array for b in flat])


def momentum_step(after, table, momentum, parts, owner_count):
    slots, rows, cols = momentum.shape
    flat = [b for part in parts for b in part]
    sizes = [len(part) for part in parts]
    return pl.pallas_call(
        functools.partial(momentum_kernel, 1.0 / owner_count, sizes, len(flat)),
        grid=(slots,),
        out_shape=[jax.ShapeDtypeStruct((slots, rows, cols), jnp.float32), token()],
        in_specs=in_smem()
        + [pl.BlockSpec((1, rows, cols), lambda s: (s, 0, 0))]
        + [
            pl.BlockSpec((1,) + b.array.shape[1:], lambda s, at=b.start: (s + at, 0, 0))
            for b in flat
        ]
        + anywhere(len(after)),
        out_specs=[
            pl.BlockSpec((1, rows, cols), lambda s: (s, 0, 0)),
            pl.BlockSpec((8, 128), lambda s: (0, 0)),
        ],
        compiler_params=limits(),
        cost_estimate=small_cost(),
    )(table, momentum, *[b.array for b in flat], *after)


def exact(a, b):
    def split(v):
        high = v.astype(jnp.bfloat16)
        return high, (v - high.astype(jnp.float32)).astype(jnp.bfloat16)

    def dot(p, q):
        return jnp.dot(p, q, preferred_element_type=jnp.float32)

    (a_high, a_low), (b_high, b_low) = split(a), split(b)
    return dot(a_high, b_high) + (dot(a_high, b_low) + dot(a_low, b_high))


def orthogonalize_kernel(factor, slots, grams, *refs):
    gram_refs = refs[:grams]
    rounded_ref = refs[grams]
    out_refs = refs[grams + 1 :]
    rows = rounded_ref.shape[1]
    row_ids = lax.broadcasted_iota(jnp.int32, (rows, rows), 0)
    col_ids = lax.broadcasted_iota(jnp.int32, (rows, rows), 1)
    diagonal = row_ids == col_ids
    held = []
    for s in range(slots):
        gram = gram_refs[0][s]
        for ref in gram_refs[1:]:
            gram = gram + ref[s]
        squares = jnp.sum(
            jnp.sum(jnp.where(diagonal, gram, 0.0), axis=0, keepdims=True),
            axis=1,
            keepdims=True,
        )
        inverse = 1.0 / (jnp.sqrt(squares) + EPSILON)
        held.append([gram * inverse * inverse, None, inverse])
    for step in range(ITERS):
        squared = [exact(h[0], h[0]) for h in held]
        factors = [
            COEF_B * h[0] + COEF_C * q + jnp.where(diagonal, COEF_A, 0.0)
            for h, q in zip(held, squared)
        ]
        for h, m in zip(held, factors):
            h[1] = m if h[1] is None else exact(m, h[1])
        if step + 1 < ITERS:
            once = [exact(m, h[0]) for h, m in zip(held, factors)]
            for h, m, o in zip(held, factors, once):
                h[0] = exact(m, o)
    for s, h in enumerate(held):
        whole = h[1] * (factor * h[2])
        high = whole.astype(jnp.bfloat16)
        low = (whole - high.astype(jnp.float32)).astype(jnp.bfloat16)
        rounded = rounded_ref[s]
        result = (
            jnp.dot(high, rounded, preferred_element_type=jnp.float32)
            + jnp.dot(low, rounded, preferred_element_type=jnp.float32)
        ).astype(jnp.bfloat16)
        first = 0
        for out_ref in out_refs:
            out_ref[s] = result[first : first + out_ref.shape[1]]
            first += out_ref.shape[1]


def orthogonalize(grams, rounded, factor, shares):
    slots, rows, cols = rounded.shape
    return pl.pallas_call(
        functools.partial(orthogonalize_kernel, factor, slots, len(grams)),
        out_shape=[
            jax.ShapeDtypeStruct((slots, share, cols), jnp.bfloat16) for share in shares
        ],
        in_specs=in_vmem(len(grams) + 1),
        out_specs=in_vmem(len(shares)),
        compiler_params=limits(),
        cost_estimate=small_cost(),
    )(*grams, rounded)


def swap(value, bit):
    count = lax.axis_size("dp")
    return lax.ppermute(value, "dp", [(i, i ^ bit) for i in range(count)])


def z_bits():
    bits, bit = [], 2 * X_BIT
    while bit < lax.axis_size("dp"):
        bits.append(bit)
        bit *= 2
    return bits


def offsets(bits):
    if not bits:
        return [0]
    rest = offsets(bits[1:])
    return [bits[0] | o for o in rest] + rest


def levels(bits):
    found = [[(0, -1)]]
    for _ in bits:
        longer = []
        for j, bit in enumerate(bits):
            longer += [(o | bit, j) for o, last in found[-1] if last < j]
        found.append(longer)
    return found


class Block:
    def __init__(self, array, start, split=1):
        self.array, self.start, self.split = array, start, split

    def item(self, slot):
        first = self.start + slot * self.split
        return tuple(range(first, first + self.split))


def sum_to_owners(gradient, me, owner, owners, slots, bits, cut):
    rest = gradient.shape[1] - cut
    level = [[o for o, _ in found] for found in levels(bits)]
    last = {o: bits[j] for found in levels(bits) for o, j in found if j >= 0}
    top = len(bits)
    other_bits = bits[::-1] + [X_BIT]
    other_order = tuple(offsets(other_bits))

    def batch(k):
        order = [o | X_BIT for o in level[k]]
        return tuple(order + (level[k + 1] if k < top else []))

    merged = {k: batch(k) for k in range(top, 0, -1)}
    merged[0] = batch(0) + (0,)

    def theirs(order):
        return tuple(CORE_BIT | o for o in order)

    split = cut // rest
    half = len(other_order) * slots // 2

    def first_items(places):
        return items_of(places(other_order), slots, cut, rest) + items_of(
            places(merged[top]), slots, 0, rest, split
        )

    def same(order):
        return order

    table, packed = first_pack(
        me, owner, owners, slots, gradient, first_items(theirs), rest
    )
    first_got = swap(packed, CORE_BIT)
    falling = range(top - 1, -1, -1)
    plans = [items_of(theirs(merged[k]), slots, 0, cut) for k in falling]
    packed = pack([packed], table, gradient, plans, cut)
    got = {k: swap(block, CORE_BIT) for k, block in zip(falling, packed)}
    after = [packed[0]]

    home = {}
    over_x = {}

    def take(k, after):
        order = merged[k]
        crossing = len(level[k]) * slots
        parts = (crossing,)
        if len(order) * slots > crossing:
            parts += (len(order) * slots - crossing,)
        items = items_of(order, slots, 0, cut)
        made = add_taken(after, table, gradient, items, got[k], parts)
        over_x[k] = made[0]
        for n, o in enumerate(order[len(level[k]) :]):
            home[o] = Block(made[1], n * slots)
        return [made[0]]

    parts = (half, half, len(merged[top]) * slots * split)
    away, kept, far = add_taken(
        after, table, gradient, first_items(same), first_got, parts
    )
    after = [away]
    other_got = swap(away, other_bits[0])
    x_got = swap(far, X_BIT)

    pending = {}
    for k in range(top, -1, -1):
        terms = {o: [] for o in level[k]}
        for n, o in enumerate(level[k]):
            cuts = split if k == top else 1
            terms[o].append(Block(x_got, n * slots * cuts, cuts))
        for o, value in pending.items():
            terms[o ^ last[o]].append(Block(value, 0))
        if k == 0:
            break
        if k == top:
            after = take(k - 1, after)
        wanted = []
        for o in level[k]:
            parts = [home[o]] + terms[o]
            wanted.append([[(b.array, b.item(s)) for b in parts] for s in range(slots)])
        half //= 2
        wanted.append(summed(kept, other_got, 0, half))
        wanted.append(summed(kept, other_got, half, 2 * half))
        held_back = k == 1
        if held_back:
            wanted.append(joined(over_x[0]))
        made = list(combine(after, *wanted))
        after = [made[0]]
        if held_back:
            over_x[0] = made.pop()
        else:
            after = take(k - 2, after)
        pending = {
            o: swap(made[n], last[o]) for n, o in reversed(list(enumerate(level[k])))
        }
        kept = made[-1]
        other_got = swap(made[-2], other_bits[top - k + 1])
        x_got = swap(over_x[k - 1], X_BIT)
    parts = [[home[0]] + terms[0], [Block(kept, 0), Block(other_got, 0)]]
    return table, parts


def spread_updates(blocks, table, slots, bits, cut, shape, early):
    level = levels(bits)
    last = [dict(found) for found in level]
    own, cur = blocks
    top = len(bits)
    cur_order = [0]
    other_bits = [X_BIT] + bits
    front, front_order = own, [0]
    pieces = {0: own}
    after, update = [early], None

    def with_core(array, first, order):
        return [
            (array, first, order),
            (swap(array, CORE_BIT), first, [CORE_BIT | o for o in order]),
        ]

    for k in range(top + 1):
        longer = {}
        for j, bit in enumerate(bits):
            for o, at in level[k]:
                if at < j:
                    longer[o | bit] = swap(pieces[o], bit)
        x_got = swap(front, X_BIT)
        other_got = swap(cur, other_bits[k])
        crossed = (x_got, 0, [X_BIT | o for o in front_order])
        crossed_other = (other_got, cut, [other_bits[k] | o for o in cur_order])
        if k == top:
            break
        if k > 0:
            update, ran = spread(after, update, shape, table, slots, waiting)
            after = [ran]
        waiting = []
        order = [o for o, _ in level[k + 1]]
        wanted = [joined(*[longer[o] for o in order]), joined(cur, other_got)]
        if k == 0:
            wanted.append(joined(front, x_got))
            front, cur, both = combine(after, *wanted)
            waiting += with_core(both, 0, front_order + crossed[2])
        else:
            front, cur = combine(after, *wanted)
            waiting += with_core(*crossed)
        after = [front]
        pieces = longer
        front_order = order
        cur_order = cur_order + crossed_other[2]
        last = with_core(front, 0, front_order)
        waiting += last if k + 1 < top else last[:1]
    waiting += with_core(cur, cut, cur_order)
    update, _ = spread(after, update, shape, table, slots, waiting)
    waiting = last[1:] + with_core(*crossed) + with_core(*crossed_other)
    return spread([], update, shape, table, slots, waiting)[0]


def per_device(grads, owner, momentum):
    owner_count = lax.axis_size("dp")
    matrices = owner.shape[0]
    slot_count = momentum.shape[1]
    head_rows, cols = grads.shape[2:]
    factor = 0.2 * math.sqrt(max(R, D))
    me = lax.axis_index("dp").astype(jnp.int32).reshape(1)

    cut = head_rows * 3 // 4
    bits = z_bits()[::-1]
    table, parts = sum_to_owners(
        grads[0], me, owner, owner_count, slot_count, bits, cut
    )
    rounded, gram = nesterov_step(momentum[0], parts, owner_count)

    width = lax.axis_size("tensor")
    grams = [gram]
    for _ in range(width - 1):
        grams.append(
            lax.ppermute(
                grams[-1], "tensor", [(i, (i + 1) % width) for i in range(width)]
            )
        )
    blocks = orthogonalize(grams, rounded, factor, [cut, head_rows - cut])
    new_momentum, early = momentum_step(
        blocks[:1], table, momentum[0], parts, owner_count
    )
    shape = (matrices, head_rows, cols)
    update = spread_updates(
        blocks, table, slot_count, bits, cut, shape, early
    )
    return (update, new_momentum[None])


def solution(mesh):
    in_specs = (P("dp", None, None, "tensor"), P(), P("dp", None, None, "tensor"))
    out_specs = (P(None, None, "tensor"), P("dp", None, None, "tensor"))
    return jax.shard_map(
        per_device, mesh=mesh, in_specs=in_specs, out_specs=out_specs, check_vma=False
    )
```

```python
import functools
import math

import jax
import jax.numpy as jnp
from jax import lax
from jax.experimental import pallas as pl
from jax.experimental.pallas import tpu as pltpu
from jax.sharding import PartitionSpec as P

R = 128
D = 4096
ITERS = 5

COEF_A = 3.4445
COEF_B = -4.775
COEF_C = 2.0315
EPSILON = 1e-07
DECAY = 0.95

CORE_BIT = 1
X_BIT = 2
VMEM_BYTES = 24 * 1024 * 1024
MORE_VMEM_BYTES = 44 * 1024 * 1024


def in_vmem(count=1):
    return [pl.BlockSpec(memory_space=pltpu.VMEM)] * count


def anywhere(count=1):
    return [pl.BlockSpec(memory_space=pl.ANY)] * count


def in_hbm():
    return [pl.BlockSpec(memory_space=pltpu.HBM)]


def in_smem(count=1):
    return [pl.BlockSpec(memory_space=pltpu.SMEM)] * count


def limits(size=VMEM_BYTES):
    return pltpu.CompilerParams(vmem_limit_bytes=size)


def small_cost():
    return pl.CostEstimate(flops=0, bytes_accessed=0, transcendentals=0)


def token():
    return jax.ShapeDtypeStruct((8, 128), jnp.float32)


def table_kernel(slots, me_ref, owner_ref, table_ref, used):
    spots, matrices = table_ref.shape[0], owner_ref.shape[0]

    @pl.loop(0, spots)
    def _(i):
        table_ref[i] = -1

    @pl.loop(0, spots // slots)
    def _(i):
        used[i] = 0

    @pl.loop(0, matrices)
    def _(m):
        at = owner_ref[m]
        rank = used[at]
        table_ref[(at ^ me_ref[0]) * slots + rank] = m
        used[at] = rank + 1


def starts(order, slots):
    return [
        (n * slots + s, offset * slots + s)
        for n, offset in enumerate(order)
        for s in range(slots)
    ]


def items_of(order, slots, first, rows, split=1):
    return tuple(
        (place, first + c * rows) for _, place in starts(order, slots) for c in range(split)
    )


def fetch(table_ref, src_ref, items, into, sem):
    rows = into.shape[1]
    for item, (place, first) in enumerate(items):
        matrix = jnp.maximum(table_ref[place], 0)
        pltpu.make_async_copy(
            src_ref.at[matrix, pl.ds(first, rows)], into.at[item], sem.at[item]
        ).start()
    return lambda i: pltpu.make_async_copy(
        src_ref.at[0, pl.ds(0, rows)], into.at[i], sem.at[i]
    )


def pack_kernel(plans, table_ref, src_ref, *rest):
    out_refs = rest[-2 * len(plans) : -len(plans)]
    sems = rest[-len(plans) :]
    copies = [
        fetch(table_ref, src_ref, items, out_ref, sem)
        for items, out_ref, sem in zip(plans, out_refs, sems)
    ]
    for copy, out_ref in zip(copies, out_refs):

        @pl.loop(0, out_ref.shape[0])
        def _(i, copy=copy):
            copy(i).wait()


def pack(after, table, src, plans, rows):
    return pl.pallas_call(
        functools.partial(pack_kernel, tuple(plans)),
        out_shape=[
            jax.ShapeDtypeStruct((len(items), rows, src.shape[2]), src.dtype)
            for items in plans
        ],
        in_specs=in_smem() + in_hbm() + anywhere(len(after)),
        out_specs=in_vmem(len(plans)),
        scratch_shapes=[pltpu.SemaphoreType.DMA((len(items),)) for items in plans],
        compiler_params=limits(MORE_VMEM_BYTES),
        cost_estimate=small_cost(),
    )(table, src, *after)


def first_pack_kernel(items, slots, me_ref, owner_ref, src_ref, *rest):
    table_ref, out_ref, used, sem = rest
    table_kernel(slots, me_ref, owner_ref, table_ref, used)
    copy = fetch(table_ref, src_ref, items, out_ref, sem)

    @pl.loop(0, out_ref.shape[0])
    def _(i):
        copy(i).wait()


def first_pack(me, owner, owners, slots, src, items, rows):
    count = len(items)
    return pl.pallas_call(
        functools.partial(first_pack_kernel, items, slots),
        out_shape=[
            jax.ShapeDtypeStruct((owners * slots,), jnp.int32),
            jax.ShapeDtypeStruct((count, rows, src.shape[2]), src.dtype),
        ],
        in_specs=in_smem(2) + in_hbm(),
        out_specs=in_smem() + in_vmem(),
        scratch_shapes=[
            pltpu.SMEM((owners,), jnp.int32),
            pltpu.SemaphoreType.DMA((count,)),
        ],
        compiler_params=limits(MORE_VMEM_BYTES),
        cost_estimate=small_cost(),
    )(me, owner, src)


def add_taken_kernel(items, parts, table_ref, src_ref, got_ref, *rest):
    mine, sem = rest[-2:]
    out_refs = rest[-2 - len(parts) : -2]
    copy = fetch(table_ref, src_ref, items, mine, sem)
    start = 0
    for size, out_ref in zip(parts, out_refs):

        @pl.loop(0, size)
        def _(i, start=start, out_ref=out_ref):
            copy(start + i).wait()
            out_ref[i] = got_ref[start + i] + mine[start + i]

        start += size


def add_taken(after, table, src, items, got, parts):
    count, rows, cols = got.shape
    return pl.pallas_call(
        functools.partial(add_taken_kernel, items, parts),
        out_shape=[jax.ShapeDtypeStruct((n, rows, cols), got.dtype) for n in parts],
        in_specs=in_smem() + in_hbm() + in_vmem() + anywhere(len(after)),
        out_specs=in_vmem(len(parts)),
        scratch_shapes=[
            pltpu.VMEM(got.shape, got.dtype),
            pltpu.SemaphoreType.DMA((count,)),
        ],
        compiler_params=limits(MORE_VMEM_BYTES),
        cost_estimate=small_cost(),
    )(table, src, got, *after)


def combine_kernel(arrays, plans, *refs):
    sources = refs[:arrays]
    outs = refs[len(refs) - len(plans) :]
    for out_ref, items in zip(outs, plans):
        for i, terms in enumerate(items):
            cuts = max(len(item) for _, item in terms)
            rows = out_ref.shape[1] // cuts
            for c in range(cuts):
                here = pl.ds(c * rows, rows)
                total = None
                for at, item in terms:
                    if len(item) == cuts:
                        term = sources[at][item[c]]
                    else:
                        term = sources[at][item[0], here]
                    total = term if total is None else total + term
                out_ref[i, here] = total


def combine(after, *wanted):
    arrays, plans = [], []
    for items in wanted:
        plan = []
        for terms in items:
            found = []
            for array, item in terms:
                places = [i for i, a in enumerate(arrays) if a is array]
                if not places:
                    arrays.append(array)
                    places = [len(arrays) - 1]
                found.append((places[0], item if isinstance(item, tuple) else (item,)))
            plan.append(tuple(found))
        plans.append(tuple(plan))
    shapes = []
    for items in wanted:
        sample = items[0][0][0]
        shapes.append(
            jax.ShapeDtypeStruct((len(items),) + sample.shape[1:], sample.dtype)
        )
    return pl.pallas_call(
        functools.partial(combine_kernel, len(arrays), tuple(plans)),
        out_shape=shapes,
        in_specs=in_vmem(len(arrays)) + anywhere(len(after)),
        out_specs=in_vmem(len(plans)),
        compiler_params=limits(),
        cost_estimate=small_cost(),
    )(*arrays, *after)


def joined(*arrays):
    return [[(array, i)] for array in arrays for i in range(array.shape[0])]


def summed(home, got, first, last):
    return [[(home, i), (got, i)] for i in range(first, last)]


def spread_kernel(plans, slots, table_ref, *refs):
    piece_refs = refs[: len(plans)]
    out_ref, token_ref, sem = refs[-3:]
    token_ref[...] = jnp.zeros_like(token_ref)
    for wait in (False, True):
        for p, (first, order) in enumerate(plans):
            for item, place in starts(order, slots):
                to = table_ref[place]

                @pl.when(to >= 0)
                def _(p=p, item=item, to=to, wait=wait, first=first):
                    rows = piece_refs[p].shape[1]
                    copy = pltpu.make_async_copy(
                        piece_refs[p].at[item],
                        out_ref.at[to, pl.ds(first, rows)],
                        sem.at[p, item],
                    )
                    if wait:
                        copy.wait()
                    else:
                        copy.start()


def spread(after, target, shape, table, slots, pieces):
    count = len(pieces)
    arrays = [array for array, _, _ in pieces]
    plans = tuple((first, tuple(order)) for _, first, order in pieces)
    most = max(a.shape[0] for a in arrays)
    more = [] if target is None else [target]
    return pl.pallas_call(
        functools.partial(spread_kernel, plans, slots),
        out_shape=[jax.ShapeDtypeStruct(shape, arrays[0].dtype), token()],
        in_specs=in_smem() + in_vmem(count) + anywhere(len(more) + len(after)),
        out_specs=anywhere() + in_vmem(),
        scratch_shapes=[pltpu.SemaphoreType.DMA((count, most))],
        input_output_aliases={1 + count: 0} if more else {},
        compiler_params=limits(MORE_VMEM_BYTES),
        cost_estimate=small_cost(),
    )(table, *arrays, *more, *after)


def mean_rows(scale, sizes, refs):
    first, used = 0, 0
    for size in sizes:
        total = None
        for ref, item in refs[used : used + size]:
            term = ref[item].astype(jnp.float32)
            total = term if total is None else total + term
        yield first, total * scale
        first += total.shape[0]
        used += size


def nesterov_kernel(scale, sizes, items, momentum_ref, *rest):
    part_refs, (rounded_ref, gram_ref) = rest[: len(items)], rest[len(items) :]
    for s in range(momentum_ref.shape[0]):
        refs = [(ref, item + s) for ref, item in zip(part_refs, items)]
        for first, mean in mean_rows(scale, sizes, refs):
            here = pl.ds(first, mean.shape[0])
            following = DECAY * momentum_ref[s, here] + mean
            rounded_ref[s, here] = (mean + DECAY * following).astype(jnp.bfloat16)
        rounded = rounded_ref[s]
        gram_ref[s] = lax.dot_general(
            rounded,
            rounded,
            (((1,), (1,)), ((), ())),
            preferred_element_type=jnp.float32,
        )


def momentum_kernel(scale, sizes, count, table_ref, momentum_ref, *rest):
    part_refs, (next_ref, token_ref) = rest[:count], rest[-2:]
    token_ref[...] = jnp.zeros_like(token_ref)
    held = table_ref[pl.program_id(0)] >= 0
    for first, mean in mean_rows(scale, sizes, [(ref, 0) for ref in part_refs]):
        here = pl.ds(first, mean.shape[0])
        previous = momentum_ref[0, here]
        next_ref[0, here] = jnp.where(held, DECAY * previous + mean, previous)


def nesterov_step(momentum, parts, owner_count):
    slots, rows, cols = momentum.shape
    flat = [b for part in parts for b in part]
    sizes = [len(part) for part in parts]
    items = [b.start for b in flat]
    return pl.pallas_call(
        functools.partial(nesterov_kernel, 1.0 / owner_count, sizes, items),
        out_shape=[
            jax.ShapeDtypeStruct((slots, rows, cols), jnp.bfloat16),
            jax.ShapeDtypeStruct((slots, rows, rows), jnp.float32),
        ],
        in_specs=in_vmem(1 + len(flat)),
        out_specs=in_vmem(2),
        compiler_params=limits(),
        cost_estimate=small_cost(),
    )(momentum, *[b.array for b in flat])


def momentum_step(after, table, momentum, parts, owner_count):
    slots, rows, cols = momentum.shape
    flat = [b for part in parts for b in part]
    sizes = [len(part) for part in parts]
    return pl.pallas_call(
        functools.partial(momentum_kernel, 1.0 / owner_count, sizes, len(flat)),
        grid=(slots,),
        out_shape=[jax.ShapeDtypeStruct((slots, rows, cols), jnp.float32), token()],
        in_specs=in_smem()
        + [pl.BlockSpec((1, rows, cols), lambda s: (s, 0, 0))]
        + [
            pl.BlockSpec((1,) + b.array.shape[1:], lambda s, at=b.start: (s + at, 0, 0))
            for b in flat
        ]
        + anywhere(len(after)),
        out_specs=[
            pl.BlockSpec((1, rows, cols), lambda s: (s, 0, 0)),
            pl.BlockSpec((8, 128), lambda s: (0, 0)),
        ],
        compiler_params=limits(),
        cost_estimate=small_cost(),
    )(table, momentum, *[b.array for b in flat], *after)


def exact(a, b):
    def split(v):
        high = v.astype(jnp.bfloat16)
        return high, (v - high.astype(jnp.float32)).astype(jnp.bfloat16)

    def dot(p, q):
        return jnp.dot(p, q, preferred_element_type=jnp.float32)

    (a_high, a_low), (b_high, b_low) = split(a), split(b)
    return dot(a_high, b_high) + (dot(a_high, b_low) + dot(a_low, b_high))


def orthogonalize_kernel(factor, slots, grams, *refs):
    gram_refs = refs[:grams]
    rounded_ref = refs[grams]
    out_refs = refs[grams + 1 :]
    rows = rounded_ref.shape[1]
    row_ids = lax.broadcasted_iota(jnp.int32, (rows, rows), 0)
    col_ids = lax.broadcasted_iota(jnp.int32, (rows, rows), 1)
    diagonal = row_ids == col_ids
    held = []
    for s in range(slots):
        gram = gram_refs[0][s]
        for ref in gram_refs[1:]:
            gram = gram + ref[s]
        squares = jnp.sum(
            jnp.sum(jnp.where(diagonal, gram, 0.0), axis=0, keepdims=True),
            axis=1,
            keepdims=True,
        )
        inverse = 1.0 / (jnp.sqrt(squares) + EPSILON)
        held.append([gram * inverse * inverse, None, inverse])
    for step in range(ITERS):
        squared = [exact(h[0], h[0]) for h in held]
        factors = [
            COEF_B * h[0] + COEF_C * q + jnp.where(diagonal, COEF_A, 0.0)
            for h, q in zip(held, squared)
        ]
        for h, m in zip(held, factors):
            h[1] = m if h[1] is None else exact(m, h[1])
        if step + 1 < ITERS:
            once = [exact(m, h[0]) for h, m in zip(held, factors)]
            for h, m, o in zip(held, factors, once):
                h[0] = exact(m, o)
    for s, h in enumerate(held):
        whole = h[1] * (factor * h[2])
        high = whole.astype(jnp.bfloat16)
        low = (whole - high.astype(jnp.float32)).astype(jnp.bfloat16)
        rounded = rounded_ref[s]
        result = (
            jnp.dot(high, rounded, preferred_element_type=jnp.float32)
            + jnp.dot(low, rounded, preferred_element_type=jnp.float32)
        ).astype(jnp.bfloat16)
        first = 0
        for out_ref in out_refs:
            out_ref[s] = result[first : first + out_ref.shape[1]]
            first += out_ref.shape[1]


def orthogonalize(grams, rounded, factor, shares):
    slots, rows, cols = rounded.shape
    return pl.pallas_call(
        functools.partial(orthogonalize_kernel, factor, slots, len(grams)),
        out_shape=[
            jax.ShapeDtypeStruct((slots, share, cols), jnp.bfloat16) for share in shares
        ],
        in_specs=in_vmem(len(grams) + 1),
        out_specs=in_vmem(len(shares)),
        compiler_params=limits(),
        cost_estimate=small_cost(),
    )(*grams, rounded)


def swap(value, bit):
    count = lax.axis_size("dp")
    return lax.ppermute(value, "dp", [(i, i ^ bit) for i in range(count)])


def z_bits():
    bits, bit = [], 2 * X_BIT
    while bit < lax.axis_size("dp"):
        bits.append(bit)
        bit *= 2
    return bits


def offsets(bits):
    if not bits:
        return [0]
    rest = offsets(bits[1:])
    return [bits[0] | o for o in rest] + rest


def levels(bits):
    found = [[(0, -1)]]
    for _ in bits:
        longer = []
        for j, bit in enumerate(bits):
            longer += [(o | bit, j) for o, last in found[-1] if last < j]
        found.append(longer)
    return found


class Block:
    def __init__(self, array, start, split=1):
        self.array, self.start, self.split = array, start, split

    def item(self, slot):
        first = self.start + slot * self.split
        return tuple(range(first, first + self.split))


def sum_to_owners(gradient, me, owner, owners, slots, bits, cut):
    rest = gradient.shape[1] - cut
    level = [[o for o, _ in found] for found in levels(bits)]
    last = {o: bits[j] for found in levels(bits) for o, j in found if j >= 0}
    top = len(bits)
    other_bits = bits[::-1] + [X_BIT]
    other_order = tuple(offsets(other_bits))

    def batch(k):
        order = [o | X_BIT for o in level[k]]
        return tuple(order + (level[k + 1] if k < top else []))

    merged = {k: batch(k) for k in range(top, 0, -1)}
    merged[0] = batch(0) + (0,)

    def theirs(order):
        return tuple(CORE_BIT | o for o in order)

    split = cut // rest
    half = len(other_order) * slots // 2

    def first_items(places):
        return items_of(places(other_order), slots, cut, rest) + items_of(
            places(merged[top]), slots, 0, rest, split
        )

    def same(order):
        return order

    table, packed = first_pack(
        me, owner, owners, slots, gradient, first_items(theirs), rest
    )
    first_got = swap(packed, CORE_BIT)
    falling = range(top - 1, -1, -1)
    plans = [items_of(theirs(merged[k]), slots, 0, cut) for k in falling]
    packed = pack([packed], table, gradient, plans, cut)
    got = {k: swap(block, CORE_BIT) for k, block in zip(falling, packed)}
    after = [packed[0]]

    home = {}
    over_x = {}

    def take(k, after):
        order = merged[k]
        crossing = len(level[k]) * slots
        parts = (crossing,)
        if len(order) * slots > crossing:
            parts += (len(order) * slots - crossing,)
        items = items_of(order, slots, 0, cut)
        made = add_taken(after, table, gradient, items, got[k], parts)
        over_x[k] = made[0]
        for n, o in enumerate(order[len(level[k]) :]):
            home[o] = Block(made[1], n * slots)
        return [made[0]]

    parts = (half, half, len(merged[top]) * slots * split)
    away, kept, far = add_taken(
        after, table, gradient, first_items(same), first_got, parts
    )
    after = [away]
    other_got = swap(away, other_bits[0])
    x_got = swap(far, X_BIT)

    pending = {}
    for k in range(top, -1, -1):
        terms = {o: [] for o in level[k]}
        for n, o in enumerate(level[k]):
            cuts = split if k == top else 1
            terms[o].append(Block(x_got, n * slots * cuts, cuts))
        for o, value in pending.items():
            terms[o ^ last[o]].append(Block(value, 0))
        if k == 0:
            break
        if k == top:
            after = take(k - 1, after)
        wanted = []
        for o in level[k]:
            parts = [home[o]] + terms[o]
            wanted.append([[(b.array, b.item(s)) for b in parts] for s in range(slots)])
        half //= 2
        wanted.append(summed(kept, other_got, 0, half))
        wanted.append(summed(kept, other_got, half, 2 * half))
        held_back = k == 1
        if held_back:
            wanted.append(joined(over_x[0]))
        made = list(combine(after, *wanted))
        after = [made[0]]
        if held_back:
            over_x[0] = made.pop()
        else:
            after = take(k - 2, after)
        pending = {
            o: swap(made[n], last[o]) for n, o in reversed(list(enumerate(level[k])))
        }
        kept = made[-1]
        other_got = swap(made[-2], other_bits[top - k + 1])
        x_got = swap(over_x[k - 1], X_BIT)
    parts = [[home[0]] + terms[0], [Block(kept, 0), Block(other_got, 0)]]
    return table, parts


def spread_updates(blocks, table, slots, bits, cut, shape, early):
    level = levels(bits)
    last = [dict(found) for found in level]
    own, cur = blocks
    top = len(bits)
    cur_order = [0]
    other_bits = [X_BIT] + bits
    front, front_order = own, [0]
    pieces = {0: own}
    after, update = [early], None

    def with_core(array, first, order):
        return [
            (array, first, order),
            (swap(array, CORE_BIT), first, [CORE_BIT | o for o in order]),
        ]

    for k in range(top + 1):
        longer = {}
        for j, bit in enumerate(bits):
            for o, at in level[k]:
                if at < j:
                    longer[o | bit] = swap(pieces[o], bit)
        x_got = swap(front, X_BIT)
        other_got = swap(cur, other_bits[k])
        crossed = (x_got, 0, [X_BIT | o for o in front_order])
        crossed_other = (other_got, cut, [other_bits[k] | o for o in cur_order])
        if k == top:
            break
        if k > 0:
            update, ran = spread(after, update, shape, table, slots, waiting)
            after = [ran]
        waiting = []
        order = [o for o, _ in level[k + 1]]
        wanted = [joined(*[longer[o] for o in order]), joined(cur, other_got)]
        if k == 0:
            wanted.append(joined(front, x_got))
            front, cur, both = combine(after, *wanted)
            waiting += with_core(both, 0, front_order + crossed[2])
        else:
            front, cur = combine(after, *wanted)
            waiting += with_core(*crossed)
        after = [front]
        pieces = longer
        front_order = order
        cur_order = cur_order + crossed_other[2]
        last = with_core(front, 0, front_order)
        waiting += last if k + 1 < top else last[:1]
    waiting += with_core(cur, cut, cur_order)
    crossed, crossed_other = with_core(*crossed), with_core(*crossed_other)
    waiting += crossed[:1] + crossed_other[:1]
    update, _ = spread(after, update, shape, table, slots, waiting)
    waiting = last[1:] + crossed[1:] + crossed_other[1:]
    return spread([], update, shape, table, slots, waiting)[0]


def per_device(grads, owner, momentum):
    owner_count = lax.axis_size("dp")
    matrices = owner.shape[0]
    slot_count = momentum.shape[1]
    head_rows, cols = grads.shape[2:]
    factor = 0.2 * math.sqrt(max(R, D))
    me = lax.axis_index("dp").astype(jnp.int32).reshape(1)

    cut = head_rows * 3 // 4
    bits = z_bits()[::-1]
    table, parts = sum_to_owners(
        grads[0], me, owner, owner_count, slot_count, bits, cut
    )
    rounded, gram = nesterov_step(momentum[0], parts, owner_count)

    width = lax.axis_size("tensor")
    grams = [gram]
    for _ in range(width - 1):
        grams.append(
            lax.ppermute(
                grams[-1], "tensor", [(i, (i + 1) % width) for i in range(width)]
            )
        )
    blocks = orthogonalize(grams, rounded, factor, [cut, head_rows - cut])
    new_momentum, early = momentum_step(
        blocks[:1], table, momentum[0], parts, owner_count
    )
    shape = (matrices, head_rows, cols)
    update = spread_updates(
        blocks, table, slot_count, bits, cut, shape, early
    )
    return (update, new_momentum[None])


def solution(mesh):
    in_specs = (P("dp", None, None, "tensor"), P(), P("dp", None, None, "tensor"))
    out_specs = (P(None, None, "tensor"), P("dp", None, None, "tensor"))
    return jax.shard_map(
        per_device, mesh=mesh, in_specs=in_specs, out_specs=out_specs, check_vma=False
    )
```

```python
import functools
import math

import jax
import jax.numpy as jnp
from jax import lax
from jax.experimental import pallas as pl
from jax.experimental.pallas import tpu as pltpu
from jax.sharding import PartitionSpec as P

R = 128
D = 4096
ITERS = 5

COEF_A = 3.4445
COEF_B = -4.775
COEF_C = 2.0315
EPSILON = 1e-07
DECAY = 0.95

CORE_BIT = 1
X_BIT = 2
VMEM_BYTES = 24 * 1024 * 1024
MORE_VMEM_BYTES = 41 * 1024 * 1024


def in_vmem(count=1):
    return [pl.BlockSpec(memory_space=pltpu.VMEM)] * count


def anywhere(count=1):
    return [pl.BlockSpec(memory_space=pl.ANY)] * count


def in_hbm():
    return [pl.BlockSpec(memory_space=pltpu.HBM)]


def in_smem(count=1):
    return [pl.BlockSpec(memory_space=pltpu.SMEM)] * count


def limits(size=VMEM_BYTES):
    return pltpu.CompilerParams(vmem_limit_bytes=size)


def small_cost():
    return pl.CostEstimate(flops=0, bytes_accessed=0, transcendentals=0)


def token():
    return jax.ShapeDtypeStruct((8, 128), jnp.float32)


def table_kernel(slots, me_ref, owner_ref, table_ref, used):
    spots, matrices = table_ref.shape[0], owner_ref.shape[0]

    @pl.loop(0, spots)
    def _(i):
        table_ref[i] = -1

    @pl.loop(0, spots // slots)
    def _(i):
        used[i] = 0

    @pl.loop(0, matrices)
    def _(m):
        at = owner_ref[m]
        rank = used[at]
        table_ref[(at ^ me_ref[0]) * slots + rank] = m
        used[at] = rank + 1


def starts(order, slots):
    return [
        (n * slots + s, offset * slots + s)
        for n, offset in enumerate(order)
        for s in range(slots)
    ]


def items_of(order, slots, first, rows, split=1):
    return tuple(
        (place, first + c * rows) for _, place in starts(order, slots) for c in range(split)
    )


def fetch(table_ref, src_ref, items, into, sem):
    rows = into.shape[1]
    for item, (place, first) in enumerate(items):
        matrix = jnp.maximum(table_ref[place], 0)
        pltpu.make_async_copy(
            src_ref.at[matrix, pl.ds(first, rows)], into.at[item], sem.at[item]
        ).start()
    return lambda i: pltpu.make_async_copy(
        src_ref.at[0, pl.ds(0, rows)], into.at[i], sem.at[i]
    )


def pack_kernel(plans, table_ref, src_ref, *rest):
    out_refs = rest[-2 * len(plans) : -len(plans)]
    sems = rest[-len(plans) :]
    copies = [
        fetch(table_ref, src_ref, items, out_ref, sem)
        for items, out_ref, sem in zip(plans, out_refs, sems)
    ]
    for copy, out_ref in zip(copies, out_refs):

        @pl.loop(0, out_ref.shape[0])
        def _(i, copy=copy):
            copy(i).wait()


def pack(after, table, src, plans, sizes):
    return pl.pallas_call(
        functools.partial(pack_kernel, tuple(plans)),
        out_shape=[
            jax.ShapeDtypeStruct((len(items), rows, src.shape[2]), src.dtype)
            for items, rows in zip(plans, sizes)
        ],
        in_specs=in_smem() + in_hbm() + anywhere(len(after)),
        out_specs=in_vmem(len(plans)),
        scratch_shapes=[pltpu.SemaphoreType.DMA((len(items),)) for items in plans],
        compiler_params=limits(MORE_VMEM_BYTES),
        cost_estimate=small_cost(),
    )(table, src, *after)


def first_pack_kernel(items, slots, me_ref, owner_ref, src_ref, *rest):
    table_ref, out_ref, used, sem = rest
    table_kernel(slots, me_ref, owner_ref, table_ref, used)
    copy = fetch(table_ref, src_ref, items, out_ref, sem)

    @pl.loop(0, out_ref.shape[0])
    def _(i):
        copy(i).wait()


def first_pack(me, owner, owners, slots, src, items, rows):
    count = len(items)
    return pl.pallas_call(
        functools.partial(first_pack_kernel, items, slots),
        out_shape=[
            jax.ShapeDtypeStruct((owners * slots,), jnp.int32),
            jax.ShapeDtypeStruct((count, rows, src.shape[2]), src.dtype),
        ],
        in_specs=in_smem(2) + in_hbm(),
        out_specs=in_smem() + in_vmem(),
        scratch_shapes=[
            pltpu.SMEM((owners,), jnp.int32),
            pltpu.SemaphoreType.DMA((count,)),
        ],
        compiler_params=limits(MORE_VMEM_BYTES),
        cost_estimate=small_cost(),
    )(me, owner, src)


def add_taken_kernel(items, parts, table_ref, src_ref, got_ref, *rest):
    mine, sem = rest[-2:]
    out_refs = rest[-2 - len(parts) : -2]
    copy = fetch(table_ref, src_ref, items, mine, sem)
    start = 0
    for size, out_ref in zip(parts, out_refs):

        @pl.loop(0, size)
        def _(i, start=start, out_ref=out_ref):
            copy(start + i).wait()
            out_ref[i] = got_ref[start + i] + mine[start + i]

        start += size


def add_taken(after, table, src, items, got, parts):
    count, rows, cols = got.shape
    return pl.pallas_call(
        functools.partial(add_taken_kernel, items, parts),
        out_shape=[jax.ShapeDtypeStruct((n, rows, cols), got.dtype) for n in parts],
        in_specs=in_smem() + in_hbm() + in_vmem() + anywhere(len(after)),
        out_specs=in_vmem(len(parts)),
        scratch_shapes=[
            pltpu.VMEM(got.shape, got.dtype),
            pltpu.SemaphoreType.DMA((count,)),
        ],
        compiler_params=limits(MORE_VMEM_BYTES),
        cost_estimate=small_cost(),
    )(table, src, got, *after)


def combine_kernel(arrays, plans, *refs):
    sources = refs[:arrays]
    outs = refs[len(refs) - len(plans) :]
    for out_ref, items in zip(outs, plans):
        for i, terms in enumerate(items):
            cuts = max(len(item) for _, item in terms)
            rows = out_ref.shape[1] // cuts
            for c in range(cuts):
                here = pl.ds(c * rows, rows)
                total = None
                for at, item in terms:
                    if len(item) == cuts:
                        term = sources[at][item[c]]
                    else:
                        term = sources[at][item[0], here]
                    total = term if total is None else total + term
                out_ref[i, here] = total


def combine(after, *wanted):
    arrays, plans = [], []
    for items in wanted:
        plan = []
        for terms in items:
            found = []
            for array, item in terms:
                places = [i for i, a in enumerate(arrays) if a is array]
                if not places:
                    arrays.append(array)
                    places = [len(arrays) - 1]
                found.append((places[0], item if isinstance(item, tuple) else (item,)))
            plan.append(tuple(found))
        plans.append(tuple(plan))
    shapes = []
    for items in wanted:
        sample = items[0][0][0]
        shapes.append(
            jax.ShapeDtypeStruct((len(items),) + sample.shape[1:], sample.dtype)
        )
    return pl.pallas_call(
        functools.partial(combine_kernel, len(arrays), tuple(plans)),
        out_shape=shapes,
        in_specs=in_vmem(len(arrays)) + anywhere(len(after)),
        out_specs=in_vmem(len(plans)),
        compiler_params=limits(),
        cost_estimate=small_cost(),
    )(*arrays, *after)


def joined(*arrays):
    return [[(array, i)] for array in arrays for i in range(array.shape[0])]


def summed(home, got, first, last):
    return [[(home, i), (got, i)] for i in range(first, last)]


def spread_kernel(plans, slots, table_ref, *refs):
    piece_refs = refs[: len(plans)]
    out_ref, token_ref, sem = refs[-3:]
    token_ref[...] = jnp.zeros_like(token_ref)
    for wait in (False, True):
        for p, (first, order) in enumerate(plans):
            for item, place in starts(order, slots):
                to = table_ref[place]

                @pl.when(to >= 0)
                def _(p=p, item=item, to=to, wait=wait, first=first):
                    rows = piece_refs[p].shape[1]
                    copy = pltpu.make_async_copy(
                        piece_refs[p].at[item],
                        out_ref.at[to, pl.ds(first, rows)],
                        sem.at[p, item],
                    )
                    if wait:
                        copy.wait()
                    else:
                        copy.start()


def spread(after, target, shape, table, slots, pieces):
    count = len(pieces)
    arrays = [array for array, _, _ in pieces]
    plans = tuple((first, tuple(order)) for _, first, order in pieces)
    most = max(a.shape[0] for a in arrays)
    more = [] if target is None else [target]
    return pl.pallas_call(
        functools.partial(spread_kernel, plans, slots),
        out_shape=[jax.ShapeDtypeStruct(shape, arrays[0].dtype), token()],
        in_specs=in_smem() + in_vmem(count) + anywhere(len(more) + len(after)),
        out_specs=anywhere() + in_vmem(),
        scratch_shapes=[pltpu.SemaphoreType.DMA((count, most))],
        input_output_aliases={1 + count: 0} if more else {},
        compiler_params=limits(MORE_VMEM_BYTES),
        cost_estimate=small_cost(),
    )(table, *arrays, *more, *after)


def mean_rows(scale, sizes, refs):
    first, used = 0, 0
    for size in sizes:
        total = None
        for ref, item in refs[used : used + size]:
            term = ref[item].astype(jnp.float32)
            total = term if total is None else total + term
        yield first, total * scale
        first += total.shape[0]
        used += size


def nesterov_kernel(scale, sizes, items, momentum_ref, *rest):
    part_refs, (rounded_ref, gram_ref) = rest[: len(items)], rest[len(items) :]
    for s in range(momentum_ref.shape[0]):
        refs = [(ref, item + s) for ref, item in zip(part_refs, items)]
        for first, mean in mean_rows(scale, sizes, refs):
            here = pl.ds(first, mean.shape[0])
            following = DECAY * momentum_ref[s, here] + mean
            rounded_ref[s, here] = (mean + DECAY * following).astype(jnp.bfloat16)
        rounded = rounded_ref[s]
        gram_ref[s] = lax.dot_general(
            rounded,
            rounded,
            (((1,), (1,)), ((), ())),
            preferred_element_type=jnp.float32,
        )


def momentum_kernel(scale, sizes, count, table_ref, momentum_ref, *rest):
    part_refs, (next_ref, token_ref) = rest[:count], rest[-2:]
    token_ref[...] = jnp.zeros_like(token_ref)
    held = table_ref[pl.program_id(0)] >= 0
    for first, mean in mean_rows(scale, sizes, [(ref, 0) for ref in part_refs]):
        here = pl.ds(first, mean.shape[0])
        previous = momentum_ref[0, here]
        next_ref[0, here] = jnp.where(held, DECAY * previous + mean, previous)


def nesterov_step(momentum, parts, owner_count):
    slots, rows, cols = momentum.shape
    flat = [b for part in parts for b in part]
    sizes = [len(part) for part in parts]
    items = [b.start for b in flat]
    return pl.pallas_call(
        functools.partial(nesterov_kernel, 1.0 / owner_count, sizes, items),
        out_shape=[
            jax.ShapeDtypeStruct((slots, rows, cols), jnp.bfloat16),
            jax.ShapeDtypeStruct((slots, rows, rows), jnp.float32),
        ],
        in_specs=in_vmem(1 + len(flat)),
        out_specs=in_vmem(2),
        compiler_params=limits(),
        cost_estimate=small_cost(),
    )(momentum, *[b.array for b in flat])


def momentum_step(after, table, momentum, parts, owner_count):
    slots, rows, cols = momentum.shape
    flat = [b for part in parts for b in part]
    sizes = [len(part) for part in parts]
    return pl.pallas_call(
        functools.partial(momentum_kernel, 1.0 / owner_count, sizes, len(flat)),
        grid=(slots,),
        out_shape=[jax.ShapeDtypeStruct((slots, rows, cols), jnp.float32), token()],
        in_specs=in_smem()
        + [pl.BlockSpec((1, rows, cols), lambda s: (s, 0, 0))]
        + [
            pl.BlockSpec((1,) + b.array.shape[1:], lambda s, at=b.start: (s + at, 0, 0))
            for b in flat
        ]
        + anywhere(len(after)),
        out_specs=[
            pl.BlockSpec((1, rows, cols), lambda s: (s, 0, 0)),
            pl.BlockSpec((8, 128), lambda s: (0, 0)),
        ],
        compiler_params=limits(),
        cost_estimate=small_cost(),
    )(table, momentum, *[b.array for b in flat], *after)


def exact(a, b):
    def split(v):
        high = v.astype(jnp.bfloat16)
        return high, (v - high.astype(jnp.float32)).astype(jnp.bfloat16)

    def dot(p, q):
        return jnp.dot(p, q, preferred_element_type=jnp.float32)

    (a_high, a_low), (b_high, b_low) = split(a), split(b)
    return dot(a_high, b_high) + (dot(a_high, b_low) + dot(a_low, b_high))


def orthogonalize_kernel(factor, slots, grams, *refs):
    gram_refs = refs[:grams]
    rounded_ref = refs[grams]
    out_refs = refs[grams + 1 :]
    rows = rounded_ref.shape[1]
    row_ids = lax.broadcasted_iota(jnp.int32, (rows, rows), 0)
    col_ids = lax.broadcasted_iota(jnp.int32, (rows, rows), 1)
    diagonal = row_ids == col_ids
    held = []
    for s in range(slots):
        gram = gram_refs[0][s]
        for ref in gram_refs[1:]:
            gram = gram + ref[s]
        squares = jnp.sum(
            jnp.sum(jnp.where(diagonal, gram, 0.0), axis=0, keepdims=True),
            axis=1,
            keepdims=True,
        )
        inverse = 1.0 / (jnp.sqrt(squares) + EPSILON)
        held.append([gram * inverse * inverse, None, inverse])
    for step in range(ITERS):
        squared = [exact(h[0], h[0]) for h in held]
        factors = [
            COEF_B * h[0] + COEF_C * q + jnp.where(diagonal, COEF_A, 0.0)
            for h, q in zip(held, squared)
        ]
        for h, m in zip(held, factors):
            h[1] = m if h[1] is None else exact(m, h[1])
        if step + 1 < ITERS:
            once = [exact(m, h[0]) for h, m in zip(held, factors)]
            for h, m, o in zip(held, factors, once):
                h[0] = exact(m, o)
    for s, h in enumerate(held):
        whole = h[1] * (factor * h[2])
        high = whole.astype(jnp.bfloat16)
        low = (whole - high.astype(jnp.float32)).astype(jnp.bfloat16)
        rounded = rounded_ref[s]
        result = (
            jnp.dot(high, rounded, preferred_element_type=jnp.float32)
            + jnp.dot(low, rounded, preferred_element_type=jnp.float32)
        ).astype(jnp.bfloat16)
        first = 0
        for out_ref in out_refs:
            out_ref[s] = result[first : first + out_ref.shape[1]]
            first += out_ref.shape[1]


def orthogonalize(grams, rounded, factor, shares):
    slots, rows, cols = rounded.shape
    return pl.pallas_call(
        functools.partial(orthogonalize_kernel, factor, slots, len(grams)),
        out_shape=[
            jax.ShapeDtypeStruct((slots, share, cols), jnp.bfloat16) for share in shares
        ],
        in_specs=in_vmem(len(grams) + 1),
        out_specs=in_vmem(len(shares)),
        compiler_params=limits(),
        cost_estimate=small_cost(),
    )(*grams, rounded)


def swap(value, bit):
    count = lax.axis_size("dp")
    return lax.ppermute(value, "dp", [(i, i ^ bit) for i in range(count)])


def z_bits():
    bits, bit = [], 2 * X_BIT
    while bit < lax.axis_size("dp"):
        bits.append(bit)
        bit *= 2
    return bits


def offsets(bits):
    if not bits:
        return [0]
    rest = offsets(bits[1:])
    return [bits[0] | o for o in rest] + rest


def levels(bits):
    found = [[(0, -1)]]
    for _ in bits:
        longer = []
        for j, bit in enumerate(bits):
            longer += [(o | bit, j) for o, last in found[-1] if last < j]
        found.append(longer)
    return found


class Block:
    def __init__(self, array, start, split=1):
        self.array, self.start, self.split = array, start, split

    def item(self, slot):
        first = self.start + slot * self.split
        return tuple(range(first, first + self.split))


def sum_to_owners(gradient, me, owner, owners, slots, bits, cut):
    rest = gradient.shape[1] - cut
    level = [[o for o, _ in found] for found in levels(bits)]
    last = {o: bits[j] for found in levels(bits) for o, j in found if j >= 0}
    top = len(bits)
    other_bits = bits[::-1] + [X_BIT]
    other_order = tuple(offsets(other_bits))

    def batch(k):
        order = [o | X_BIT for o in level[k]]
        return tuple(order + (level[k + 1] if k < top else []))

    merged = {k: batch(k) for k in range(top, 0, -1)}
    merged[0] = batch(0) + (0,)

    def theirs(order):
        return tuple(CORE_BIT | o for o in order)

    split = cut // rest
    half = len(other_order) * slots // 2

    def first_items(places):
        return items_of(places(other_order), slots, cut, rest) + items_of(
            places(merged[top]), slots, 0, rest, split
        )

    def same(order):
        return order

    table, packed = first_pack(
        me, owner, owners, slots, gradient, first_items(theirs), rest
    )
    first_got = swap(packed, CORE_BIT)
    falling = range(top - 1, -1, -1)
    plans = [items_of(theirs(merged[k]), slots, 0, cut) for k in falling]
    plans.append(first_items(same))
    *packed, mine = pack([packed], table, gradient, plans, [cut] * top + [rest])
    got = {k: swap(block, CORE_BIT) for k, block in zip(falling, packed)}
    after = [packed[0]]

    home = {}
    over_x = {}

    def take(k, after):
        order = merged[k]
        crossing = len(level[k]) * slots
        parts = (crossing,)
        if len(order) * slots > crossing:
            parts += (len(order) * slots - crossing,)
        items = items_of(order, slots, 0, cut)
        made = add_taken(after, table, gradient, items, got[k], parts)
        over_x[k] = made[0]
        for n, o in enumerate(order[len(level[k]) :]):
            home[o] = Block(made[1], n * slots)
        return [made[0]]

    away, kept, far = combine(
        after,
        summed(mine, first_got, 0, half),
        summed(mine, first_got, half, 2 * half),
        summed(mine, first_got, 2 * half, mine.shape[0]),
    )
    after = [away]
    other_got = swap(away, other_bits[0])
    x_got = swap(far, X_BIT)

    pending = {}
    for k in range(top, -1, -1):
        terms = {o: [] for o in level[k]}
        for n, o in enumerate(level[k]):
            cuts = split if k == top else 1
            terms[o].append(Block(x_got, n * slots * cuts, cuts))
        for o, value in pending.items():
            terms[o ^ last[o]].append(Block(value, 0))
        if k == 0:
            break
        if k == top:
            after = take(k - 1, after)
        wanted = []
        for o in level[k]:
            parts = [home[o]] + terms[o]
            wanted.append([[(b.array, b.item(s)) for b in parts] for s in range(slots)])
        half //= 2
        wanted.append(summed(kept, other_got, 0, half))
        wanted.append(summed(kept, other_got, half, 2 * half))
        held_back = k == 1
        if held_back:
            wanted.append(joined(over_x[0]))
        made = list(combine(after, *wanted))
        after = [made[0]]
        if held_back:
            over_x[0] = made.pop()
        else:
            after = take(k - 2, after)
        pending = {
            o: swap(made[n], last[o]) for n, o in reversed(list(enumerate(level[k])))
        }
        kept = made[-1]
        other_got = swap(made[-2], other_bits[top - k + 1])
        x_got = swap(over_x[k - 1], X_BIT)
    parts = [[home[0]] + terms[0], [Block(kept, 0), Block(other_got, 0)]]
    return table, parts


def spread_updates(blocks, table, slots, bits, cut, shape, early):
    level = levels(bits)
    last = [dict(found) for found in level]
    own, cur = blocks
    top = len(bits)
    cur_order = [0]
    other_bits = [X_BIT] + bits
    front, front_order = own, [0]
    pieces = {0: own}
    after, update = [early], None

    def with_core(array, first, order):
        return [
            (array, first, order),
            (swap(array, CORE_BIT), first, [CORE_BIT | o for o in order]),
        ]

    for k in range(top + 1):
        longer = {}
        for j, bit in enumerate(bits):
            for o, at in level[k]:
                if at < j:
                    longer[o | bit] = swap(pieces[o], bit)
        x_got = swap(front, X_BIT)
        other_got = swap(cur, other_bits[k])
        crossed = (x_got, 0, [X_BIT | o for o in front_order])
        crossed_other = (other_got, cut, [other_bits[k] | o for o in cur_order])
        if k == top:
            break
        if k > 0:
            update, ran = spread(after, update, shape, table, slots, waiting)
            after = [ran]
        waiting = []
        order = [o for o, _ in level[k + 1]]
        wanted = [joined(*[longer[o] for o in order]), joined(cur, other_got)]
        if k == 0:
            wanted.append(joined(front, x_got))
            front, cur, both = combine(after, *wanted)
            waiting += with_core(both, 0, front_order + crossed[2])
        else:
            front, cur = combine(after, *wanted)
            waiting += with_core(*crossed)
        after = [front]
        pieces = longer
        front_order = order
        cur_order = cur_order + crossed_other[2]
        last = with_core(front, 0, front_order)
        waiting += last if k + 1 < top else last[:1]
    waiting += with_core(cur, cut, cur_order)
    crossed, crossed_other = with_core(*crossed), with_core(*crossed_other)
    waiting += crossed[:1] + crossed_other[:1]
    update, _ = spread(after, update, shape, table, slots, waiting)
    waiting = last[1:] + crossed[1:] + crossed_other[1:]
    return spread([], update, shape, table, slots, waiting)[0]


def per_device(grads, owner, momentum):
    owner_count = lax.axis_size("dp")
    matrices = owner.shape[0]
    slot_count = momentum.shape[1]
    head_rows, cols = grads.shape[2:]
    factor = 0.2 * math.sqrt(max(R, D))
    me = lax.axis_index("dp").astype(jnp.int32).reshape(1)

    cut = head_rows * 3 // 4
    bits = z_bits()[::-1]
    table, parts = sum_to_owners(
        grads[0], me, owner, owner_count, slot_count, bits, cut
    )
    rounded, gram = nesterov_step(momentum[0], parts, owner_count)

    width = lax.axis_size("tensor")
    grams = [gram]
    for _ in range(width - 1):
        grams.append(
            lax.ppermute(
                grams[-1], "tensor", [(i, (i + 1) % width) for i in range(width)]
            )
        )
    blocks = orthogonalize(grams, rounded, factor, [cut, head_rows - cut])
    new_momentum, early = momentum_step(
        blocks[:1], table, momentum[0], parts, owner_count
    )
    shape = (matrices, head_rows, cols)
    update = spread_updates(
        blocks, table, slot_count, bits, cut, shape, early
    )
    return (update, new_momentum[None])


def solution(mesh):
    in_specs = (P("dp", None, None, "tensor"), P(), P("dp", None, None, "tensor"))
    out_specs = (P(None, None, "tensor"), P("dp", None, None, "tensor"))
    return jax.shard_map(
        per_device, mesh=mesh, in_specs=in_specs, out_specs=out_specs, check_vma=False
    )
```

```python
import functools
import math

import jax
import jax.numpy as jnp
from jax import lax
from jax.experimental import pallas as pl
from jax.experimental.pallas import tpu as pltpu
from jax.sharding import PartitionSpec as P

R = 128
D = 4096
ITERS = 5

COEF_A = 3.4445
COEF_B = -4.775
COEF_C = 2.0315
EPSILON = 1e-07
DECAY = 0.95

CORE_BIT = 1
X_BIT = 2
VMEM_BYTES = 24 * 1024 * 1024
MORE_VMEM_BYTES = 41 * 1024 * 1024


def in_vmem(count=1):
    return [pl.BlockSpec(memory_space=pltpu.VMEM)] * count


def anywhere(count=1):
    return [pl.BlockSpec(memory_space=pl.ANY)] * count


def in_hbm():
    return [pl.BlockSpec(memory_space=pltpu.HBM)]


def in_smem(count=1):
    return [pl.BlockSpec(memory_space=pltpu.SMEM)] * count


def limits(size=VMEM_BYTES):
    return pltpu.CompilerParams(vmem_limit_bytes=size)


def small_cost():
    return pl.CostEstimate(flops=0, bytes_accessed=0, transcendentals=0)


def token():
    return jax.ShapeDtypeStruct((8, 128), jnp.float32)


def table_kernel(slots, me_ref, owner_ref, table_ref, used):
    spots, matrices = table_ref.shape[0], owner_ref.shape[0]

    @pl.loop(0, spots)
    def _(i):
        table_ref[i] = -1

    @pl.loop(0, spots // slots)
    def _(i):
        used[i] = 0

    @pl.loop(0, matrices)
    def _(m):
        at = owner_ref[m]
        rank = used[at]
        table_ref[(at ^ me_ref[0]) * slots + rank] = m
        used[at] = rank + 1


def starts(order, slots):
    return [
        (n * slots + s, offset * slots + s)
        for n, offset in enumerate(order)
        for s in range(slots)
    ]


def items_of(order, slots, first, rows, split=1):
    return tuple(
        (place, first + c * rows) for _, place in starts(order, slots) for c in range(split)
    )


def fetch(table_ref, src_ref, items, into, sem):
    rows = into.shape[1]
    for item, (place, first) in enumerate(items):
        matrix = jnp.maximum(table_ref[place], 0)
        pltpu.make_async_copy(
            src_ref.at[matrix, pl.ds(first, rows)], into.at[item], sem.at[item]
        ).start()
    return lambda i: pltpu.make_async_copy(
        src_ref.at[0, pl.ds(0, rows)], into.at[i], sem.at[i]
    )


def pack_kernel(plans, table_ref, src_ref, *rest):
    out_refs = rest[-2 * len(plans) : -len(plans)]
    sems = rest[-len(plans) :]
    copies = [
        fetch(table_ref, src_ref, items, out_ref, sem)
        for items, out_ref, sem in zip(plans, out_refs, sems)
    ]
    for copy, out_ref in zip(copies, out_refs):

        @pl.loop(0, out_ref.shape[0])
        def _(i, copy=copy):
            copy(i).wait()


def pack(after, table, src, plans, sizes):
    return pl.pallas_call(
        functools.partial(pack_kernel, tuple(plans)),
        out_shape=[
            jax.ShapeDtypeStruct((len(items), rows, src.shape[2]), src.dtype)
            for items, rows in zip(plans, sizes)
        ],
        in_specs=in_smem() + in_hbm() + anywhere(len(after)),
        out_specs=in_vmem(len(plans)),
        scratch_shapes=[pltpu.SemaphoreType.DMA((len(items),)) for items in plans],
        compiler_params=limits(MORE_VMEM_BYTES),
        cost_estimate=small_cost(),
    )(table, src, *after)


def first_pack_kernel(items, slots, me_ref, owner_ref, src_ref, *rest):
    table_ref, out_ref, used, sem = rest
    table_kernel(slots, me_ref, owner_ref, table_ref, used)
    copy = fetch(table_ref, src_ref, items, out_ref, sem)

    @pl.loop(0, out_ref.shape[0])
    def _(i):
        copy(i).wait()


def first_pack(me, owner, owners, slots, src, items, rows):
    count = len(items)
    return pl.pallas_call(
        functools.partial(first_pack_kernel, items, slots),
        out_shape=[
            jax.ShapeDtypeStruct((owners * slots,), jnp.int32),
            jax.ShapeDtypeStruct((count, rows, src.shape[2]), src.dtype),
        ],
        in_specs=in_smem(2) + in_hbm(),
        out_specs=in_smem() + in_vmem(),
        scratch_shapes=[
            pltpu.SMEM((owners,), jnp.int32),
            pltpu.SemaphoreType.DMA((count,)),
        ],
        compiler_params=limits(MORE_VMEM_BYTES),
        cost_estimate=small_cost(),
    )(me, owner, src)


def add_taken_kernel(items, parts, offset, table_ref, src_ref, got_ref, *rest):
    mine, sem = rest[-2:]
    out_refs = rest[-2 - len(parts) : -2]
    copy = fetch(table_ref, src_ref, items, mine, sem)
    start = 0
    for size, out_ref in zip(parts, out_refs):

        @pl.loop(0, size)
        def _(i, start=start, out_ref=out_ref):
            copy(start + i).wait()
            out_ref[i] = got_ref[offset + start + i] + mine[start + i]

        start += size


def add_taken(after, table, src, items, got, parts, offset=0):
    count, (_, rows, cols) = len(items), got.shape
    return pl.pallas_call(
        functools.partial(add_taken_kernel, items, parts, offset),
        out_shape=[jax.ShapeDtypeStruct((n, rows, cols), got.dtype) for n in parts],
        in_specs=in_smem() + in_hbm() + in_vmem() + anywhere(len(after)),
        out_specs=in_vmem(len(parts)),
        scratch_shapes=[
            pltpu.VMEM((count, rows, cols), got.dtype),
            pltpu.SemaphoreType.DMA((count,)),
        ],
        compiler_params=limits(MORE_VMEM_BYTES),
        cost_estimate=small_cost(),
    )(table, src, got, *after)


def combine_kernel(arrays, plans, *refs):
    sources = refs[:arrays]
    outs = refs[len(refs) - len(plans) :]
    for out_ref, items in zip(outs, plans):
        for i, terms in enumerate(items):
            cuts = max(len(item) for _, item in terms)
            rows = out_ref.shape[1] // cuts
            for c in range(cuts):
                here = pl.ds(c * rows, rows)
                total = None
                for at, item in terms:
                    if len(item) == cuts:
                        term = sources[at][item[c]]
                    else:
                        term = sources[at][item[0], here]
                    total = term if total is None else total + term
                out_ref[i, here] = total


def combine(after, *wanted):
    arrays, plans = [], []
    for items in wanted:
        plan = []
        for terms in items:
            found = []
            for array, item in terms:
                places = [i for i, a in enumerate(arrays) if a is array]
                if not places:
                    arrays.append(array)
                    places = [len(arrays) - 1]
                found.append((places[0], item if isinstance(item, tuple) else (item,)))
            plan.append(tuple(found))
        plans.append(tuple(plan))
    shapes = []
    for items in wanted:
        sample = items[0][0][0]
        shapes.append(
            jax.ShapeDtypeStruct((len(items),) + sample.shape[1:], sample.dtype)
        )
    return pl.pallas_call(
        functools.partial(combine_kernel, len(arrays), tuple(plans)),
        out_shape=shapes,
        in_specs=in_vmem(len(arrays)) + anywhere(len(after)),
        out_specs=in_vmem(len(plans)),
        compiler_params=limits(),
        cost_estimate=small_cost(),
    )(*arrays, *after)


def joined(*arrays):
    return [[(array, i)] for array in arrays for i in range(array.shape[0])]


def summed(home, got, first, last):
    return [[(home, i), (got, i)] for i in range(first, last)]


def spread_kernel(plans, slots, table_ref, *refs):
    piece_refs = refs[: len(plans)]
    out_ref, token_ref, sem = refs[-3:]
    token_ref[...] = jnp.zeros_like(token_ref)
    for wait in (False, True):
        for p, (first, order) in enumerate(plans):
            for item, place in starts(order, slots):
                to = table_ref[place]

                @pl.when(to >= 0)
                def _(p=p, item=item, to=to, wait=wait, first=first):
                    rows = piece_refs[p].shape[1]
                    copy = pltpu.make_async_copy(
                        piece_refs[p].at[item],
                        out_ref.at[to, pl.ds(first, rows)],
                        sem.at[p, item],
                    )
                    if wait:
                        copy.wait()
                    else:
                        copy.start()


def spread(after, target, shape, table, slots, pieces):
    count = len(pieces)
    arrays = [array for array, _, _ in pieces]
    plans = tuple((first, tuple(order)) for _, first, order in pieces)
    most = max(a.shape[0] for a in arrays)
    more = [] if target is None else [target]
    return pl.pallas_call(
        functools.partial(spread_kernel, plans, slots),
        out_shape=[jax.ShapeDtypeStruct(shape, arrays[0].dtype), token()],
        in_specs=in_smem() + in_vmem(count) + anywhere(len(more) + len(after)),
        out_specs=anywhere() + in_vmem(),
        scratch_shapes=[pltpu.SemaphoreType.DMA((count, most))],
        input_output_aliases={1 + count: 0} if more else {},
        compiler_params=limits(MORE_VMEM_BYTES),
        cost_estimate=small_cost(),
    )(table, *arrays, *more, *after)


def mean_rows(scale, sizes, refs):
    first, used = 0, 0
    for size in sizes:
        total = None
        for ref, item in refs[used : used + size]:
            term = ref[item].astype(jnp.float32)
            total = term if total is None else total + term
        yield first, total * scale
        first += total.shape[0]
        used += size


def nesterov_kernel(scale, sizes, items, momentum_ref, *rest):
    part_refs, (rounded_ref, gram_ref) = rest[: len(items)], rest[len(items) :]
    for s in range(momentum_ref.shape[0]):
        refs = [(ref, item + s) for ref, item in zip(part_refs, items)]
        for first, mean in mean_rows(scale, sizes, refs):
            here = pl.ds(first, mean.shape[0])
            following = DECAY * momentum_ref[s, here] + mean
            rounded_ref[s, here] = (mean + DECAY * following).astype(jnp.bfloat16)
        rounded = rounded_ref[s]
        gram_ref[s] = lax.dot_general(
            rounded,
            rounded,
            (((1,), (1,)), ((), ())),
            preferred_element_type=jnp.float32,
        )


def momentum_kernel(scale, sizes, count, table_ref, momentum_ref, *rest):
    part_refs, (next_ref, token_ref) = rest[:count], rest[-2:]
    token_ref[...] = jnp.zeros_like(token_ref)
    held = table_ref[pl.program_id(0)] >= 0
    for first, mean in mean_rows(scale, sizes, [(ref, 0) for ref in part_refs]):
        here = pl.ds(first, mean.shape[0])
        previous = momentum_ref[0, here]
        next_ref[0, here] = jnp.where(held, DECAY * previous + mean, previous)


def nesterov_step(momentum, parts, owner_count):
    slots, rows, cols = momentum.shape
    flat = [b for part in parts for b in part]
    sizes = [len(part) for part in parts]
    items = [b.start for b in flat]
    return pl.pallas_call(
        functools.partial(nesterov_kernel, 1.0 / owner_count, sizes, items),
        out_shape=[
            jax.ShapeDtypeStruct((slots, rows, cols), jnp.bfloat16),
            jax.ShapeDtypeStruct((slots, rows, rows), jnp.float32),
        ],
        in_specs=in_vmem(1 + len(flat)),
        out_specs=in_vmem(2),
        compiler_params=limits(),
        cost_estimate=small_cost(),
    )(momentum, *[b.array for b in flat])


def momentum_step(after, table, momentum, parts, owner_count):
    slots, rows, cols = momentum.shape
    flat = [b for part in parts for b in part]
    sizes = [len(part) for part in parts]
    return pl.pallas_call(
        functools.partial(momentum_kernel, 1.0 / owner_count, sizes, len(flat)),
        grid=(slots,),
        out_shape=[jax.ShapeDtypeStruct((slots, rows, cols), jnp.float32), token()],
        in_specs=in_smem()
        + [pl.BlockSpec((1, rows, cols), lambda s: (s, 0, 0))]
        + [
            pl.BlockSpec((1,) + b.array.shape[1:], lambda s, at=b.start: (s + at, 0, 0))
            for b in flat
        ]
        + anywhere(len(after)),
        out_specs=[
            pl.BlockSpec((1, rows, cols), lambda s: (s, 0, 0)),
            pl.BlockSpec((8, 128), lambda s: (0, 0)),
        ],
        compiler_params=limits(),
        cost_estimate=small_cost(),
    )(table, momentum, *[b.array for b in flat], *after)


def exact(a, b):
    def split(v):
        high = v.astype(jnp.bfloat16)
        return high, (v - high.astype(jnp.float32)).astype(jnp.bfloat16)

    def dot(p, q):
        return jnp.dot(p, q, preferred_element_type=jnp.float32)

    (a_high, a_low), (b_high, b_low) = split(a), split(b)
    return dot(a_high, b_high) + (dot(a_high, b_low) + dot(a_low, b_high))


def orthogonalize_kernel(factor, slots, grams, *refs):
    gram_refs = refs[:grams]
    rounded_ref = refs[grams]
    out_refs = refs[grams + 1 :]
    rows = rounded_ref.shape[1]
    row_ids = lax.broadcasted_iota(jnp.int32, (rows, rows), 0)
    col_ids = lax.broadcasted_iota(jnp.int32, (rows, rows), 1)
    diagonal = row_ids == col_ids
    held = []
    for s in range(slots):
        gram = gram_refs[0][s]
        for ref in gram_refs[1:]:
            gram = gram + ref[s]
        squares = jnp.sum(
            jnp.sum(jnp.where(diagonal, gram, 0.0), axis=0, keepdims=True),
            axis=1,
            keepdims=True,
        )
        inverse = 1.0 / (jnp.sqrt(squares) + EPSILON)
        held.append([gram * inverse * inverse, None, inverse])
    for step in range(ITERS):
        squared = [exact(h[0], h[0]) for h in held]
        factors = [
            COEF_B * h[0] + COEF_C * q + jnp.where(diagonal, COEF_A, 0.0)
            for h, q in zip(held, squared)
        ]
        for h, m in zip(held, factors):
            h[1] = m if h[1] is None else exact(m, h[1])
        if step + 1 < ITERS:
            once = [exact(m, h[0]) for h, m in zip(held, factors)]
            for h, m, o in zip(held, factors, once):
                h[0] = exact(m, o)
    for s, h in enumerate(held):
        whole = h[1] * (factor * h[2])
        high = whole.astype(jnp.bfloat16)
        low = (whole - high.astype(jnp.float32)).astype(jnp.bfloat16)
        rounded = rounded_ref[s]
        result = (
            jnp.dot(high, rounded, preferred_element_type=jnp.float32)
            + jnp.dot(low, rounded, preferred_element_type=jnp.float32)
        ).astype(jnp.bfloat16)
        first = 0
        for out_ref in out_refs:
            out_ref[s] = result[first : first + out_ref.shape[1]]
            first += out_ref.shape[1]


def orthogonalize(grams, rounded, factor, shares):
    slots, rows, cols = rounded.shape
    return pl.pallas_call(
        functools.partial(orthogonalize_kernel, factor, slots, len(grams)),
        out_shape=[
            jax.ShapeDtypeStruct((slots, share, cols), jnp.bfloat16) for share in shares
        ],
        in_specs=in_vmem(len(grams) + 1),
        out_specs=in_vmem(len(shares)),
        compiler_params=limits(),
        cost_estimate=small_cost(),
    )(*grams, rounded)


def swap(value, bit):
    count = lax.axis_size("dp")
    return lax.ppermute(value, "dp", [(i, i ^ bit) for i in range(count)])


def z_bits():
    bits, bit = [], 2 * X_BIT
    while bit < lax.axis_size("dp"):
        bits.append(bit)
        bit *= 2
    return bits


def offsets(bits):
    if not bits:
        return [0]
    rest = offsets(bits[1:])
    return [bits[0] | o for o in rest] + rest


def levels(bits):
    found = [[(0, -1)]]
    for _ in bits:
        longer = []
        for j, bit in enumerate(bits):
            longer += [(o | bit, j) for o, last in found[-1] if last < j]
        found.append(longer)
    return found


class Block:
    def __init__(self, array, start, split=1):
        self.array, self.start, self.split = array, start, split

    def item(self, slot):
        first = self.start + slot * self.split
        return tuple(range(first, first + self.split))


def sum_to_owners(gradient, me, owner, owners, slots, bits, cut):
    rest = gradient.shape[1] - cut
    level = [[o for o, _ in found] for found in levels(bits)]
    last = {o: bits[j] for found in levels(bits) for o, j in found if j >= 0}
    top = len(bits)
    other_bits = bits[::-1] + [X_BIT]
    other_order = tuple(offsets(other_bits))

    def batch(k):
        order = [o | X_BIT for o in level[k]]
        return tuple(order + (level[k + 1] if k < top else []))

    merged = {k: batch(k) for k in range(top, 0, -1)}
    merged[0] = batch(0) + (0,)

    def theirs(order):
        return tuple(CORE_BIT | o for o in order)

    split = cut // rest
    half = len(other_order) * slots // 2

    def first_items(places):
        return items_of(places(other_order), slots, cut, rest) + items_of(
            places(merged[top]), slots, 0, rest, split
        )

    def same(order):
        return order

    table, packed = first_pack(
        me, owner, owners, slots, gradient, first_items(theirs), rest
    )
    first_got = swap(packed, CORE_BIT)
    falling = range(top - 1, -1, -1)
    plans = [items_of(theirs(merged[k]), slots, 0, cut) for k in falling]
    staying = items_of(other_order, slots, cut, rest)[half:]
    wanted_first = first_items(same)
    plans.append(wanted_first[:half] + wanted_first[2 * half :])
    *packed, mine = pack([packed], table, gradient, plans, [cut] * top + [rest])
    got = {k: swap(block, CORE_BIT) for k, block in zip(falling, packed)}
    after = [packed[0]]

    home = {}
    over_x = {}

    def take(k, after):
        order = merged[k]
        crossing = len(level[k]) * slots
        parts = (crossing,)
        if len(order) * slots > crossing:
            parts += (len(order) * slots - crossing,)
        items = items_of(order, slots, 0, cut)
        made = add_taken(after, table, gradient, items, got[k], parts)
        over_x[k] = made[0]
        for n, o in enumerate(order[len(level[k]) :]):
            home[o] = Block(made[1], n * slots)
        return [made[0]]

    away, far = combine(
        after,
        summed(mine, first_got, 0, half),
        [
            [(mine, half + i), (first_got, 2 * half + i)]
            for i in range(len(wanted_first) - 2 * half)
        ],
    )
    after = [away]
    other_got = swap(away, other_bits[0])
    x_got = swap(far, X_BIT)

    pending = {}
    for k in range(top, -1, -1):
        terms = {o: [] for o in level[k]}
        for n, o in enumerate(level[k]):
            cuts = split if k == top else 1
            terms[o].append(Block(x_got, n * slots * cuts, cuts))
        for o, value in pending.items():
            terms[o ^ last[o]].append(Block(value, 0))
        if k == 0:
            break
        if k == top:
            after = take(k - 1, after)
            (kept,) = add_taken(
                after, table, gradient, staying, first_got, (half,), half
            )
            after = [kept]
        wanted = []
        for o in level[k]:
            parts = [home[o]] + terms[o]
            wanted.append([[(b.array, b.item(s)) for b in parts] for s in range(slots)])
        half //= 2
        wanted.append(summed(kept, other_got, 0, half))
        wanted.append(summed(kept, other_got, half, 2 * half))
        held_back = k == 1
        if held_back:
            wanted.append(joined(over_x[0]))
        made = list(combine(after, *wanted))
        after = [made[0]]
        if held_back:
            over_x[0] = made.pop()
        else:
            after = take(k - 2, after)
        pending = {
            o: swap(made[n], last[o]) for n, o in reversed(list(enumerate(level[k])))
        }
        kept = made[-1]
        other_got = swap(made[-2], other_bits[top - k + 1])
        x_got = swap(over_x[k - 1], X_BIT)
    parts = [[home[0]] + terms[0], [Block(kept, 0), Block(other_got, 0)]]
    return table, parts


def spread_updates(blocks, table, slots, bits, cut, shape, early):
    level = levels(bits)
    last = [dict(found) for found in level]
    own, cur = blocks
    top = len(bits)
    cur_order = [0]
    other_bits = [X_BIT] + bits
    front, front_order = own, [0]
    pieces = {0: own}
    after, update = [early], None

    def with_core(array, first, order):
        return [
            (array, first, order),
            (swap(array, CORE_BIT), first, [CORE_BIT | o for o in order]),
        ]

    for k in range(top + 1):
        longer = {}
        for j, bit in enumerate(bits):
            for o, at in level[k]:
                if at < j:
                    longer[o | bit] = swap(pieces[o], bit)
        x_got = swap(front, X_BIT)
        other_got = swap(cur, other_bits[k])
        crossed = (x_got, 0, [X_BIT | o for o in front_order])
        crossed_other = (other_got, cut, [other_bits[k] | o for o in cur_order])
        if k == top:
            break
        if k > 0:
            update, ran = spread(after, update, shape, table, slots, waiting)
            after = [ran]
        waiting = []
        order = [o for o, _ in level[k + 1]]
        wanted = [joined(*[longer[o] for o in order]), joined(cur, other_got)]
        if k == 0:
            wanted.append(joined(front, x_got))
            front, cur, both = combine(after, *wanted)
            waiting += with_core(both, 0, front_order + crossed[2])
        else:
            front, cur = combine(after, *wanted)
            waiting += with_core(*crossed)
        after = [front]
        pieces = longer
        front_order = order
        cur_order = cur_order + crossed_other[2]
        last = with_core(front, 0, front_order)
        waiting += last if k + 1 < top else last[:1]
    waiting += with_core(cur, cut, cur_order)
    crossed, crossed_other = with_core(*crossed), with_core(*crossed_other)
    waiting += crossed[:1] + crossed_other[:1]
    update, _ = spread(after, update, shape, table, slots, waiting)
    waiting = last[1:] + crossed[1:] + crossed_other[1:]
    return spread([], update, shape, table, slots, waiting)[0]


def per_device(grads, owner, momentum):
    owner_count = lax.axis_size("dp")
    matrices = owner.shape[0]
    slot_count = momentum.shape[1]
    head_rows, cols = grads.shape[2:]
    factor = 0.2 * math.sqrt(max(R, D))
    me = lax.axis_index("dp").astype(jnp.int32).reshape(1)

    cut = head_rows * 3 // 4
    bits = z_bits()[::-1]
    table, parts = sum_to_owners(
        grads[0], me, owner, owner_count, slot_count, bits, cut
    )
    rounded, gram = nesterov_step(momentum[0], parts, owner_count)

    width = lax.axis_size("tensor")
    grams = [gram]
    for _ in range(width - 1):
        grams.append(
            lax.ppermute(
                grams[-1], "tensor", [(i, (i + 1) % width) for i in range(width)]
            )
        )
    blocks = orthogonalize(grams, rounded, factor, [cut, head_rows - cut])
    new_momentum, early = momentum_step(
        blocks[:1], table, momentum[0], parts, owner_count
    )
    shape = (matrices, head_rows, cols)
    update = spread_updates(
        blocks, table, slot_count, bits, cut, shape, early
    )
    return (update, new_momentum[None])


def solution(mesh):
    in_specs = (P("dp", None, None, "tensor"), P(), P("dp", None, None, "tensor"))
    out_specs = (P(None, None, "tensor"), P("dp", None, None, "tensor"))
    return jax.shard_map(
        per_device, mesh=mesh, in_specs=in_specs, out_specs=out_specs, check_vma=False
    )
```

```python
import functools
import math

import jax
import jax.numpy as jnp
from jax import lax
from jax.experimental import pallas as pl
from jax.experimental.pallas import tpu as pltpu
from jax.sharding import PartitionSpec as P

R = 128
D = 4096
ITERS = 5

COEF_A = 3.4445
COEF_B = -4.775
COEF_C = 2.0315
EPSILON = 1e-07
DECAY = 0.95

CORE_BIT = 1
X_BIT = 2
VMEM_BYTES = 24 * 1024 * 1024
MORE_VMEM_BYTES = 41 * 1024 * 1024


def in_vmem(count=1):
    return [pl.BlockSpec(memory_space=pltpu.VMEM)] * count


def anywhere(count=1):
    return [pl.BlockSpec(memory_space=pl.ANY)] * count


def in_hbm():
    return [pl.BlockSpec(memory_space=pltpu.HBM)]


def in_smem(count=1):
    return [pl.BlockSpec(memory_space=pltpu.SMEM)] * count


def limits(size=VMEM_BYTES):
    return pltpu.CompilerParams(vmem_limit_bytes=size)


def small_cost():
    return pl.CostEstimate(flops=0, bytes_accessed=0, transcendentals=0)


def token():
    return jax.ShapeDtypeStruct((8, 128), jnp.float32)


def table_kernel(slots, me_ref, owner_ref, table_ref, used):
    spots, matrices = table_ref.shape[0], owner_ref.shape[0]

    @pl.loop(0, spots, unroll=True)
    def _(i):
        table_ref[i] = -1

    @pl.loop(0, spots // slots, unroll=True)
    def _(i):
        used[i] = 0

    @pl.loop(0, matrices, unroll=True)
    def _(m):
        at = owner_ref[m]
        rank = used[at]
        table_ref[(at ^ me_ref[0]) * slots + rank] = m
        used[at] = rank + 1


def starts(order, slots):
    return [
        (n * slots + s, offset * slots + s)
        for n, offset in enumerate(order)
        for s in range(slots)
    ]


def items_of(order, slots, first, rows, split=1):
    return tuple(
        (place, first + c * rows) for _, place in starts(order, slots) for c in range(split)
    )


def fetch(table_ref, src_ref, items, into, sem):
    rows = into.shape[1]
    for item, (place, first) in enumerate(items):
        matrix = jnp.maximum(table_ref[place], 0)
        pltpu.make_async_copy(
            src_ref.at[matrix, pl.ds(first, rows)], into.at[item], sem.at[item]
        ).start()
    return lambda i: pltpu.make_async_copy(
        src_ref.at[0, pl.ds(0, rows)], into.at[i], sem.at[i]
    )


def pack_kernel(plans, table_ref, src_ref, *rest):
    out_refs = rest[-2 * len(plans) : -len(plans)]
    sems = rest[-len(plans) :]
    copies = [
        fetch(table_ref, src_ref, items, out_ref, sem)
        for items, out_ref, sem in zip(plans, out_refs, sems)
    ]
    for copy, out_ref in zip(copies, out_refs):

        @pl.loop(0, out_ref.shape[0])
        def _(i, copy=copy):
            copy(i).wait()


def pack(after, table, src, plans, sizes):
    return pl.pallas_call(
        functools.partial(pack_kernel, tuple(plans)),
        out_shape=[
            jax.ShapeDtypeStruct((len(items), rows, src.shape[2]), src.dtype)
            for items, rows in zip(plans, sizes)
        ],
        in_specs=in_smem() + in_hbm() + anywhere(len(after)),
        out_specs=in_vmem(len(plans)),
        scratch_shapes=[pltpu.SemaphoreType.DMA((len(items),)) for items in plans],
        compiler_params=limits(MORE_VMEM_BYTES),
        cost_estimate=small_cost(),
    )(table, src, *after)


def first_pack_kernel(items, slots, me_ref, owner_ref, src_ref, *rest):
    table_ref, out_ref, used, sem = rest
    table_kernel(slots, me_ref, owner_ref, table_ref, used)
    copy = fetch(table_ref, src_ref, items, out_ref, sem)

    @pl.loop(0, out_ref.shape[0])
    def _(i):
        copy(i).wait()


def first_pack(me, owner, owners, slots, src, items, rows):
    count = len(items)
    return pl.pallas_call(
        functools.partial(first_pack_kernel, items, slots),
        out_shape=[
            jax.ShapeDtypeStruct((owners * slots,), jnp.int32),
            jax.ShapeDtypeStruct((count, rows, src.shape[2]), src.dtype),
        ],
        in_specs=in_smem(2) + in_hbm(),
        out_specs=in_smem() + in_vmem(),
        scratch_shapes=[
            pltpu.SMEM((owners,), jnp.int32),
            pltpu.SemaphoreType.DMA((count,)),
        ],
        compiler_params=limits(MORE_VMEM_BYTES),
        cost_estimate=small_cost(),
    )(me, owner, src)


def add_taken_kernel(items, parts, offset, table_ref, src_ref, got_ref, *rest):
    mine, sem = rest[-2:]
    out_refs = rest[-2 - len(parts) : -2]
    copy = fetch(table_ref, src_ref, items, mine, sem)
    start = 0
    for size, out_ref in zip(parts, out_refs):

        @pl.loop(0, size)
        def _(i, start=start, out_ref=out_ref):
            copy(start + i).wait()
            out_ref[i] = got_ref[offset + start + i] + mine[start + i]

        start += size


def add_taken(after, table, src, items, got, parts, offset=0):
    count, (_, rows, cols) = len(items), got.shape
    return pl.pallas_call(
        functools.partial(add_taken_kernel, items, parts, offset),
        out_shape=[jax.ShapeDtypeStruct((n, rows, cols), got.dtype) for n in parts],
        in_specs=in_smem() + in_hbm() + in_vmem() + anywhere(len(after)),
        out_specs=in_vmem(len(parts)),
        scratch_shapes=[
            pltpu.VMEM((count, rows, cols), got.dtype),
            pltpu.SemaphoreType.DMA((count,)),
        ],
        compiler_params=limits(MORE_VMEM_BYTES),
        cost_estimate=small_cost(),
    )(table, src, got, *after)


def combine_kernel(arrays, plans, *refs):
    sources = refs[:arrays]
    outs = refs[len(refs) - len(plans) :]
    for out_ref, items in zip(outs, plans):
        for i, terms in enumerate(items):
            cuts = max(len(item) for _, item in terms)
            rows = out_ref.shape[1] // cuts
            for c in range(cuts):
                here = pl.ds(c * rows, rows)
                total = None
                for at, item in terms:
                    if len(item) == cuts:
                        term = sources[at][item[c]]
                    else:
                        term = sources[at][item[0], here]
                    total = term if total is None else total + term
                out_ref[i, here] = total


def combine(after, *wanted):
    arrays, plans = [], []
    for items in wanted:
        plan = []
        for terms in items:
            found = []
            for array, item in terms:
                places = [i for i, a in enumerate(arrays) if a is array]
                if not places:
                    arrays.append(array)
                    places = [len(arrays) - 1]
                found.append((places[0], item if isinstance(item, tuple) else (item,)))
            plan.append(tuple(found))
        plans.append(tuple(plan))
    shapes = []
    for items in wanted:
        sample = items[0][0][0]
        shapes.append(
            jax.ShapeDtypeStruct((len(items),) + sample.shape[1:], sample.dtype)
        )
    return pl.pallas_call(
        functools.partial(combine_kernel, len(arrays), tuple(plans)),
        out_shape=shapes,
        in_specs=in_vmem(len(arrays)) + anywhere(len(after)),
        out_specs=in_vmem(len(plans)),
        compiler_params=limits(),
        cost_estimate=small_cost(),
    )(*arrays, *after)


def joined(*arrays):
    return [[(array, i)] for array in arrays for i in range(array.shape[0])]


def summed(home, got, first, last):
    return [[(home, i), (got, i)] for i in range(first, last)]


def spread_kernel(plans, slots, table_ref, *refs):
    piece_refs = refs[: len(plans)]
    out_ref, token_ref, sem = refs[-3:]
    token_ref[...] = jnp.zeros_like(token_ref)
    for wait in (False, True):
        for p, (first, order) in enumerate(plans):
            for item, place in starts(order, slots):
                to = table_ref[place]

                @pl.when(to >= 0)
                def _(p=p, item=item, to=to, wait=wait, first=first):
                    rows = piece_refs[p].shape[1]
                    copy = pltpu.make_async_copy(
                        piece_refs[p].at[item],
                        out_ref.at[to, pl.ds(first, rows)],
                        sem.at[p, item],
                    )
                    if wait:
                        copy.wait()
                    else:
                        copy.start()


def spread(after, target, shape, table, slots, pieces):
    count = len(pieces)
    arrays = [array for array, _, _ in pieces]
    plans = tuple((first, tuple(order)) for _, first, order in pieces)
    most = max(a.shape[0] for a in arrays)
    more = [] if target is None else [target]
    return pl.pallas_call(
        functools.partial(spread_kernel, plans, slots),
        out_shape=[jax.ShapeDtypeStruct(shape, arrays[0].dtype), token()],
        in_specs=in_smem() + in_vmem(count) + anywhere(len(more) + len(after)),
        out_specs=anywhere() + in_vmem(),
        scratch_shapes=[pltpu.SemaphoreType.DMA((count, most))],
        input_output_aliases={1 + count: 0} if more else {},
        compiler_params=limits(MORE_VMEM_BYTES),
        cost_estimate=small_cost(),
    )(table, *arrays, *more, *after)


def mean_rows(scale, sizes, refs):
    first, used = 0, 0
    for size in sizes:
        total = None
        for ref, item in refs[used : used + size]:
            term = ref[item].astype(jnp.float32)
            total = term if total is None else total + term
        yield first, total * scale
        first += total.shape[0]
        used += size


def nesterov_kernel(scale, sizes, items, momentum_ref, *rest):
    part_refs, (rounded_ref, gram_ref) = rest[: len(items)], rest[len(items) :]
    for s in range(momentum_ref.shape[0]):
        refs = [(ref, item + s) for ref, item in zip(part_refs, items)]
        for first, mean in mean_rows(scale, sizes, refs):
            here = pl.ds(first, mean.shape[0])
            following = DECAY * momentum_ref[s, here] + mean
            rounded_ref[s, here] = (mean + DECAY * following).astype(jnp.bfloat16)
        rounded = rounded_ref[s]
        gram_ref[s] = lax.dot_general(
            rounded,
            rounded,
            (((1,), (1,)), ((), ())),
            preferred_element_type=jnp.float32,
        )


def momentum_kernel(scale, sizes, count, table_ref, momentum_ref, *rest):
    part_refs, (next_ref, token_ref) = rest[:count], rest[-2:]
    token_ref[...] = jnp.zeros_like(token_ref)
    held = table_ref[pl.program_id(0)] >= 0
    for first, mean in mean_rows(scale, sizes, [(ref, 0) for ref in part_refs]):
        here = pl.ds(first, mean.shape[0])
        previous = momentum_ref[0, here]
        next_ref[0, here] = jnp.where(held, DECAY * previous + mean, previous)


def nesterov_step(momentum, parts, owner_count):
    slots, rows, cols = momentum.shape
    flat = [b for part in parts for b in part]
    sizes = [len(part) for part in parts]
    items = [b.start for b in flat]
    return pl.pallas_call(
        functools.partial(nesterov_kernel, 1.0 / owner_count, sizes, items),
        out_shape=[
            jax.ShapeDtypeStruct((slots, rows, cols), jnp.bfloat16),
            jax.ShapeDtypeStruct((slots, rows, rows), jnp.float32),
        ],
        in_specs=in_vmem(1 + len(flat)),
        out_specs=in_vmem(2),
        compiler_params=limits(),
        cost_estimate=small_cost(),
    )(momentum, *[b.array for b in flat])


def momentum_step(after, table, momentum, parts, owner_count):
    slots, rows, cols = momentum.shape
    flat = [b for part in parts for b in part]
    sizes = [len(part) for part in parts]
    return pl.pallas_call(
        functools.partial(momentum_kernel, 1.0 / owner_count, sizes, len(flat)),
        grid=(slots,),
        out_shape=[jax.ShapeDtypeStruct((slots, rows, cols), jnp.float32), token()],
        in_specs=in_smem()
        + [pl.BlockSpec((1, rows, cols), lambda s: (s, 0, 0))]
        + [
            pl.BlockSpec((1,) + b.array.shape[1:], lambda s, at=b.start: (s + at, 0, 0))
            for b in flat
        ]
        + anywhere(len(after)),
        out_specs=[
            pl.BlockSpec((1, rows, cols), lambda s: (s, 0, 0)),
            pl.BlockSpec((8, 128), lambda s: (0, 0)),
        ],
        compiler_params=limits(),
        cost_estimate=small_cost(),
    )(table, momentum, *[b.array for b in flat], *after)


def exact(a, b):
    def split(v):
        high = v.astype(jnp.bfloat16)
        return high, (v - high.astype(jnp.float32)).astype(jnp.bfloat16)

    def dot(p, q):
        return jnp.dot(p, q, preferred_element_type=jnp.float32)

    (a_high, a_low), (b_high, b_low) = split(a), split(b)
    return dot(a_high, b_high) + (dot(a_high, b_low) + dot(a_low, b_high))


def orthogonalize_kernel(factor, slots, grams, *refs):
    gram_refs = refs[:grams]
    rounded_ref = refs[grams]
    out_refs = refs[grams + 1 :]
    rows = rounded_ref.shape[1]
    row_ids = lax.broadcasted_iota(jnp.int32, (rows, rows), 0)
    col_ids = lax.broadcasted_iota(jnp.int32, (rows, rows), 1)
    diagonal = row_ids == col_ids
    held = []
    for s in range(slots):
        gram = gram_refs[0][s]
        for ref in gram_refs[1:]:
            gram = gram + ref[s]
        squares = jnp.sum(
            jnp.sum(jnp.where(diagonal, gram, 0.0), axis=0, keepdims=True),
            axis=1,
            keepdims=True,
        )
        inverse = 1.0 / (jnp.sqrt(squares) + EPSILON)
        held.append([gram * inverse * inverse, None, inverse])
    for step in range(ITERS):
        squared = [exact(h[0], h[0]) for h in held]
        factors = [
            COEF_B * h[0] + COEF_C * q + jnp.where(diagonal, COEF_A, 0.0)
            for h, q in zip(held, squared)
        ]
        for h, m in zip(held, factors):
            h[1] = m if h[1] is None else exact(m, h[1])
        if step + 1 < ITERS:
            once = [exact(m, h[0]) for h, m in zip(held, factors)]
            for h, m, o in zip(held, factors, once):
                h[0] = exact(m, o)
    for s, h in enumerate(held):
        whole = h[1] * (factor * h[2])
        high = whole.astype(jnp.bfloat16)
        low = (whole - high.astype(jnp.float32)).astype(jnp.bfloat16)
        rounded = rounded_ref[s]
        result = (
            jnp.dot(high, rounded, preferred_element_type=jnp.float32)
            + jnp.dot(low, rounded, preferred_element_type=jnp.float32)
        ).astype(jnp.bfloat16)
        first = 0
        for out_ref in out_refs:
            out_ref[s] = result[first : first + out_ref.shape[1]]
            first += out_ref.shape[1]


def orthogonalize(grams, rounded, factor, shares):
    slots, rows, cols = rounded.shape
    return pl.pallas_call(
        functools.partial(orthogonalize_kernel, factor, slots, len(grams)),
        out_shape=[
            jax.ShapeDtypeStruct((slots, share, cols), jnp.bfloat16) for share in shares
        ],
        in_specs=in_vmem(len(grams) + 1),
        out_specs=in_vmem(len(shares)),
        compiler_params=limits(),
        cost_estimate=small_cost(),
    )(*grams, rounded)


def swap(value, bit):
    count = lax.axis_size("dp")
    return lax.ppermute(value, "dp", [(i, i ^ bit) for i in range(count)])


def z_bits():
    bits, bit = [], 2 * X_BIT
    while bit < lax.axis_size("dp"):
        bits.append(bit)
        bit *= 2
    return bits


def offsets(bits):
    if not bits:
        return [0]
    rest = offsets(bits[1:])
    return [bits[0] | o for o in rest] + rest


def levels(bits):
    found = [[(0, -1)]]
    for _ in bits:
        longer = []
        for j, bit in enumerate(bits):
            longer += [(o | bit, j) for o, last in found[-1] if last < j]
        found.append(longer)
    return found


class Block:
    def __init__(self, array, start, split=1):
        self.array, self.start, self.split = array, start, split

    def item(self, slot):
        first = self.start + slot * self.split
        return tuple(range(first, first + self.split))


def sum_to_owners(gradient, me, owner, owners, slots, bits, cut):
    rest = gradient.shape[1] - cut
    level = [[o for o, _ in found] for found in levels(bits)]
    last = {o: bits[j] for found in levels(bits) for o, j in found if j >= 0}
    top = len(bits)
    other_bits = bits[::-1] + [X_BIT]
    other_order = tuple(offsets(other_bits))

    def batch(k):
        order = [o | X_BIT for o in level[k]]
        return tuple(order + (level[k + 1] if k < top else []))

    merged = {k: batch(k) for k in range(top, 0, -1)}
    merged[0] = batch(0) + (0,)

    def theirs(order):
        return tuple(CORE_BIT | o for o in order)

    split = cut // rest
    half = len(other_order) * slots // 2

    def first_items(places):
        return items_of(places(other_order), slots, cut, rest) + items_of(
            places(merged[top]), slots, 0, rest, split
        )

    def same(order):
        return order

    table, packed = first_pack(
        me, owner, owners, slots, gradient, first_items(theirs), rest
    )
    first_got = swap(packed, CORE_BIT)
    falling = range(top - 1, -1, -1)
    plans = [items_of(theirs(merged[k]), slots, 0, cut) for k in falling]
    staying = items_of(other_order, slots, cut, rest)[half:]
    wanted_first = first_items(same)
    plans.append(wanted_first[:half] + wanted_first[2 * half :])
    *packed, mine = pack([packed], table, gradient, plans, [cut] * top + [rest])
    got = {k: swap(block, CORE_BIT) for k, block in zip(falling, packed)}
    after = [packed[0]]

    home = {}
    over_x = {}

    def take(k, after):
        order = merged[k]
        crossing = len(level[k]) * slots
        parts = (crossing,)
        if len(order) * slots > crossing:
            parts += (len(order) * slots - crossing,)
        items = items_of(order, slots, 0, cut)
        made = add_taken(after, table, gradient, items, got[k], parts)
        over_x[k] = made[0]
        for n, o in enumerate(order[len(level[k]) :]):
            home[o] = Block(made[1], n * slots)
        return [made[0]]

    away, far = combine(
        after,
        summed(mine, first_got, 0, half),
        [
            [(mine, half + i), (first_got, 2 * half + i)]
            for i in range(len(wanted_first) - 2 * half)
        ],
    )
    after = [away]
    other_got = swap(away, other_bits[0])
    x_got = swap(far, X_BIT)

    pending = {}
    for k in range(top, -1, -1):
        terms = {o: [] for o in level[k]}
        for n, o in enumerate(level[k]):
            cuts = split if k == top else 1
            terms[o].append(Block(x_got, n * slots * cuts, cuts))
        for o, value in pending.items():
            terms[o ^ last[o]].append(Block(value, 0))
        if k == 0:
            break
        if k == top:
            after = take(k - 1, after)
            (kept,) = add_taken(
                after, table, gradient, staying, first_got, (half,), half
            )
            after = [kept]
        wanted = []
        for o in level[k]:
            parts = [home[o]] + terms[o]
            wanted.append([[(b.array, b.item(s)) for b in parts] for s in range(slots)])
        half //= 2
        wanted.append(summed(kept, other_got, 0, half))
        wanted.append(summed(kept, other_got, half, 2 * half))
        held_back = k == 1
        if held_back:
            wanted.append(joined(over_x[0]))
        made = list(combine(after, *wanted))
        after = [made[0]]
        if held_back:
            over_x[0] = made.pop()
        else:
            after = take(k - 2, after)
        pending = {
            o: swap(made[n], last[o]) for n, o in reversed(list(enumerate(level[k])))
        }
        kept = made[-1]
        other_got = swap(made[-2], other_bits[top - k + 1])
        x_got = swap(over_x[k - 1], X_BIT)
    parts = [[home[0]] + terms[0], [Block(kept, 0), Block(other_got, 0)]]
    return table, parts


def spread_updates(blocks, table, slots, bits, cut, shape, early):
    level = levels(bits)
    last = [dict(found) for found in level]
    own, cur = blocks
    top = len(bits)
    cur_order = [0]
    other_bits = [X_BIT] + bits
    front, front_order = own, [0]
    pieces = {0: own}
    after, update = [early], None

    def with_core(array, first, order):
        return [
            (array, first, order),
            (swap(array, CORE_BIT), first, [CORE_BIT | o for o in order]),
        ]

    for k in range(top + 1):
        longer = {}
        for j, bit in enumerate(bits):
            for o, at in level[k]:
                if at < j:
                    longer[o | bit] = swap(pieces[o], bit)
        x_got = swap(front, X_BIT)
        other_got = swap(cur, other_bits[k])
        crossed = (x_got, 0, [X_BIT | o for o in front_order])
        crossed_other = (other_got, cut, [other_bits[k] | o for o in cur_order])
        if k == top:
            break
        if k > 0:
            update, ran = spread(after, update, shape, table, slots, waiting)
            after = [ran]
        waiting = []
        order = [o for o, _ in level[k + 1]]
        wanted = [joined(*[longer[o] for o in order]), joined(cur, other_got)]
        if k == 0:
            wanted.append(joined(front, x_got))
            front, cur, both = combine(after, *wanted)
            waiting += with_core(both, 0, front_order + crossed[2])
        else:
            front, cur = combine(after, *wanted)
            waiting += with_core(*crossed)
        after = [front]
        pieces = longer
        front_order = order
        cur_order = cur_order + crossed_other[2]
        last = with_core(front, 0, front_order)
        waiting += last if k + 1 < top else last[:1]
    waiting += with_core(cur, cut, cur_order)
    crossed, crossed_other = with_core(*crossed), with_core(*crossed_other)
    waiting += crossed[:1] + crossed_other[:1]
    update, _ = spread(after, update, shape, table, slots, waiting)
    waiting = last[1:] + crossed[1:] + crossed_other[1:]
    return spread([], update, shape, table, slots, waiting)[0]


def per_device(grads, owner, momentum):
    owner_count = lax.axis_size("dp")
    matrices = owner.shape[0]
    slot_count = momentum.shape[1]
    head_rows, cols = grads.shape[2:]
    factor = 0.2 * math.sqrt(max(R, D))
    me = lax.axis_index("dp").astype(jnp.int32).reshape(1)

    cut = head_rows * 3 // 4
    bits = z_bits()[::-1]
    table, parts = sum_to_owners(
        grads[0], me, owner, owner_count, slot_count, bits, cut
    )
    rounded, gram = nesterov_step(momentum[0], parts, owner_count)

    width = lax.axis_size("tensor")
    grams = [gram]
    for _ in range(width - 1):
        grams.append(
            lax.ppermute(
                grams[-1], "tensor", [(i, (i + 1) % width) for i in range(width)]
            )
        )
    blocks = orthogonalize(grams, rounded, factor, [cut, head_rows - cut])
    new_momentum, early = momentum_step(
        blocks[:1], table, momentum[0], parts, owner_count
    )
    shape = (matrices, head_rows, cols)
    update = spread_updates(
        blocks, table, slot_count, bits, cut, shape, early
    )
    return (update, new_momentum[None])


def solution(mesh):
    in_specs = (P("dp", None, None, "tensor"), P(), P("dp", None, None, "tensor"))
    out_specs = (P(None, None, "tensor"), P("dp", None, None, "tensor"))
    return jax.shard_map(
        per_device, mesh=mesh, in_specs=in_specs, out_specs=out_specs, check_vma=False
    )
```
